32 devices in a mesh: ctx: 8 (over z, x), fsdp: 4 (over y, core).
Axes of the slice: x: 2, y: 2, z: 4, core: 2. Of those that a mesh axis runs over, the one named last changes fastest.
Arguments:
- layer_input: bfloat16 [4, 3072, 1536], P('fsdp', 'ctx'), may hold values from -6 to 6
- lengths: int32 [4, 3], P('fsdp'), may hold values from 64 to 2944, as said below
- expert_ids: int32 [4, 3072, 4], P('fsdp', 'ctx'), may hold values from 0 to 15, all different within a row; in each aligned block of 384 rows (0 to 383, 384 to 767, ..., all dimensions but the last counted through in order) at most 144 rows name the same one
- gate_weights: float32 [4, 3072, 4], P('fsdp', 'ctx'), may hold values from 0.15 to 0.35
- attn_gain: bfloat16 [1536], P(('ctx', 'fsdp')), may hold values from 0.5 to 1.5
- wq: bfloat16 [1536, 1536], P(('ctx', 'fsdp')), may hold values from -0.15625 to 0.15625
- wk: bfloat16 [1536, 256], P(('ctx', 'fsdp')), may hold values from -0.15625 to 0.15625
- wv: bfloat16 [1536, 256], P(('ctx', 'fsdp')), may hold values from -0.15625 to 0.15625
- wo: bfloat16 [1536, 1536], P(None, ('ctx', 'fsdp')), may hold values from -2.5 to 2.5
- moe_gain: bfloat16 [1536], P(('ctx', 'fsdp')), may hold values from 0.5 to 1.5
- w_gate: bfloat16 [16, 1536, 768], P('ctx', 'fsdp'), may hold values from -0.15625 to 0.15625
- w_up: bfloat16 [16, 1536, 768], P('ctx', 'fsdp'), may hold values from -0.15625 to 0.15625
- w_down: bfloat16 [16, 768, 1536], P('ctx', None, 'fsdp'), may hold values from -0.625 to 0.625
- cotangent: bfloat16 [4, 3072, 1536], P('fsdp', 'ctx'), may hold values from -6 to 6
Outputs:
- output: bfloat16 [4, 3072, 1536], P('fsdp', 'ctx')
- input_grad: bfloat16 [4, 3072, 1536], P('fsdp', 'ctx')
- attn_gain_grad: float32 [1536], P(('ctx', 'fsdp'))
- wq_grad: float32 [1536, 1536], P(('ctx', 'fsdp'))
- wk_grad: float32 [1536, 256], P(('ctx', 'fsdp'))
- wv_grad: float32 [1536, 256], P(('ctx', 'fsdp'))
- wo_grad: float32 [1536, 1536], P(None, ('ctx', 'fsdp'))
- moe_gain_grad: float32 [1536], P(('ctx', 'fsdp'))
- w_gate_grad: float32 [16, 1536, 768], P('ctx', 'fsdp')
- w_up_grad: float32 [16, 1536, 768], P('ctx', 'fsdp')
- w_down_grad: float32 [16, 768, 1536], P('ctx', None, 'fsdp')
The draws below stay inside these ranges and needn't reach their ends.
Inputs may be any that keep to these rules, and one draw needn't show every extreme that they name: Each row holds the lengths of the 3 sequences that fill a group's 3072 tokens in order. In each row one sequence is long and the other 2 each have at most 192 tokens; the long one spans from the group's first device to its last. In some row the short ones all equal the least. `expert_ids`: A token names 4 different experts. Among the 384 tokens of one device (aligned blocks of rows) no expert is named more than 144 times, a bound that some block reaches.
All inputs are finite; a program needn't handle non-finite values.
Results may differ from the reference program's by a relative error of at most 0.018.
Values may be sent and summed in bfloat16 or wider, within the bound.
No kernel may reach another device: no remote copies, remote signals or barrier semaphores. Data moves between devices by JAX's collectives and lax.ppermute only.
A program may use at most 256 MiB of HBM per device.

```python
import math
import jax
import jax.numpy as jnp
import numpy as np
from jax import lax

D = 1536
HEADS = 12
KV_HEADS = 2
HEAD = 128
FF = 768
TOPK = 4
SEQS = 3
MINLEN = 64
TOK_DEV = 384
GROUPS = 4
GTOK = 3072
EXPERTS = 16
CAP = 144
HQ = 1536
KVW = 256
N_CTX = 8


def draw_lengths(key, part):
    key = jax.random.fold_in(key, 17)
    short_top = TOK_DEV // (SEQS - 1)
    short_key, order_key, pick_key = jax.random.split(key, 3)
    shorts = jax.random.randint(short_key, (GROUPS, SEQS - 1), MINLEN, short_top + 1, dtype=jnp.int32)
    chosen = jax.random.randint(pick_key, (), 0, GROUPS, dtype=jnp.int32)
    shorts = jnp.where((jnp.arange(GROUPS, dtype=jnp.int32) == chosen)[:, None], MINLEN, shorts)
    longest = GTOK - jnp.sum(shorts, 1, keepdims=True)
    base = jnp.concatenate([longest, shorts], 1)

    def shuffle(sub_key):
        return jax.random.permutation(sub_key, SEQS)
    orders = jax.vmap(shuffle)(jax.random.split(order_key, GROUPS))
    return jnp.take_along_axis(base, orders, axis=1).astype(jnp.int32)


def block_scale(own_key, dims, cuts, low, top_value):
    loudness = 1.0
    for dim, shards_of in cuts:
        steps = jax.random.uniform(jax.random.fold_in(jax.random.fold_in(own_key, 6), dim), (shards_of,), jnp.float32, low / len(cuts), top_value / len(cuts))
        loudness = loudness * jnp.repeat(jnp.exp(steps), dims[dim] // shards_of).reshape((-1,) + (1,) * (len(dims) - 1 - dim))
    return loudness


def shared_out(own_key, own, number, rows, number_of, top, limit, lean):
    ranking = jax.random.permutation(own_key, number_of)
    heavy_load, usual = portions_of(number_of, rows * top, limit, lean, True), portions_of(number_of, rows * top, limit, lean, False)
    places = jnp.arange(number_of)

    def named(sizes, offset_by):
        used = int((sizes > 0).sum())
        fixed = max(1, used // 4)
        moved = fixed + (places - fixed + offset_by * (used - fixed)) % max(1, number_of - fixed)
        return jnp.zeros((number_of,), jnp.int32).at[ranking[jnp.where(places < fixed, places, moved)]].set(jnp.asarray(sizes, jnp.int32))

    sizes = jnp.where(number % 4 == 0, named(heavy_load, number // 4), named(usual, number - number // 4 - 1))
    mixed = jax.random.permutation(jax.random.fold_in(own, 3), number_of)
    source_of, taker = mixed[0:number_of // 2 * 2:2], mixed[1:number_of // 2 * 2:2]
    slack = jnp.minimum(sizes[source_of] - 1, limit - sizes[taker]) // 2
    slack = jnp.where((source_of == ranking[0]) | (taker == ranking[0]) | (sizes[taker] == 0), 0, jnp.maximum(slack, 0))
    moved = jax.random.randint(jax.random.fold_in(own, 4), (number_of // 2,), 0, 1 << 20) % (slack + 1)
    sizes = sizes.at[source_of].add(-moved).at[taker].add(moved)
    items = jnp.searchsorted(jnp.cumsum(sizes), jnp.arange(rows * top), side="right").astype(jnp.int32)
    grid = items.reshape(top, rows).T
    grid = grid[jax.random.permutation(jax.random.fold_in(own, 1), rows)]
    offset_by = jax.random.randint(jax.random.fold_in(own, 2), (rows, 1), 0, top)
    return jnp.take_along_axis(grid, (jnp.arange(top)[None, :] + offset_by) % top, axis=1)


def portions_of(number_of, total, limit, slope, full):
    portions = [(1 << 20) // math.isqrt(standing ** slope) + 1 for standing in range(1, number_of + 1)]
    largest = limit if full else min(limit, max(-(-total // number_of), total * portions[0] // sum(portions)))
    least = 1 if total - largest >= number_of - 1 else 0
    holding, spare = [largest] + [least] * (number_of - 1), total - largest - least * (number_of - 1)
    while spare > 0:
        movable = [i for i in range(1, number_of) if holding[i] < largest] or [i for i in range(1, number_of) if holding[i] < limit]
        mass, budget = sum([portions[i] for i in movable]), spare
        for i in movable:
            addition = min(limit - holding[i], max(1, budget * portions[i] // mass), spare)
            holding[i] = holding[i] + addition
            spare = spare - addition
    return np.array(holding)


def scatter_about(stream_key, extent, deviation, most, cuts=(), kind=jnp.bfloat16):
    array = deviation * jax.random.normal(stream_key, extent, jnp.float32)
    if cuts:
        array = array * block_scale(stream_key, extent, cuts, -0.22, 0.18)
    return jnp.clip(array, -most, most).astype(kind)


def setup_inputs(seed: int = 0) -> dict:
    keys = jax.random.split(jax.random.key(seed), 15)
    layer_input = scatter_about(keys[0], (GROUPS, GTOK, D), 1.0, 6.0, ((0, 4), (1, 8)))
    lengths = draw_lengths(jax.random.fold_in(keys[14], 71), 0)
    expert_ids_keys = jax.random.split(jax.random.fold_in(keys[2], 1), GROUPS * GTOK // TOK_DEV)
    expert_ids_turns = jax.random.permutation(jax.random.fold_in(keys[2], 3), GROUPS * GTOK // TOK_DEV)
    expert_ids = jax.vmap(lambda own, number: shared_out(jax.random.fold_in(keys[2], 2), own, number, TOK_DEV, EXPERTS, TOPK, CAP, 1))(expert_ids_keys, expert_ids_turns).reshape((GROUPS, GTOK, TOPK))
    gate_weights = jnp.clip(0.15 + 0.19999999 * jax.random.uniform(keys[3], (GROUPS, GTOK, TOPK), jnp.float32) ** block_scale(keys[3], (GROUPS, GTOK, TOPK), ((0, 4), (1, 8)), -0.2, 0.2), 0.15, 0.35)
    attn_gain = jnp.clip(1.0 + 0.1 * jax.random.normal(keys[4], (D,), jnp.float32), 0.5, 1.5).astype(jnp.bfloat16)
    wq = scatter_about(keys[5], (D, HQ), D ** -0.5, 0.15625, ((0, 32),))
    wk = scatter_about(keys[6], (D, KVW), D ** -0.5, 0.15625, ((0, 32),))
    wv = scatter_about(keys[7], (D, KVW), D ** -0.5, 0.15625, ((0, 32),))
    wo = scatter_about(keys[8], (HQ, D), (max(1, HQ // 256)) ** -0.5, 2.5, ((1, 32),))
    moe_gain = jnp.clip(1.0 + 0.1 * jax.random.normal(keys[9], (D,), jnp.float32), 0.5, 1.5).astype(jnp.bfloat16)
    w_gate = scatter_about(keys[10], (EXPERTS, D, FF), D ** -0.5, 0.15625, ((0, 8), (1, 4)))
    w_up = scatter_about(keys[11], (EXPERTS, D, FF), D ** -0.5, 0.15625, ((0, 8), (1, 4)))
    w_down = scatter_about(keys[12], (EXPERTS, FF, D), (FF // 8) ** -0.5, 0.625, ((0, 8), (2, 4)))
    cotangent = scatter_about(keys[13], (GROUPS, GTOK, D), 1.0, 6.0, ((0, 4), (1, 8)))
    return {"layer_input": layer_input, "lengths": lengths, "expert_ids": expert_ids, "gate_weights": gate_weights, "attn_gain": attn_gain, "wq": wq, "wk": wk, "wv": wv, "wo": wo, "moe_gain": moe_gain, "w_gate": w_gate, "w_up": w_up, "w_down": w_down, "cotangent": cotangent}


EPS = 1e-06
ROPE_BASE = 10000.0
NEG = -1e+30
HIGH = lax.Precision.HIGHEST

@jax.custom_vjp
def low(v):
    return lax.optimization_barrier(v.astype(jnp.bfloat16)).astype(jnp.float32)

@jax.custom_vjp
def low_back(v):
    return v

def low_keep(v):
    return (low(v), None)

def low_pass(kept, grad):
    return (grad,)

def back_keep(v):
    return (v, None)

def back_low(kept, grad):
    return (low(grad),)
low.defvjp(low_keep, low_pass)
low_back.defvjp(back_keep, back_low)

def rope_tables(positions, head_size):
    half = head_size // 2
    freq = jnp.exp(jnp.arange(half, dtype=jnp.float32) * (-2.0 * math.log(ROPE_BASE) / head_size))
    angle = positions.astype(jnp.float32)[:, None] * freq[None, :]
    return (jnp.cos(angle), jnp.sin(angle))

def rotate(values, cosine, sine):
    half = values.shape[-1] // 2
    first = values[..., :half]
    second = values[..., half:]
    cosine = cosine[:, None, :]
    sine = sine[:, None, :]
    return jnp.concatenate([first * cosine - second * sine, second * cosine + first * sine], -1)

def seq_info(index, seq_lengths):
    ends = jnp.cumsum(seq_lengths)
    after = (index[:, None] >= ends[None, :]).astype(jnp.int32)
    return (lax.optimization_barrier(jnp.sum(after, 1)), index - lax.optimization_barrier(jnp.sum(after * seq_lengths[None, :], 1)))

def rms_norm(values, gain):
    return values * lax.rsqrt(lax.optimization_barrier(jnp.mean(values * values, -1, keepdims=True)) + EPS) * gain

def attend_group(operands):
    q_group, k_group, v_group, seq_lengths = operands
    total = q_group.shape[0]
    repeat = HEADS // KV_HEADS
    index = jnp.arange(total, dtype=jnp.int32)
    seq_ids = seq_info(index, seq_lengths)[0]
    block = math.gcd(total, 512)
    keys_all = k_group.reshape(total, KV_HEADS, HEAD)
    values_all = v_group.reshape(total, KV_HEADS, HEAD)

    def one_block(pieces):
        q_block, q_index, q_seq = pieces
        raw = jnp.einsum('qgrd,kgd->grqk', q_block, keys_all, precision=HIGH) * HEAD ** (-0.5)
        raw = low_back(raw)
        mask = (q_seq[:, None] == seq_ids[None, :]) & (index[None, :] <= q_index[:, None])
        masked = jnp.where(mask[None, None], raw, NEG)
        shifted = masked - lax.optimization_barrier(jnp.max(masked, -1, keepdims=True))
        weights = jnp.exp(shifted)
        probs = weights / lax.optimization_barrier(jnp.sum(weights, -1, keepdims=True))
        return jnp.einsum('grqk,kgd->qgrd', low(probs), values_all, precision=HIGH)
    outs = lax.map(jax.checkpoint(one_block), (q_group.reshape(total // block, block, KV_HEADS, repeat, HEAD), index.reshape(-1, block), seq_ids.reshape(-1, block)))
    return outs.reshape(total, HEADS * HEAD)

def run_expert(operands):
    rows, gate_w, up_w, down_w = operands
    gate_pre = low_back(jnp.dot(rows, gate_w, precision=HIGH))
    up_pre = low_back(jnp.dot(rows, up_w, precision=HIGH))
    hidden = low(gate_pre * jax.nn.sigmoid(gate_pre) * up_pre)
    return low(low_back(jnp.dot(hidden, down_w, precision=HIGH)))

def reference(layer_input, lengths, expert_ids, gate_weights, attn_gain, wq, wk, wv, wo, moe_gain, w_gate, w_up, w_down, cotangent):
    groups, total, width = layer_input.shape
    index = jnp.arange(total, dtype=jnp.int32)

    def positions_of(row):
        return seq_info(index, row)[1]
    positions = jax.vmap(positions_of)(lengths).reshape(-1)
    cosine, sine = rope_tables(positions, HEAD)
    blocks = groups * N_CTX
    flat_ids = expert_ids.reshape(blocks, TOK_DEV * TOPK)
    onehot = (flat_ids[:, :, None] == jnp.arange(EXPERTS, dtype=jnp.int32)[None, None, :]).astype(jnp.int32)
    rank = lax.optimization_barrier(jnp.sum((jnp.cumsum(onehot, 1) - 1) * onehot, 2))
    target = ((flat_ids * blocks + jnp.arange(blocks, dtype=jnp.int32)[:, None]) * CAP + rank).reshape(-1)
    per_expert = blocks * CAP
    gates = gate_weights.reshape(-1, TOPK)

    def layer(layer_arg, gain_a, q_w, k_w, v_w, o_w, gain_m, gate_w, up_w, down_w):
        flat_input = layer_arg.reshape(-1, width)
        attn_input = low_back(flat_input)
        normed1 = low(rms_norm(attn_input, gain_a))
        q_raw = jnp.dot(normed1, q_w, precision=HIGH)
        k_raw = jnp.dot(normed1, k_w, precision=HIGH)
        v_raw = jnp.dot(normed1, v_w, precision=HIGH)
        q_rot = low(rotate(low_back(q_raw).reshape(-1, HEADS, HEAD), cosine, sine)).reshape(groups, total, HEADS * HEAD)
        k_rot = low(rotate(low_back(k_raw).reshape(-1, KV_HEADS, HEAD), cosine, sine)).reshape(groups, total, KV_HEADS * HEAD)
        v_low = low(low_back(v_raw)).reshape(groups, total, KV_HEADS * HEAD)
        attended = lax.map(attend_group, (q_rot, k_rot, v_low, lengths))
        attended = low(low_back(attended.reshape(-1, HEADS * HEAD)))
        attn_rows = low(low_back(jnp.dot(attended, o_w, precision=HIGH)))
        resid = flat_input + attn_rows
        normed2 = low(rms_norm(resid, gain_m))
        buffer = jnp.zeros((EXPERTS * per_expert, width), jnp.float32).at[target].set(jnp.repeat(normed2, TOPK, axis=0))
        buffer = low_back(buffer)
        expert_out = lax.map(jax.checkpoint(run_expert), (buffer.reshape(EXPERTS, per_expert, width), gate_w, up_w, down_w))
        picked = expert_out.reshape(-1, width)[target].reshape(-1, TOPK, width)
        moe = lax.optimization_barrier(jnp.sum(gates[:, :, None] * picked, 1))
        return (resid + moe).reshape(groups, total, width)
    params = tuple((value.astype(jnp.float32) for value in (layer_input, attn_gain, wq, wk, wv, wo, moe_gain, w_gate, w_up, w_down)))
    result, pull = jax.vjp(layer, *params)
    grads = pull(cotangent.astype(jnp.float32))
    return (result.astype(jnp.bfloat16), grads[0].astype(jnp.bfloat16), grads[1], grads[2], grads[3], grads[4], grads[5], grads[6], grads[7], grads[8], grads[9])
```

```python
import math

import jax
import jax.numpy as jnp
from jax import lax
from jax.experimental import pallas as pl
from jax.experimental.pallas import tpu as pltpu
from jax.sharding import PartitionSpec as P

HEADS = 12
KV_HEADS = 2
HEAD = 128
TOPK = 4
REPEAT = HEADS // KV_HEADS
HQ = HEADS * HEAD
KVW = KV_HEADS * HEAD
LANES = 128

EPS = 1e-06
ROPE_BASE = 10000.0
NEG = -1e30
BF = jnp.bfloat16
F32 = jnp.float32
NN = ((1,), (0,))
NT = ((1,), (1,))
TN = ((0,), (0,))
ANY = pl.BlockSpec(memory_space=pl.ANY)
MIB = 1024 * 1024


def mm(left, right, dims=NN):
    return lax.dot_general(left, right, (dims, ((), ())), preferred_element_type=F32)


def params(grid_rank, limit=56):
    return pltpu.CompilerParams(
        dimension_semantics=("arbitrary",) * grid_rank, vmem_limit_bytes=limit * MIB
    )


def cost(flops, size, exps=0):
    return pl.CostEstimate(flops=int(flops), bytes_accessed=int(size), transcendentals=int(exps))


def sds(shape, dtype):
    return jax.ShapeDtypeStruct(shape, dtype)


def whole(shape):
    return pl.BlockSpec(shape, lambda *_: (0,) * len(shape))


class Ring:
    def __init__(self, count):
        self.count = count
        self.low_pair = count == 8
        self.length = count // 2
        self.me = lax.axis_index("ctx")
        if self.low_pair:
            self.line, self.pair = self.me // 2, self.me % 2
        else:
            self.line, self.pair = self.me % self.length, self.me // self.length
        if self.length == 4:
            self.table = [[0, 1, 2, 3], [1, 0, 2, 3], [2, 3, 1, 0], [3, 2, 1, 0]]
        else:
            self.table = [
                [(place + step) % self.length for step in range(self.length)]
                for place in range(self.length)
            ]

    def index(self, line, pair):
        return line * 2 + pair if self.low_pair else pair * self.length + line

    def move(self, array, hops):
        pairs = [
            (self.index(source, side), self.index(target, side))
            for source, target in hops
            for side in (0, 1)
        ]
        return lax.ppermute(array, "ctx", pairs)

    def swap(self, array):
        pairs = [
            (self.index(place, side), self.index(place, 1 - side))
            for place in range(self.length)
            for side in (0, 1)
        ]
        return lax.ppermute(array, "ctx", pairs)

    def sources(self):
        line = jnp.asarray(self.table, jnp.int32)[self.line]
        side = jnp.stack([self.pair, 1 - self.pair]).astype(jnp.int32)
        return self.index(line[:, None], side[None, :]).reshape(-1).astype(jnp.int32)

    def gather(self, array):
        if self.length != 4:
            everything = lax.all_gather(array, "ctx", axis=0)
            order = self.sources()
            rows = [
                lax.dynamic_index_in_dim(everything, order[slot], 0, keepdims=False)
                for slot in range(self.count)
            ]
            return [(rows[2 * step], rows[2 * step + 1]) for step in range(self.length)]
        ends = [(1, 0), (2, 3)]
        middle = [(1, 2), (2, 1)]
        couples = [(0, 1), (1, 0), (2, 3), (3, 2)]
        first = self.move(array, couples)
        cross = self.move(array, middle)
        swapped = self.swap(array)
        outward = self.move(cross, ends)
        cross_two = self.move(first, middle)
        second = cross + outward
        outward_two = self.move(cross_two, ends)
        third = cross_two + outward_two
        return [
            (array, swapped),
            (first, self.swap(first)),
            (second, self.swap(second)),
            (third, self.swap(third)),
        ]

    def scatter(self, parts):
        if self.length != 4:
            order = self.sources()
            rows = jnp.stack([part for couple in parts for part in couple])
            placed = jnp.zeros_like(rows).at[order].set(rows)
            return [lax.psum_scatter(placed, "ctx", scatter_dimension=0, tiled=False)]
        inward = [(0, 1), (3, 2)]
        middle = [(1, 2), (2, 1)]
        couples = [(0, 1), (1, 0), (2, 3), (3, 2)]
        third = parts[3][0] + self.swap(parts[3][1])
        from_end = self.move(third, inward)
        second = parts[2][0] + self.swap(parts[2][1])
        from_end_two = self.move(second, inward)
        crossed = self.move(third + from_end, middle)
        first = parts[1][0] + self.swap(parts[1][1])
        crossed_two = self.move(second + from_end_two, middle)
        last = self.move(first + crossed, couples)
        swapped = self.swap(parts[0][1])
        return [parts[0][0], swapped, crossed_two, last]


def neighbour(array, axis_size, bit):
    pairs = [(index, index ^ (1 << bit)) for index in range(axis_size)]
    return lax.ppermute(array, "fsdp", pairs)


def gather_shards(array, axis_size):
    slots = {0: array}
    bits = axis_size.bit_length() - 1
    for bit in reversed(range(bits)):
        for slot in list(slots):
            slots[slot | (1 << bit)] = neighbour(slots[slot], axis_size, bit)
    return [slots[slot] for slot in range(axis_size)]


def scatter_shards(slots, axis_size):
    bits = axis_size.bit_length() - 1
    slots = dict(enumerate(slots))
    for bit in range(bits):
        far = [slot for slot in slots if slot >> bit & 1]
        near = {slot: value for slot, value in slots.items() if not slot >> bit & 1}
        for slot in far:
            arrived = neighbour(slots[slot], axis_size, bit)
            if bit == bits - 1:
                return near[0], arrived
            near[slot ^ (1 << bit)] = near[slot ^ (1 << bit)] + arrived
        slots = near
    return slots[0], jnp.zeros_like(slots[0])


def turn(values, cosine, sine):
    return values * cosine + pltpu.roll(values, HEAD // 2, 1) * sine


def qkv_kernel(x_ref, w_ref, g_ref, cos_ref, sin_ref, q_ref, kv_ref, low_ref, gain_ref):
    step = pl.program_id(0)
    blocks = HQ // 512

    @pl.when(step == 0)
    def _():
        gains = jnp.transpose(g_ref[...].astype(F32))
        gain_ref[...] = gains[0:8]
        wide = x_ref[...].astype(F32)
        scale = lax.rsqrt(jnp.mean(wide * wide, -1, keepdims=True) + EPS)
        low_ref[...] = (wide * scale * gains[0:1]).astype(BF)

    raw = mm(low_ref[...], w_ref[...])
    cosine, sine = cos_ref[...], sin_ref[...]

    def turned(count):
        return [
            turn(raw[:, head * HEAD : (head + 1) * HEAD], cosine, sine).astype(BF)
            for head in range(count)
        ]

    @pl.when(step < blocks)
    def _():
        for head, value in enumerate(turned(4)):
            q_ref[:, head * HEAD : (head + 1) * HEAD] = value

    @pl.when(step == blocks)
    def _():
        for head, value in enumerate(turned(KV_HEADS)):
            kv_ref[:, head * HEAD : (head + 1) * HEAD] = value
        kv_ref[:, KVW:] = raw[:, KVW:].astype(BF)


def qkv_call(x, w_full, cosine, sine):
    tokens, width = x.shape
    blocks = HQ // 512
    return pl.pallas_call(
        qkv_kernel,
        name="qkv",
        grid=(blocks + 1,),
        in_specs=[
            whole((tokens, width)),
            pl.BlockSpec((width, 512), lambda i: (0, i)),
            pl.BlockSpec((width, LANES), lambda i: (0, (HQ + 2 * KVW) // LANES)),
            whole((tokens, HEAD)),
            whole((tokens, HEAD)),
        ],
        out_specs=[
            pl.BlockSpec((tokens, 512), lambda i: (0, jnp.minimum(i, HQ // 512 - 1))),
            whole((tokens, 2 * KVW)),
            whole((tokens, width)),
            whole((8, width)),
        ],
        out_shape=[
            sds((tokens, HQ), BF),
            sds((tokens, 2 * KVW), BF),
            sds((tokens, width), BF),
            sds((8, width), F32),
        ],
        compiler_params=params(1),
        cost_estimate=cost(2 * tokens * width * 2048, 10 * MIB),
    )(x, w_full, w_full, cosine, sine)


def load_kv(order_ref, slots, kv_all, sems):
    copies = [
        pltpu.make_async_copy(slot, kv_all.at[order_ref[2 + place]], sems.at[place])
        for place, slot in enumerate(slots)
    ]
    for copy in copies:
        copy.start()
    for copy in copies:
        copy.wait()


def attn_kernel(count, order_ref, q_ref, start_ref, *rest):
    slots = rest[:count]
    out_ref, total_ref, kv_all, totals, sems = rest[count:]
    head = pl.program_id(0)
    tokens = q_ref.shape[0]
    scale = HEAD ** (-0.5)
    me, first = order_ref[0], order_ref[1]

    @pl.when(head == 0)
    def _():
        load_kv(order_ref, slots, kv_all, sems)
        totals[...] = jnp.zeros_like(totals)

    group = head // REPEAT
    q = q_ref[...]
    start = start_ref[:, 0:1]
    rows = me * tokens + lax.broadcasted_iota(jnp.int32, (tokens, 1), 0)
    lanes = lax.broadcasted_iota(jnp.int32, (1, tokens), 1)

    def visit(block, carry):
        peak, total, acc = carry
        key = kv_all[block, :, pl.ds(pl.multiple_of(group * HEAD, HEAD), HEAD)]
        value = kv_all[block, :, pl.ds(pl.multiple_of(KVW + group * HEAD, HEAD), HEAD)]
        index = block * tokens + lanes
        mask = (index >= start) & (index <= rows)
        scores = jnp.where(mask, mm(q, key, NT) * scale, NEG)
        new_peak = jnp.maximum(peak, jnp.max(scores, -1, keepdims=True))
        weights = jnp.exp(scores - new_peak)
        keep = jnp.exp(peak - new_peak)
        total = total * keep + jnp.sum(weights, -1, keepdims=True)
        acc = acc * keep + mm(weights.astype(BF), value)
        return new_peak, total, acc

    begin = (
        jnp.full((tokens, 1), NEG, F32),
        jnp.zeros((tokens, 1), F32),
        jnp.zeros((tokens, HEAD), F32),
    )
    state = visit(me, begin)
    peak, total, acc = lax.fori_loop(first, me, visit, state)
    out_ref[...] = (acc / total).astype(BF)
    here = lax.broadcasted_iota(jnp.int32, (tokens, LANES), 1) == head
    totals[...] = jnp.where(here, peak + jnp.log(total), totals[...])

    @pl.when(head == HEADS - 1)
    def _():
        total_ref[...] = jnp.transpose(totals[...])[0:16]


def attn_call(order, q, start, slots):
    tokens = q.shape[0]
    count = len(slots)
    grid = pltpu.PrefetchScalarGridSpec(
        num_scalar_prefetch=1,
        grid=(HEADS,),
        in_specs=[
            pl.BlockSpec((tokens, HEAD), lambda h, _: (0, h)),
            pl.BlockSpec((tokens, LANES), lambda h, _: (0, 0)),
        ]
        + [ANY] * count,
        out_specs=[
            pl.BlockSpec((tokens, HEAD), lambda h, _: (0, h)),
            pl.BlockSpec((16, tokens), lambda h, _: (0, 0)),
        ],
        scratch_shapes=[
            pltpu.VMEM((count, tokens, 2 * KVW), BF),
            pltpu.VMEM((tokens, LANES), F32),
            pltpu.SemaphoreType.DMA((count,)),
        ],
    )
    return pl.pallas_call(
        lambda *refs: attn_kernel(count, *refs),
        name="attention",
        grid_spec=grid,
        out_shape=[sds((tokens, HQ), BF), sds((16, tokens), F32)],
        compiler_params=params(1),
        cost_estimate=cost(4 * tokens * tokens * count * HQ, 6 * MIB),
    )(order, q, start, *slots)


def attn_back_kernel(count, order_ref, q_ref, do_ref, start_ref, total_ref, delta_ref, *rest):
    cos_ref, sin_ref = rest[:2]
    slots = rest[2 : 2 + count]
    dq_ref = rest[2 + count]
    outs = rest[3 + count : 3 + 2 * count]
    kv_all, d_k, d_v, packed, sems = rest[3 + 2 * count :]
    head = pl.program_id(0)
    tokens = q_ref.shape[0]
    scale = HEAD ** (-0.5)
    me, first = order_ref[0], order_ref[1]

    @pl.when(head == 0)
    def _():
        load_kv(order_ref, slots, kv_all, sems)
        d_k[...] = jnp.zeros_like(d_k)
        d_v[...] = jnp.zeros_like(d_v)

    group = head // REPEAT
    own = pl.ds(pl.multiple_of(group * HEAD, HEAD), HEAD)
    q = q_ref[...]
    grad = do_ref[...]
    start = start_ref[0:1, :]
    log_total = total_ref[pl.ds(head, 1), :]
    delta = delta_ref[pl.ds(head, 1), :]
    columns = me * tokens + lax.broadcasted_iota(jnp.int32, (1, tokens), 1)
    sublanes = lax.broadcasted_iota(jnp.int32, (tokens, 1), 0)

    def visit(block, d_q):
        key = kv_all[block, :, own]
        value = kv_all[block, :, pl.ds(pl.multiple_of(KVW + group * HEAD, HEAD), HEAD)]
        index = block * tokens + sublanes
        mask = (index >= start) & (index <= columns)
        scores = jnp.where(mask, mm(key, q, NT) * scale - log_total, NEG)
        probs = jnp.exp(scores)
        grad_probs = mm(value, grad, NT)
        grad_scores = (probs * (grad_probs - delta)).astype(BF)
        d_v[block, :, own] += mm(probs.astype(BF), grad)
        d_k[block, :, own] += mm(grad_scores, q)
        return d_q + mm(grad_scores, key, TN)

    d_q = lax.fori_loop(first, me + 1, visit, jnp.zeros((tokens, HEAD), F32))
    dq_ref[...] = turn(d_q * scale, cos_ref[...], -sin_ref[...]).astype(BF)

    @pl.when(head == HEADS - 1)
    def _():
        copies = []
        for place in range(count):
            block = order_ref[2 + place]
            packed[place, :, 0:KVW] = d_k[block].astype(BF)
            packed[place, :, KVW:] = d_v[block].astype(BF)
            copies.append(pltpu.make_async_copy(packed.at[place], outs[place], sems.at[place]))
            copies[-1].start()
        for copy in copies:
            copy.wait()


def attn_back_call(order, q, grad, start, log_total, delta, cosine, sine, slots):
    tokens = q.shape[0]
    count = len(slots)

    def column(h, _):
        return (0, h)

    def fixed(h, _):
        return (0, 0)

    grid = pltpu.PrefetchScalarGridSpec(
        num_scalar_prefetch=1,
        grid=(HEADS,),
        in_specs=[
            pl.BlockSpec((tokens, HEAD), column),
            pl.BlockSpec((tokens, HEAD), column),
            pl.BlockSpec((8, tokens), fixed),
            pl.BlockSpec((16, tokens), fixed),
            pl.BlockSpec((16, tokens), fixed),
            pl.BlockSpec((tokens, HEAD), fixed),
            pl.BlockSpec((tokens, HEAD), fixed),
        ]
        + [ANY] * count,
        out_specs=[pl.BlockSpec((tokens, HEAD), column)] + [ANY] * count,
        scratch_shapes=[
            pltpu.VMEM((count, tokens, 2 * KVW), BF),
            pltpu.VMEM((count, tokens, KVW), F32),
            pltpu.VMEM((count, tokens, KVW), F32),
            pltpu.VMEM((count, tokens, 2 * KVW), BF),
            pltpu.SemaphoreType.DMA((count,)),
        ],
    )
    return pl.pallas_call(
        lambda *refs: attn_back_kernel(count, *refs),
        name="attention_back",
        grid_spec=grid,
        out_shape=[sds((tokens, HQ), BF)] + [sds((tokens, 2 * KVW), BF)] * count,
        compiler_params=params(1),
        cost_estimate=cost(10 * tokens * tokens * count * HQ, 10 * MIB),
    )(order, q, grad, start, log_total, delta, cosine, sine, *slots)


def out_kernel(x_ref, a_ref, w_ref, gain_ref, rows_ref, low_ref):
    rows = mm(a_ref[...], w_ref[...], NT).astype(BF)
    rows_ref[...] = rows
    resid = x_ref[...].astype(F32) + rows.astype(F32)
    scale = lax.rsqrt(jnp.mean(resid * resid, -1, keepdims=True) + EPS)
    low_ref[...] = (resid * scale * gain_ref[1:2]).astype(BF)


def out_call(x, attended, wo_t, gains):
    tokens, width = x.shape
    tile = 128
    return pl.pallas_call(
        out_kernel,
        name="attention_out",
        grid=(tokens // tile,),
        in_specs=[
            pl.BlockSpec((tile, width), lambda i: (i, 0)),
            pl.BlockSpec((tile, HQ), lambda i: (i, 0)),
            whole((width, HQ)),
            whole((8, width)),
        ],
        out_specs=[pl.BlockSpec((tile, width), lambda i: (i, 0))] * 2,
        out_shape=[sds((tokens, width), BF)] * 2,
        compiler_params=params(1),
        cost_estimate=cost(2 * tokens * width * HQ, 10 * MIB),
    )(x, attended, wo_t, gains)


def weight_copies(shards, own, kinds, held, sems):
    size = shards[0].shape[2]
    groups = []
    for expert in range(shards[0].shape[1]):
        copies = []
        for slot, shard in enumerate(shards):
            rows = pl.ds(pl.multiple_of((own ^ slot) * size, 16), size)
            for place, kind in enumerate(kinds):
                copies.append(
                    pltpu.make_async_copy(
                        shard.at[kind, expert],
                        held.at[place, expert, rows],
                        sems.at[place, expert, slot],
                    )
                )
        groups.append(copies)
    return groups


def fetch_weights(shards, own, kinds, held, sems):
    groups = weight_copies(shards, own, kinds, held, sems)
    step = pl.program_id(0)

    @pl.when(step == 0)
    def _():
        for copies in groups:
            for copy in copies:
                copy.start()

    for expert, copies in enumerate(groups):

        @pl.when(step == expert)
        def _():
            for copy in copies:
                copy.wait()


def route_kernel(shards_of, capacity, order_ref, d0_ref, d1_ref, *rest):
    shards = rest[:shards_of]
    p0_ref, p1_ref, gate_ref, rows_ref, hid_ref, held, sems = rest[shards_of:]
    expert = pl.program_id(0)
    tokens = d0_ref.shape[0]
    width = rows_ref.shape[2]
    fetch_weights(shards, order_ref[0], (2,), held, sems)
    wanted = (order_ref[1] * held.shape[1] + expert).astype(F32)
    before = lax.broadcasted_iota(jnp.int32, (tokens, tokens), 0) < lax.broadcasted_iota(
        jnp.int32, (tokens, tokens), 1
    )
    before = jnp.where(before, 1.0, 0.0).astype(BF)
    places = lax.broadcasted_iota(jnp.int32, (capacity, tokens), 0).astype(F32)
    for side, (ref, p_ref) in enumerate(((d0_ref, p0_ref), (d1_ref, p1_ref))):
        info = jnp.transpose(ref[:, width:].astype(F32))
        chosen = jnp.where(info[0:TOPK] == wanted, 1.0, 0.0)
        gate = jnp.sum(
            chosen * (info[TOPK : 2 * TOPK] + info[2 * TOPK : 3 * TOPK] + info[3 * TOPK : 4 * TOPK]),
            0,
            keepdims=True,
        )
        named = jnp.sum(chosen, 0, keepdims=True)
        rank = mm(jnp.broadcast_to(named, (8, tokens)).astype(BF), before)[0:1]
        picks = jnp.where((places == rank) & (named > 0.5), 1.0, 0.0)
        weight = jnp.sum(picks * gate, 1, keepdims=True)
        picks = picks.astype(BF)
        p_ref[0] = picks
        span = slice(side * capacity, (side + 1) * capacity)
        gate_ref[0, span] = jnp.broadcast_to(weight, (capacity, LANES))
        rows_ref[0, span] = (mm(picks, ref[:, :width]) * weight).astype(BF)
    hid_ref[0] = mm(rows_ref[0], held[0, expert])


def route_call(order, grads, shards, capacity, width):
    tokens = grads[0].shape[0]
    _, experts, size, hidden = shards[0].shape
    rows = 2 * capacity
    by_expert = lambda e, _: (e, 0, 0)
    grid = pltpu.PrefetchScalarGridSpec(
        num_scalar_prefetch=1,
        grid=(experts,),
        in_specs=[pl.BlockSpec(grads[0].shape, lambda e, _: (0, 0))] * 2 + [ANY] * len(shards),
        out_specs=[pl.BlockSpec((1, capacity, tokens), by_expert)] * 2
        + [
            pl.BlockSpec((1, rows, LANES), by_expert),
            pl.BlockSpec((1, rows, width), by_expert),
            pl.BlockSpec((1, rows, hidden), by_expert),
        ],
        scratch_shapes=[
            pltpu.VMEM((1, experts, width, hidden), BF),
            pltpu.SemaphoreType.DMA((1, experts, len(shards))),
        ],
    )
    return pl.pallas_call(
        lambda *refs: route_kernel(len(shards), capacity, *refs),
        name="route",
        grid_spec=grid,
        out_shape=[sds((experts, capacity, tokens), BF)] * 2
        + [
            sds((experts, rows, LANES), F32),
            sds((experts, rows, width), BF),
            sds((experts, rows, hidden), F32),
        ],
        compiler_params=params(1),
        cost_estimate=cost(2 * experts * rows * width * (hidden + tokens), 14 * MIB),
    )(order, *grads, *shards)


def expert_kernel(shards_of, capacity, order_ref, x0_ref, x1_ref, p0_ref, p1_ref, gh_ref, *rest):
    shards = rest[:shards_of]
    rows_ref, hid_ref, gg_ref, gu_ref, out0_ref, out1_ref, held, slot, acc, sems = rest[shards_of:]
    expert = pl.program_id(0)
    hidden = gh_ref.shape[2]
    width = x0_ref.shape[1]
    fetch_weights(shards, order_ref[0], (0, 1), held, sems)
    for side, (ref, p_ref) in enumerate(((x0_ref, p0_ref), (x1_ref, p1_ref))):
        span = slice(side * capacity, (side + 1) * capacity)
        rows_ref[0, span] = mm(p_ref[0], ref[...]).astype(BF)
    rows = rows_ref[0]
    tile = 256
    for start in range(0, hidden, tile):
        span = slice(start, start + tile)
        gate = mm(rows, held[0, expert, :, span])
        up = mm(rows, held[1, expert, :, span])
        grad = gh_ref[0, :, span]
        sigma = 1.0 / (1.0 + jnp.exp(-gate))
        active = gate * sigma
        hid_ref[0, :, span] = (active * up).astype(BF)
        gg_ref[0, :, span] = (grad * up * (sigma * (1.0 + gate * (1.0 - sigma)))).astype(BF)
        gu_ref[0, :, span] = (grad * active).astype(BF)
    tile = 512
    for start in range(0, width, tile):
        span = slice(start, start + tile)
        slot[:, span] = (
            mm(gg_ref[0], held[0, expert, span, :], NT)
            + mm(gu_ref[0], held[1, expert, span, :], NT)
        ).astype(BF)
    for side, (p_ref, out_ref) in enumerate(((p0_ref, out0_ref), (p1_ref, out1_ref))):
        span = slice(side * capacity, (side + 1) * capacity)
        term = mm(p_ref[0], slot[span], TN)

        @pl.when(expert == 0)
        def _():
            acc[side] = term

        @pl.when(expert > 0)
        def _():
            acc[side] += term

        @pl.when(expert == pl.num_programs(0) - 1)
        def _():
            out_ref[...] = acc[side].astype(BF)


def expert_call(order, xs, picks, grad_hidden, shards, capacity):
    tokens, width = xs[0].shape
    _, experts, size, hidden = shards[0].shape
    rows = 2 * capacity
    by_expert = lambda e, _: (e, 0, 0)
    fixed = lambda e, _: (0, 0)
    grid = pltpu.PrefetchScalarGridSpec(
        num_scalar_prefetch=1,
        grid=(experts,),
        in_specs=[pl.BlockSpec((tokens, width), fixed)] * 2
        + [pl.BlockSpec((1, capacity, tokens), by_expert)] * 2
        + [pl.BlockSpec((1, rows, hidden), by_expert)]
        + [ANY] * len(shards),
        out_specs=[pl.BlockSpec((1, rows, width), by_expert)]
        + [pl.BlockSpec((1, rows, hidden), by_expert)] * 3
        + [pl.BlockSpec((tokens, width), fixed)] * 2,
        scratch_shapes=[
            pltpu.VMEM((2, experts, width, hidden), BF),
            pltpu.VMEM((rows, width), BF),
            pltpu.VMEM((2, tokens, width), F32),
            pltpu.SemaphoreType.DMA((2, experts, len(shards))),
        ],
    )
    return pl.pallas_call(
        lambda *refs: expert_kernel(len(shards), capacity, *refs),
        name="experts",
        grid_spec=grid,
        out_shape=[sds((experts, rows, width), BF)]
        + [sds((experts, rows, hidden), BF)] * 3
        + [sds((tokens, width), BF)] * 2,
        compiler_params=params(1),
        cost_estimate=cost(2 * experts * rows * width * (4 * hidden + 2 * tokens), 24 * MIB),
    )(order, *xs, *picks, grad_hidden, *shards)


def down_kernel(shards_of, capacity, order_ref, hid_ref, gate_ref, p0_ref, p1_ref, *rest):
    shards = rest[:shards_of]
    out0_ref, out1_ref, held, slot, acc, sems = rest[shards_of:]
    expert = pl.program_id(0)
    width = out0_ref.shape[1]
    fetch_weights(shards, order_ref[0], (2,), held, sems)
    tile = 512
    for start in range(0, width, tile):
        span = slice(start, start + tile)
        made = mm(hid_ref[0], held[0, expert, span, :], NT).astype(BF).astype(F32)
        slot[:, span] = (made * gate_ref[0, :, 0:1]).astype(BF)
    for side, (p_ref, out_ref) in enumerate(((p0_ref, out0_ref), (p1_ref, out1_ref))):
        span = slice(side * capacity, (side + 1) * capacity)
        term = mm(p_ref[0], slot[span], TN)

        @pl.when(expert == 0)
        def _():
            acc[side] = term

        @pl.when(expert > 0)
        def _():
            acc[side] += term

        @pl.when(expert == pl.num_programs(0) - 1)
        def _():
            out_ref[...] = acc[side].astype(BF)


def down_call(order, hid, gates, picks, shards, capacity, width):
    tokens = picks[0].shape[2]
    _, experts, size, hidden = shards[0].shape
    rows = 2 * capacity
    by_expert = lambda e, _: (e, 0, 0)
    fixed = lambda e, _: (0, 0)
    grid = pltpu.PrefetchScalarGridSpec(
        num_scalar_prefetch=1,
        grid=(experts,),
        in_specs=[
            pl.BlockSpec((1, rows, hidden), by_expert),
            pl.BlockSpec((1, rows, LANES), by_expert),
        ]
        + [pl.BlockSpec((1, capacity, tokens), by_expert)] * 2
        + [ANY] * len(shards),
        out_specs=[pl.BlockSpec((tokens, width), fixed)] * 2,
        scratch_shapes=[
            pltpu.VMEM((1, experts, width, hidden), BF),
            pltpu.VMEM((rows, width), BF),
            pltpu.VMEM((2, tokens, width), F32),
            pltpu.SemaphoreType.DMA((1, experts, len(shards))),
        ],
    )
    return pl.pallas_call(
        lambda *refs: down_kernel(len(shards), capacity, *refs),
        name="experts_down",
        grid_spec=grid,
        out_shape=[sds((tokens, width), BF)] * 2,
        compiler_params=params(1),
        cost_estimate=cost(2 * experts * rows * width * (hidden + tokens), 14 * MIB),
    )(order, hid, gates, *picks, *shards)


def weight_grad_kernel(chunks, shards_of, order_ref, *rest):
    xs, gs = rest[:chunks], rest[chunks : 2 * chunks]
    ggs, gus = rest[2 * chunks : 3 * chunks], rest[3 * chunks : 4 * chunks]
    hids = rest[4 * chunks : 5 * chunks]
    outs = rest[5 * chunks : 5 * chunks + shards_of]
    held, sems = rest[5 * chunks + shards_of :]
    expert = pl.program_id(0)
    width = xs[0].shape[2]
    size = outs[0].shape[2]
    own = order_ref[0]

    def copies(kind, which):
        return [
            pltpu.make_async_copy(
                held.at[kind, pl.ds(pl.multiple_of((own ^ slot) * size, 16), size)],
                out.at[kind, which],
                sems.at[kind, slot],
            )
            for slot, out in enumerate(outs)
        ]

    for kind, (lefts, rights) in enumerate(((xs, ggs), (xs, gus), (gs, hids))):

        @pl.when(expert > 0)
        def _():
            for copy in copies(kind, expert - 1):
                copy.wait()

        tile = 256

        @pl.loop(0, width // tile)
        def _(step):
            span = pl.ds(pl.multiple_of(step * tile, tile), tile)
            total = mm(lefts[0][0, :, span], rights[0][0], TN)
            for left, right in zip(lefts[1:], rights[1:]):
                total += mm(left[0, :, span], right[0], TN)
            held[kind, span] = total.astype(BF)

        for copy in copies(kind, expert):
            copy.start()

    @pl.when(expert == pl.num_programs(0) - 1)
    def _():
        for kind in range(3):
            for copy in copies(kind, expert):
                copy.wait()


def weight_grad_call(order, xs, gs, ggs, gus, hids, shards_of):
    chunks = len(xs)
    experts, rows, width = xs[0].shape
    hidden = ggs[0].shape[2]
    size = width // shards_of
    by_expert = lambda e, _: (e, 0, 0)
    grid = pltpu.PrefetchScalarGridSpec(
        num_scalar_prefetch=1,
        grid=(experts,),
        in_specs=[pl.BlockSpec((1, rows, width), by_expert)] * (2 * chunks)
        + [pl.BlockSpec((1, rows, hidden), by_expert)] * (3 * chunks),
        out_specs=[ANY] * shards_of,
        scratch_shapes=[
            pltpu.VMEM((3, width, hidden), BF),
            pltpu.SemaphoreType.DMA((3, shards_of)),
        ],
    )
    return pl.pallas_call(
        lambda *refs: weight_grad_kernel(chunks, shards_of, *refs),
        name="expert_weight_grads",
        grid_spec=grid,
        out_shape=[sds((3, experts, size, hidden), BF)] * shards_of,
        compiler_params=params(1),
        cost_estimate=cost(6 * experts * chunks * rows * width * hidden, 40 * MIB),
    )(order, *xs, *gs, *ggs, *gus, *hids)


def resid_back_kernel(
    terms, x_ref, rows_ref, dy_ref, gain_ref, w_ref, att_ref, *rest
):
    parts = rest[:terms]
    resid_ref, attn_ref, do_ref, delta_ref, gain_out, deltas = rest[terms:]
    step = pl.program_id(0)
    grad = parts[0][...].astype(F32)
    for part in parts[1:]:
        grad += part[...].astype(F32)
    resid = x_ref[...].astype(F32) + rows_ref[...].astype(F32)
    scale = lax.rsqrt(jnp.mean(resid * resid, -1, keepdims=True) + EPS)
    normed = resid * scale
    product = grad * normed
    partial = jnp.sum(product, 0, keepdims=True)

    @pl.when(step == 0)
    def _():
        gain_out[...] = jnp.broadcast_to(partial, gain_out.shape)

    @pl.when(step > 0)
    def _():
        gain_out[...] += partial

    gain = gain_ref[1:2]
    mean = jnp.mean(product * gain, -1, keepdims=True)
    total = dy_ref[...].astype(F32) + scale * (grad * gain - normed * mean)
    resid_ref[...] = total
    low = total.astype(BF)
    attn_ref[...] = low
    back = mm(low, w_ref[...]).astype(BF)
    do_ref[...] = back
    each = back.astype(F32) * att_ref[...].astype(F32)
    lanes = lax.broadcasted_iota(jnp.int32, deltas.shape, 1)
    made = jnp.zeros(deltas.shape, F32)
    for head in range(HEADS):
        value = jnp.sum(each[:, head * HEAD : (head + 1) * HEAD], -1, keepdims=True)
        made = jnp.where(lanes == head, value, made)
    deltas[...] = made
    delta_ref[...] = jnp.transpose(deltas[...])[0:16]


def resid_back_call(x, rows, dy, gains, wo_t, attended, parts):
    tokens, width = x.shape
    tile = 128
    by_row = lambda i: (i, 0)
    return pl.pallas_call(
        lambda *refs: resid_back_kernel(len(parts), *refs),
        name="resid_back",
        grid=(tokens // tile,),
        in_specs=[pl.BlockSpec((tile, width), by_row)] * 3
        + [whole((8, width)), whole((width, HQ)), pl.BlockSpec((tile, HQ), by_row)]
        + [pl.BlockSpec((tile, width), by_row)] * len(parts),
        out_specs=[pl.BlockSpec((tile, width), by_row)] * 2
        + [
            pl.BlockSpec((tile, HQ), by_row),
            pl.BlockSpec((16, tile), lambda i: (0, i)),
            whole((8, width)),
        ],
        out_shape=[
            sds((tokens, width), F32),
            sds((tokens, width), BF),
            sds((tokens, HQ), BF),
            sds((16, tokens), F32),
            sds((8, width), F32),
        ],
        scratch_shapes=[pltpu.VMEM((tile, LANES), F32)],
        compiler_params=params(1),
        cost_estimate=cost(2 * tokens * width * HQ, 16 * MIB),
    )(x, rows, dy, gains, wo_t, attended, *parts)


def cross_kernel(left_ref, right_ref, out_ref):
    out_ref[...] = mm(left_ref[...], right_ref[...], TN).astype(out_ref.dtype)


def cross_call(left, right, name):
    tokens, rows = left.shape
    columns = right.shape[1]
    tile = 512 if rows % 512 == 0 else rows
    return pl.pallas_call(
        cross_kernel,
        name=name,
        grid=(rows // tile,),
        in_specs=[pl.BlockSpec((tokens, tile), lambda i: (0, i)), whole((tokens, columns))],
        out_specs=pl.BlockSpec((tile, columns), lambda i: (i, 0)),
        out_shape=sds((rows, columns), BF),
        compiler_params=params(1),
        cost_estimate=cost(2 * tokens * rows * columns, 8 * MIB),
    )(left, right)


def input_q_kernel(dq_ref, w_ref, out_ref):
    out_ref[...] = mm(dq_ref[...], w_ref[...], NT)


def input_q_call(d_q, w_full):
    tokens = d_q.shape[0]
    width = w_full.shape[0]
    tile = 512
    return pl.pallas_call(
        input_q_kernel,
        name="input_grad_q",
        grid=(width // tile,),
        in_specs=[whole((tokens, HQ)), pl.BlockSpec((tile, HQ), lambda i: (i, 0))],
        out_specs=pl.BlockSpec((tokens, tile), lambda i: (0, i)),
        out_shape=sds((tokens, width), F32),
        compiler_params=params(1),
        cost_estimate=cost(2 * tokens * width * HQ, 9 * MIB),
    )(d_q, w_full)


def final_kernel(
    terms, x_ref, low_ref, resid_ref, gq_ref, gain_ref, moe_ref, w_ref, cos_ref, sin_ref, *rest
):
    parts = rest[:terms]
    grad_ref, out_ref = rest[terms:]
    scale_k = HEAD ** (-0.5)
    total = parts[0][...].astype(F32)
    for part in parts[1:]:
        total += part[...].astype(F32)
    cosine, sine = cos_ref[...], -sin_ref[...]
    pieces = [
        turn(total[:, head * HEAD : (head + 1) * HEAD] * scale_k, cosine, sine).astype(BF)
        for head in range(KV_HEADS)
    ]
    low = jnp.concatenate(pieces + [total[:, KVW:].astype(BF)], 1)
    out_ref[:, 0 : 2 * KVW] = mm(low_ref[...], low, TN).astype(BF)
    wide = x_ref[...].astype(F32)
    scale = lax.rsqrt(jnp.mean(wide * wide, -1, keepdims=True) + EPS)
    normed = wide * scale
    grad = gq_ref[...] + mm(low, w_ref[...], NT)
    product = grad * normed
    gain_part = jnp.sum(product, 0, keepdims=True)
    gain = gain_ref[0:1]
    mean = jnp.mean(product * gain, -1, keepdims=True)
    own = (scale * (grad * gain - normed * mean)).astype(BF)
    grad_ref[...] = (resid_ref[...] + own.astype(F32)).astype(BF)
    width = x_ref.shape[1]
    lines = lax.broadcasted_iota(jnp.int32, (LANES, width), 0)
    both = jnp.where(lines == 0, gain_part, jnp.where(lines == 1, moe_ref[0:1], 0.0))
    out_ref[:, 2 * KVW :] = jnp.transpose(both).astype(BF)


def final_call(x, low, resid, grad_q, gains, moe_part, w_full, cosine, sine, parts):
    tokens, width = x.shape
    columns = 2 * KVW + LANES
    return pl.pallas_call(
        lambda *refs: final_kernel(len(parts), *refs),
        name="final",
        grid=(1,),
        in_specs=[whole((tokens, width))] * 4
        + [whole((8, width))] * 2
        + [pl.BlockSpec((width, 2 * KVW), lambda i: (0, HQ // (2 * KVW)))]
        + [whole((tokens, HEAD))] * 2
        + [whole((tokens, 2 * KVW))] * len(parts),
        out_specs=[whole((tokens, width)), whole((width, columns))],
        out_shape=[sds((tokens, width), BF), sds((width, columns), BF)],
        compiler_params=params(1),
        cost_estimate=cost(4 * tokens * width * 2 * KVW, 14 * MIB),
    )(x, low, resid, grad_q, gains, moe_part, w_full, cosine, sine, *parts)


def hold_kernel(count, *refs):
    del count, refs


def hold(arrays, until):
    count = len(arrays)
    return pl.pallas_call(
        lambda *refs: hold_kernel(count, *refs),
        name="hold",
        in_specs=[ANY] * (count + 1),
        out_specs=[ANY] * count,
        out_shape=[sds(array.shape, array.dtype) for array in arrays],
        input_output_aliases={place: place for place in range(count)},
    )(*arrays, until)


def local(
    layer_input,
    lengths,
    expert_ids,
    gate_weights,
    attn_gain,
    wq,
    wk,
    wv,
    wo,
    moe_gain,
    w_gate,
    w_up,
    w_down,
    cotangent,
):
    count = lax.axis_size("ctx")
    shards_of = lax.axis_size("fsdp")
    both = ("ctx", "fsdp")
    ring = Ring(count)
    me = lax.axis_index("ctx").astype(jnp.int32)
    own = lax.axis_index("fsdp").astype(jnp.int32)
    x = layer_input[0]
    dy = cotangent[0]
    tokens, width = x.shape
    exp_dev = w_gate.shape[0]
    experts = exp_dev * count
    capacity = 3 * tokens * TOPK // (2 * experts)

    rows = wq.shape[0]
    gains_part = jnp.concatenate(
        [attn_gain[:, None], moe_gain[:, None], jnp.zeros((rows, LANES - 2), BF)], 1
    )
    w_full = lax.all_gather(
        jnp.concatenate([wq, wk, wv, gains_part], 1), both, axis=0, tiled=True
    )
    wo_t = lax.all_gather(wo.T, both, axis=0, tiled=True)

    shards = gather_shards(
        jnp.stack([w_gate, w_up, jnp.swapaxes(w_down, 1, 2)]), shards_of
    )
    gates = gate_weights[0]
    gate_high = gates.astype(BF)
    rest = gates - gate_high.astype(F32)
    gate_mid = rest.astype(BF)
    gate_low = (rest - gate_mid.astype(F32)).astype(BF)
    info = jnp.concatenate(
        [
            dy,
            expert_ids[0].astype(BF),
            gate_high,
            gate_mid,
            gate_low,
            jnp.zeros((tokens, LANES - 4 * TOPK), BF),
        ],
        1,
    )
    grads = ring.gather(info)

    ends = jnp.cumsum(lengths[0])
    index = me * tokens + jnp.arange(tokens, dtype=jnp.int32)
    after = (index[:, None] >= ends[None, :]).astype(jnp.int32)
    start = jnp.sum(after * lengths[0][None, :], 1)
    half = HEAD // 2
    freq = jnp.exp(jnp.arange(half, dtype=F32) * (-2.0 * math.log(ROPE_BASE) / HEAD))
    angle = (index - start).astype(F32)[:, None] * freq[None, :]
    cosine = jnp.cos(angle)
    sine = jnp.sin(angle)
    cosine = jnp.concatenate([cosine, cosine], 1)
    sine = jnp.concatenate([-sine, sine], 1)
    start_column = jnp.broadcast_to(start[:, None], (tokens, LANES))
    start_row = jnp.broadcast_to(start[None, :], (8, tokens))
    order = jnp.concatenate([me[None], (start[0] // tokens)[None], ring.sources()])
    places = jnp.stack([own, me])

    q, kv, low_one, gains = qkv_call(x, w_full, cosine, sine)
    kv_slots = [part for couple in ring.gather(kv) for part in couple]
    attended, log_total = attn_call(order, q, start_column, kv_slots)
    attn_rows, low_two = out_call(x, attended, wo_t, gains)

    routed = [route_call(places, couple, shards, capacity, width) for couple in grads]
    parts, made = [], []
    for couple, (pick0, pick1, _, _, grad_hidden) in zip(ring.gather(low_two), routed):
        found = expert_call(places, couple, (pick0, pick1), grad_hidden, shards, capacity)
        made.append(found[:4])
        parts.append((found[4], found[5]))
    grad_parts = ring.scatter(parts)

    resid, grad_attn, grad_out, delta, moe_part = resid_back_call(
        x, attn_rows, dy, gains, wo_t, attended, grad_parts
    )
    back = attn_back_call(
        order, q, grad_out, start_row, log_total, delta, cosine, sine, kv_slots
    )
    d_q, kv_parts = back[0], back[1:]
    kv_terms = ring.scatter(
        [(kv_parts[2 * step], kv_parts[2 * step + 1]) for step in range(count // 2)]
    )

    y_parts = []
    for (pick0, pick1, gate_rows, _, _), (_, hid, _, _) in zip(routed, made):
        y_parts.append(
            down_call(places, hid, gate_rows, (pick0, pick1), shards, capacity, width)
        )
    flat = hold([part for couple in y_parts for part in couple], resid)
    y_terms = ring.scatter(
        [(flat[2 * step], flat[2 * step + 1]) for step in range(count // 2)]
    )
    moe = y_terms[0].astype(F32)
    for term in y_terms[1:]:
        moe = moe + term.astype(F32)
    output = (x.astype(F32) + attn_rows.astype(F32) + moe).astype(BF)

    grad_shards = weight_grad_call(
        places,
        [entry[0] for entry in made],
        [entry[3] for entry in routed],
        [entry[2] for entry in made],
        [entry[3] for entry in made],
        [entry[1] for entry in made],
        shards_of,
    )
    near, arrived = scatter_shards(grad_shards, shards_of)
    expert_grads = near.astype(F32) + arrived.astype(F32)

    wo_grad = lax.psum_scatter(
        cross_call(grad_attn, attended, "wo_grad"), both, scatter_dimension=0, tiled=True
    ).astype(F32)
    wq_grad = lax.psum_scatter(
        cross_call(low_one, d_q, "wq_grad"), both, scatter_dimension=0, tiled=True
    ).astype(F32)
    grad_q = input_q_call(d_q, w_full)
    input_grad, tail = final_call(
        x, low_one, resid, grad_q, gains, moe_part, w_full, cosine, sine, kv_terms
    )
    tail = lax.psum_scatter(tail, both, scatter_dimension=0, tiled=True).astype(F32)
    return (
        output[None],
        input_grad[None],
        tail[:, 2 * KVW],
        wq_grad,
        tail[:, 0:KVW],
        tail[:, KVW : 2 * KVW],
        wo_grad.T,
        tail[:, 2 * KVW + 1],
        expert_grads[0],
        expert_grads[1],
        jnp.swapaxes(expert_grads[2], 1, 2),
    )


def solution(mesh):
    return jax.shard_map(
        local,
        mesh=mesh,
        in_specs=(
            P("fsdp", "ctx", None),
            P("fsdp", None),
            P("fsdp", "ctx", None),
            P("fsdp", "ctx", None),
            P(("ctx", "fsdp")),
            P(("ctx", "fsdp"), None),
            P(("ctx", "fsdp"), None),
            P(("ctx", "fsdp"), None),
            P(None, ("ctx", "fsdp")),
            P(("ctx", "fsdp")),
            P("ctx", "fsdp", None),
            P("ctx", "fsdp", None),
            P("ctx", None, "fsdp"),
            P("fsdp", "ctx", None),
        ),
        out_specs=(
            P("fsdp", "ctx", None),
            P("fsdp", "ctx", None),
            P(("ctx", "fsdp")),
            P(("ctx", "fsdp"), None),
            P(("ctx", "fsdp"), None),
            P(("ctx", "fsdp"), None),
            P(None, ("ctx", "fsdp")),
            P(("ctx", "fsdp")),
            P("ctx", "fsdp", None),
            P("ctx", "fsdp", None),
            P("ctx", None, "fsdp"),
        ),
        check_vma=False,
    )
```

```python
import math

import jax
import jax.numpy as jnp
from jax import lax
from jax.experimental import pallas as pl
from jax.experimental.pallas import tpu as pltpu
from jax.sharding import PartitionSpec as P

HEADS = 12
KV_HEADS = 2
HEAD = 128
TOPK = 4
REPEAT = HEADS // KV_HEADS
HQ = HEADS * HEAD
KVW = KV_HEADS * HEAD
LANES = 128

EPS = 1e-06
ROPE_BASE = 10000.0
NEG = -1e30
BF = jnp.bfloat16
F32 = jnp.float32
NN = ((1,), (0,))
NT = ((1,), (1,))
TN = ((0,), (0,))
ANY = pl.BlockSpec(memory_space=pl.ANY)
MIB = 1024 * 1024
SCALE = 0.4


def mm(left, right, dims=NN):
    return lax.dot_general(left, right, (dims, ((), ())), preferred_element_type=F32)


def params(grid_rank, limit=56):
    return pltpu.CompilerParams(
        dimension_semantics=("arbitrary",) * grid_rank, vmem_limit_bytes=limit * MIB
    )


def busy(microseconds):
    return pl.CostEstimate(
        flops=int(microseconds * SCALE * 1.15e9), bytes_accessed=1024, transcendentals=0
    )


def sds(shape, dtype):
    return jax.ShapeDtypeStruct(shape, dtype)


def whole(shape):
    return pl.BlockSpec(shape, lambda *_: (0,) * len(shape))


def without(kernel, place, extra):
    def run(*refs):
        kernel(*refs[:place], *refs[place + extra :])

    return run


class Ring:
    def __init__(self, count):
        self.count = count
        self.low_pair = count == 8
        self.length = count // 2
        self.me = lax.axis_index("ctx")
        if self.low_pair:
            self.line, self.pair = self.me // 2, self.me % 2
        else:
            self.line, self.pair = self.me % self.length, self.me // self.length
        if self.length == 4:
            self.table = [[0, 1, 2, 3], [1, 0, 2, 3], [2, 3, 1, 0], [3, 2, 1, 0]]
        else:
            self.table = [
                [(place + step) % self.length for step in range(self.length)]
                for place in range(self.length)
            ]

    def index(self, line, pair):
        return line * 2 + pair if self.low_pair else pair * self.length + line

    def move(self, array, hops):
        pairs = [
            (self.index(source, side), self.index(target, side))
            for source, target in hops
            for side in (0, 1)
        ]
        return lax.ppermute(array, "ctx", pairs)

    def swap(self, array):
        pairs = [
            (self.index(place, side), self.index(place, 1 - side))
            for place in range(self.length)
            for side in (0, 1)
        ]
        return lax.ppermute(array, "ctx", pairs)

    def sources(self):
        line = jnp.asarray(self.table, jnp.int32)[self.line]
        side = jnp.stack([self.pair, 1 - self.pair]).astype(jnp.int32)
        return self.index(line[:, None], side[None, :]).reshape(-1).astype(jnp.int32)

    def spread(self, array):
        everything = lax.all_gather(array, "ctx", axis=0)
        order = self.sources()
        rows = [
            lax.dynamic_index_in_dim(everything, order[slot], 0, keepdims=False)
            for slot in range(self.count)
        ]
        return [(rows[2 * step], rows[2 * step + 1]) for step in range(self.length)]

    def gather(self, array, late=()):
        if self.length != 4:
            yield
            for couple in self.spread(array):
                yield couple
            return
        ends = [(1, 0), (2, 3)]
        middle = [(1, 2), (2, 1)]
        couples = [(0, 1), (1, 0), (2, 3), (3, 2)]
        first = self.move(array, couples)
        cross = self.move(array, middle)
        swapped = self.swap(array)
        until = yield
        first, cross = hold([first, cross], until, swapped)
        swapped = hold([swapped], cross)[0]
        outward = self.move(cross, ends)
        cross_two = self.move(first, middle)
        swapped_first = self.swap(first)
        until = yield (array, swapped)
        outward, cross_two = hold([outward, cross_two], until, swapped_first)
        second = cross + outward
        if late:
            cross_two, second = hold([cross_two, second], late[0])
        outward_two = self.move(cross_two, ends)
        swapped_second = self.swap(second)
        until = yield (first, swapped_first)
        outward_two = hold([outward_two], until, swapped_second)[0]
        third = cross_two + outward_two
        swapped_third = self.swap(third)
        yield (second, swapped_second)
        yield (third, swapped_third)

    def gather_now(self, array):
        run = self.gather(array)
        next(run)
        return [run.send(None) for _ in range(self.length)]

    def scatter(self, parts):
        if self.length != 4:
            order = self.sources()
            rows = jnp.stack([part for couple in parts for part in couple])
            placed = jnp.zeros_like(rows).at[order].set(rows)
            total = lax.psum_scatter(placed, "ctx", scatter_dimension=0, tiled=False)
            for _ in range(4):
                yield total
            yield [total]
            return
        inward = [(0, 1), (3, 2)]
        middle = [(1, 2), (2, 1)]
        couples = [(0, 1), (1, 0), (2, 3), (3, 2)]
        swapped = [self.swap(part[1]) for part in parts]
        until = yield parts[3][1]
        third = parts[3][0] + hold([swapped[3]], until)[0]
        from_end = self.move(third, inward)
        until = yield third
        from_end, arrived = hold([from_end, swapped[2]], until)
        sent = third + from_end
        crossed = self.move(sent, middle)
        second = parts[2][0] + arrived
        from_end_two = self.move(second, inward)
        until = yield second
        crossed, from_end_two, arrived = hold([crossed, from_end_two, swapped[1]], until)
        sent = parts[1][0] + arrived + crossed
        last = self.move(sent, couples)
        crossed_two = self.move(second + from_end_two, middle)
        until = yield sent
        last, crossed_two, arrived = hold([last, crossed_two, swapped[0]], until)
        yield [parts[0][0], arrived, crossed_two, last]

    def scatter_pairs(self, parts, pairs):
        if self.length != 4:
            flat = [pair[place] for pair in pairs for place in range(self.length // 2)]
            yield from self.scatter(list(zip(parts, reversed(flat))))
            return
        inward = [(0, 1), (3, 2)]
        middle = [(1, 2), (2, 1)]
        couples = [(0, 1), (1, 0), (2, 3), (3, 2)]
        swapped = [self.swap(pair) for pair in pairs]
        until = yield pairs[0]
        arrived = hold([swapped[0]], until)[0]
        third = parts[3] + arrived[0]
        second = parts[2] + arrived[1]
        from_end = self.move(third, inward)
        from_end_two = self.move(second, inward)
        until = yield second
        from_end, from_end_two, arrived = hold([from_end, from_end_two, swapped[1]], until)
        crossed = self.move(third + from_end, middle)
        sent = second + from_end_two
        crossed_two = self.move(sent, middle)
        until = yield sent
        crossed = hold([crossed], until)[0]
        sent = parts[1] + arrived[0] + crossed
        last = self.move(sent, couples)
        until = yield sent
        last, crossed_two = hold([last, crossed_two], until)
        yield [parts[0], arrived[1], crossed_two, last]

    def scatter_now(self, parts):
        run = self.scatter(parts)
        next(run)
        made = [run.send(None) for _ in range(4)]
        return made[-1]


def neighbour(array, axis_size, bit):
    pairs = [(index, index ^ (1 << bit)) for index in range(axis_size)]
    return lax.ppermute(array, "fsdp", pairs)


def gather_shards(array, axis_size, until=None):
    slots = {0: array}
    bits = axis_size.bit_length() - 1
    for bit in reversed(range(bits)):
        for slot in list(slots):
            taken = slots[slot]
            if slot and bit == 0 and until is not None:
                taken = slots[slot] = hold([taken], until)[0]
            slots[slot | (1 << bit)] = neighbour(taken, axis_size, bit)
    return [slots[slot] for slot in range(axis_size)]


def scatter_all_across(near, far, axis_size):
    arrived = neighbour(far, axis_size, 0)
    sent = near[1] + arrived[1]
    return near[0] + arrived[0] + neighbour(sent, axis_size, 1), sent


def scatter_all_along(terms, ring):
    swapped = ring.swap(terms[1])
    swapped = hold([swapped], (yield))[0]
    lines = terms[0] + swapped
    ends = ring.move(lines[2:4], [(0, 1), (3, 2)])
    ends = hold([ends], (yield))[0]
    middle = ring.move(lines[2:4] + ends, [(1, 2), (2, 1)])
    middle = hold([middle], (yield))[0]
    last = ring.move(lines[1] + middle[1], [(0, 1), (1, 0), (2, 3), (3, 2)])
    last = hold([last], (yield))[0]
    yield lines[0].astype(F32) + middle[0].astype(F32) + last.astype(F32)


def turn(values, cosine, sine):
    return values * cosine + pltpu.roll(values, HEAD // 2, 1) * sine


def qkv_kernel(x_ref, w_ref, g_ref, cos_ref, sin_ref, q_ref, kv_ref, low_ref, gain_ref):
    step = pl.program_id(0)
    blocks = HQ // 512

    @pl.when(step == 0)
    def _():
        gains = jnp.transpose(g_ref[...].astype(F32))
        gain_ref[...] = gains[0:8]
        wide = x_ref[...].astype(F32)
        scale = lax.rsqrt(jnp.mean(wide * wide, -1, keepdims=True) + EPS)
        low_ref[...] = (wide * scale * gains[0:1]).astype(BF)

    raw = mm(low_ref[...], w_ref[...])
    cosine, sine = cos_ref[...], sin_ref[...]

    def turned(count):
        return [
            turn(raw[:, head * HEAD : (head + 1) * HEAD], cosine, sine).astype(BF)
            for head in range(count)
        ]

    @pl.when(step < blocks)
    def _():
        for head, value in enumerate(turned(4)):
            q_ref[:, head * HEAD : (head + 1) * HEAD] = value

    @pl.when(step == blocks)
    def _():
        for head, value in enumerate(turned(KV_HEADS)):
            kv_ref[:, head * HEAD : (head + 1) * HEAD] = value
        kv_ref[:, KVW:] = raw[:, KVW:].astype(BF)


def qkv_call(x, w_full, cosine, sine, after=()):
    tokens, width = x.shape
    blocks = HQ // 512
    return pl.pallas_call(
        without(qkv_kernel, 5, len(after)),
        name="qkv",
        grid=(blocks + 1,),
        in_specs=[
            whole((tokens, width)),
            pl.BlockSpec((width, 512), lambda i: (0, i)),
            pl.BlockSpec((width, LANES), lambda i: (0, (2 * HQ + 2 * KVW) // LANES)),
            whole((tokens, HEAD)),
            whole((tokens, HEAD)),
        ]
        + [ANY] * len(after),
        out_specs=[
            pl.BlockSpec((tokens, 512), lambda i: (0, jnp.minimum(i, HQ // 512 - 1))),
            whole((tokens, 2 * KVW)),
            whole((tokens, width)),
            whole((8, width)),
        ],
        out_shape=[
            sds((tokens, HQ), BF),
            sds((tokens, 2 * KVW), BF),
            sds((tokens, width), BF),
            sds((8, width), F32),
        ],
        compiler_params=params(1),
        cost_estimate=busy(9),
    )(x, w_full, w_full, cosine, sine, *after)


HEADER = 5
SEQS = 3
COUPLE = 2
COUPLES = HEADS // COUPLE
LOG2E = math.log2(math.e)


def load_kv(slots, kv_all, sems):
    copies = [
        pltpu.make_async_copy(slot, kv_all.at[place], sems.at[place])
        for place, slot in enumerate(slots)
    ]
    for copy in copies:
        copy.start()
    for copy in copies:
        copy.wait()


def sequence_of(order_ref, index):
    ends = [order_ref[2 + place] for place in range(SEQS - 1)]
    return sum((index >= end).astype(jnp.int32) for end in ends)


def extend_queries(order_ref, q_ref, wide):
    tokens = q_ref.shape[0]
    rows = order_ref[0] * tokens + lax.broadcasted_iota(jnp.int32, (tokens, LANES), 0)
    lanes = lax.broadcasted_iota(jnp.int32, (tokens, LANES), 1)
    other = (lanes < SEQS) & (lanes != sequence_of(order_ref, rows))
    extra = jnp.where(other | (lanes > SEQS + order_ref[0]), NEG, 0.0).astype(BF)
    for place in range(COUPLE):
        span = slice(place * tokens, (place + 1) * tokens)
        wide[span, 0:HEAD] = q_ref[:, place * HEAD : (place + 1) * HEAD]
        wide[span, HEAD:] = extra


def extend_keys(order_ref, base, kv_all, groups, wide, turned, which):
    count, tokens, columns = kv_all.shape
    lanes = lax.broadcasted_iota(jnp.int32, (tokens, LANES), 1)
    sublanes = lax.broadcasted_iota(jnp.int32, (tokens, LANES), 0)
    for slot in range(count):
        block = order_ref[HEADER + base + slot]
        mine = lanes == sequence_of(order_ref, block * tokens + sublanes)
        unit = jnp.where(mine | (lanes == SEQS + block), 1.0, 0.0).astype(BF)
        for group in range(groups):
            span = slice(group * HEAD, (group + 1) * HEAD)
            wide[group, slot, :, 0:HEAD] = kv_all[slot, :, span]
            wide[group, slot, :, HEAD:] = unit
            start = which * groups * HEAD + group * HEAD
            taken = kv_all[slot, :, start : start + HEAD].astype(F32)
            turned[
                group * HEAD : (group + 1) * HEAD, slot * tokens : (slot + 1) * tokens
            ] = jnp.transpose(taken).astype(BF)


def causal(scores):
    tokens = scores.shape[0]
    keys = lax.broadcasted_iota(jnp.int32, (tokens, tokens), 0)
    queries = lax.broadcasted_iota(jnp.int32, (tokens, tokens), 1)
    kept = jnp.concatenate([keys <= queries] * COUPLE, 1)
    return jnp.where(kept, scores, NEG)


def attn_kernel(count, base, last, order_ref, q_ref, *rest):
    slots, rest = rest[:count], rest[count:]
    if base:
        acc_in, stat_in, *rest = rest
    if last:
        out_ref, total_ref, *rest = rest
    else:
        acc_out, stat_out, *rest = rest
    kv_all, keys, values, queries, spread, acc, stat, sems = rest
    step = pl.program_id(0)
    tokens = q_ref.shape[0]
    factor = HEAD ** (-0.5) * LOG2E

    @pl.when(step == 0)
    def _():
        load_kv(slots, kv_all, sems)
        extend_keys(order_ref, base, kv_all, KV_HEADS, keys, values, 1)

    group = step * COUPLE // REPEAT
    extend_queries(order_ref, q_ref, queries)
    if base:
        acc[...] = acc_in[0]
        stat[...] = stat_in[0]
    else:
        acc[...] = jnp.zeros_like(acc)
        stat[...] = jnp.zeros_like(stat)
        stat[0:1] = jnp.full((1, COUPLE * tokens), NEG, F32)

    scores = []
    new_peak = stat[0:1]
    for slot in range(count):
        made = mm(keys[group, slot], queries[...], NT)
        if base + slot == 0:
            made = causal(made)
        new_peak = jnp.maximum(new_peak, jnp.max(made, 0, keepdims=True))
        scores.append(made)
    keep = jnp.exp2((stat[0:1] - new_peak) * factor)
    total = stat[1:2] * keep
    added = acc[...] * keep
    for slot in range(count):
        weights = jnp.exp2((scores[slot] - new_peak) * factor)
        total += jnp.sum(weights, 0, keepdims=True)
        spread[slot * tokens : (slot + 1) * tokens] = weights.astype(BF)
    own = pl.ds(pl.multiple_of(group * HEAD, HEAD), HEAD)
    added += mm(values[own, :], spread[...])
    stat[0:1] = new_peak
    stat[1:2] = total
    acc[...] = added

    if last:
        made = acc[...] / stat[1:2]
        log_total = stat[0:1] * factor + jnp.log(stat[1:2]) * LOG2E
        for place in range(COUPLE):
            span = slice(place * tokens, (place + 1) * tokens)
            out_ref[:, place * HEAD : (place + 1) * HEAD] = jnp.transpose(made[:, span]).astype(BF)
            total_ref[0, place : place + 1] = log_total[:, span]
    else:
        acc_out[0] = acc[...]
        stat_out[0] = stat[...]


def attn_call(order, q, slots, base, last, state=(), after=()):
    tokens = q.shape[0]
    count = len(slots)
    wide = COUPLE * tokens
    column = lambda h, _: (0, h)
    by_step = lambda h, _: (h, 0, 0)
    if last:
        out_specs = [
            pl.BlockSpec((tokens, COUPLE * HEAD), column),
            pl.BlockSpec((1, 8, tokens), by_step),
        ]
        out_shape = [sds((tokens, HQ), BF), sds((COUPLES, 8, tokens), F32)]
    else:
        out_specs = [
            pl.BlockSpec((1, HEAD, wide), by_step),
            pl.BlockSpec((1, 8, wide), by_step),
        ]
        out_shape = [sds((COUPLES, HEAD, wide), F32), sds((COUPLES, 8, wide), F32)]
    state_specs = [
        pl.BlockSpec((1, HEAD, wide), by_step),
        pl.BlockSpec((1, 8, wide), by_step),
    ]
    grid = pltpu.PrefetchScalarGridSpec(
        num_scalar_prefetch=1,
        grid=(COUPLES,),
        in_specs=[pl.BlockSpec((tokens, COUPLE * HEAD), column)]
        + [ANY] * count
        + (state_specs if base else [])
        + [ANY] * len(after),
        out_specs=out_specs,
        scratch_shapes=[
            pltpu.VMEM((count, tokens, 2 * KVW), BF),
            pltpu.VMEM((KV_HEADS, count, tokens, 2 * HEAD), BF),
            pltpu.VMEM((KV_HEADS * HEAD, count * tokens), BF),
            pltpu.VMEM((wide, 2 * HEAD), BF),
            pltpu.VMEM((count * tokens, wide), BF),
            pltpu.VMEM((HEAD, wide), F32),
            pltpu.VMEM((8, wide), F32),
            pltpu.SemaphoreType.DMA((count,)),
        ],
    )
    return pl.pallas_call(
        without(
            lambda *refs: attn_kernel(count, base, last, *refs),
            2 + count + len(state),
            len(after),
        ),
        name="attention",
        grid_spec=grid,
        out_shape=out_shape,
        compiler_params=params(1),
        cost_estimate=busy(18),
    )(order, q, *slots, *state, *after)


def attn_back_kernel(count, group, order_ref, q_ref, do_ref, total_ref, delta_ref, *rest):
    cos_ref, sin_ref = rest[:2]
    slots, rest = rest[2 : 2 + count], rest[2 + count :]
    if group:
        rest = rest[count:]
    dq_ref, rest = rest[0], rest[1:]
    outs, rest = rest[:count], rest[count:]
    kv_all, keys, turned, queries, grads, spread, d_k, d_v, packed, sems = rest
    step = pl.program_id(0)
    tokens = q_ref.shape[0]
    scale = HEAD ** (-0.5)

    @pl.when(step == 0)
    def _():
        for part in range(2):
            columns = slice(part * KVW + group * HEAD, part * KVW + (group + 1) * HEAD)
            load_kv(
                [slot.at[:, columns] for slot in slots],
                kv_all.at[:, :, part * HEAD : (part + 1) * HEAD],
                sems,
            )
        extend_keys(order_ref, 0, kv_all, 1, keys, turned, 0)
        d_k[...] = jnp.zeros_like(d_k)
        d_v[...] = jnp.zeros_like(d_v)

    extend_queries(order_ref, q_ref, queries)
    for place in range(COUPLE):
        span = slice(place * tokens, (place + 1) * tokens)
        grads[span] = do_ref[:, place * HEAD : (place + 1) * HEAD]

    log_total = jnp.concatenate([total_ref[0, place : place + 1] for place in range(COUPLE)], 1)
    delta = jnp.concatenate([delta_ref[0, place : place + 1] for place in range(COUPLE)], 1)

    for slot in range(count):
        scores = mm(keys[0, slot], queries[...], NT)
        if slot == 0:
            scores = causal(scores)
        probs = jnp.exp2(scores * (scale * LOG2E) - log_total)
        grad_probs = mm(kv_all[slot, :, HEAD:], grads[...], NT)
        grad_scores = (probs * (grad_probs - delta)).astype(BF)
        spread[slot * tokens : (slot + 1) * tokens] = grad_scores
        d_v[slot] += mm(probs.astype(BF), grads[...])
        d_k[slot] += mm(grad_scores, queries[:, 0:HEAD])
    d_q = mm(turned[...], spread[...])
    for place in range(COUPLE):
        span = slice(place * tokens, (place + 1) * tokens)
        piece = jnp.transpose(d_q[:, span]) * scale
        dq_ref[:, place * HEAD : (place + 1) * HEAD] = turn(
            piece, cos_ref[...], -sin_ref[...]
        ).astype(BF)

    @pl.when(step == pl.num_programs(0) - 1)
    def _():
        copies = []
        for place in range(count):
            packed[place, :, 0:HEAD] = d_k[place].astype(BF)
            packed[place, :, HEAD:] = d_v[place].astype(BF)
            columns = pl.ds(group * 2 * HEAD, 2 * HEAD)
            copies.append(
                pltpu.make_async_copy(
                    packed.at[place], outs[place].at[:, columns], sems.at[place]
                )
            )
            copies[-1].start()
        for copy in copies:
            copy.wait()


def attn_back_call(
    group, order, q, grad, log_total, delta, cosine, sine, slots, held=(), after=()
):
    tokens = q.shape[0]
    count = len(slots)
    steps = REPEAT // COUPLE
    column = lambda h, _: (0, group * steps + h)
    by_step = lambda h, _: (group * steps + h, 0, 0)
    fixed = lambda h, _: (0, 0)
    grid = pltpu.PrefetchScalarGridSpec(
        num_scalar_prefetch=1,
        grid=(steps,),
        in_specs=[
            pl.BlockSpec((tokens, COUPLE * HEAD), column),
            pl.BlockSpec((tokens, COUPLE * HEAD), column),
            pl.BlockSpec((1, 8, tokens), by_step),
            pl.BlockSpec((1, 8, tokens), by_step),
            pl.BlockSpec((tokens, HEAD), fixed),
            pl.BlockSpec((tokens, HEAD), fixed),
        ]
        + [ANY] * (count + len(held) + len(after)),
        out_specs=[pl.BlockSpec((tokens, COUPLE * HEAD), lambda h, _: (0, h))] + [ANY] * count,
        scratch_shapes=[
            pltpu.VMEM((count, tokens, 2 * HEAD), BF),
            pltpu.VMEM((1, count, tokens, 2 * HEAD), BF),
            pltpu.VMEM((HEAD, count * tokens), BF),
            pltpu.VMEM((COUPLE * tokens, 2 * HEAD), BF),
            pltpu.VMEM((COUPLE * tokens, HEAD), BF),
            pltpu.VMEM((count * tokens, COUPLE * tokens), BF),
            pltpu.VMEM((count, tokens, HEAD), F32),
            pltpu.VMEM((count, tokens, HEAD), F32),
            pltpu.VMEM((count, tokens, 2 * HEAD), BF),
            pltpu.SemaphoreType.DMA((count,)),
        ],
    )
    return pl.pallas_call(
        without(
            lambda *refs: attn_back_kernel(count, group, *refs),
            7 + count + len(held),
            len(after),
        ),
        name="attention_back",
        input_output_aliases={7 + count + place: 1 + place for place in range(len(held))},
        grid_spec=grid,
        out_shape=[sds((tokens, HQ // KV_HEADS), BF)] + [sds((tokens, 2 * KVW), BF)] * count,
        compiler_params=params(1),
        cost_estimate=busy(26),
    )(order, q, grad, log_total, delta, cosine, sine, *slots, *held, *after)


def out_kernel(x_ref, a_ref, *rest):
    w_refs, (gain_ref, rows_ref, low_ref) = rest[:-3], rest[-3:]
    made = mm(a_ref[:, 0:512], w_refs[0][...], NT)
    for place, w_ref in enumerate(w_refs[1:], 1):
        made += mm(a_ref[:, place * 512 : (place + 1) * 512], w_ref[...], NT)
    rows = made.astype(BF)
    rows_ref[...] = rows
    resid = x_ref[...].astype(F32) + rows.astype(F32)
    scale = lax.rsqrt(jnp.mean(resid * resid, -1, keepdims=True) + EPS)
    low_ref[...] = (resid * scale * gain_ref[1:2]).astype(BF)


def wo_specs(width):
    start = (HQ + 2 * KVW) // 512
    return [
        pl.BlockSpec((width, 512), lambda i, place=place: (0, start + place))
        for place in range(HQ // 512)
    ]


def out_call(x, attended, wo_t, gains, after=()):
    tokens, width = x.shape
    tile = 128
    return pl.pallas_call(
        without(out_kernel, 3 + HQ // 512, len(after)),
        name="attention_out",
        grid=(tokens // tile,),
        in_specs=[
            pl.BlockSpec((tile, width), lambda i: (i, 0)),
            pl.BlockSpec((tile, HQ), lambda i: (i, 0)),
            *wo_specs(width),
            whole((8, width)),
        ]
        + [ANY] * len(after),
        out_specs=[pl.BlockSpec((tile, width), lambda i: (i, 0))] * 2,
        out_shape=[sds((tokens, width), BF)] * 2,
        compiler_params=params(1),
        cost_estimate=busy(9),
    )(x, attended, *[wo_t] * (HQ // 512), gains, *after)


def weight_copies(shards, own, kinds, held, sems):
    size = shards[0].shape[2]
    groups = []
    for expert in range(shards[0].shape[1]):
        copies = []
        for slot, shard in enumerate(shards):
            rows = pl.ds(pl.multiple_of((own ^ slot) * size, 16), size)
            for place, kind in enumerate(kinds):
                copies.append(
                    pltpu.make_async_copy(
                        shard.at[kind, expert],
                        held.at[place, expert, rows],
                        sems.at[place, expert, slot],
                    )
                )
        groups.append(copies)
    return groups


def fetch_weights(shards, own, kinds, held, sems):
    groups = weight_copies(shards, own, kinds, held, sems)
    step = pl.program_id(0)

    @pl.when(step == 0)
    def _():
        for copies in groups:
            for copy in copies:
                copy.start()

    for expert, copies in enumerate(groups):

        @pl.when(step == expert)
        def _():
            for copy in copies:
                copy.wait()


def route_kernel(shards_of, capacity, order_ref, d0_ref, d1_ref, *rest):
    shards = rest[:shards_of]
    p0_ref, p1_ref, gate_ref, rows_ref, hid_ref, held, sems = rest[shards_of:]
    expert = pl.program_id(0)
    tokens = d0_ref.shape[0]
    width = rows_ref.shape[2]
    fetch_weights(shards, order_ref[0], (2,), held, sems)
    wanted = (order_ref[1] * held.shape[1] + expert).astype(F32)
    before = lax.broadcasted_iota(jnp.int32, (tokens, tokens), 0) < lax.broadcasted_iota(
        jnp.int32, (tokens, tokens), 1
    )
    before = jnp.where(before, 1.0, 0.0).astype(BF)
    places = lax.broadcasted_iota(jnp.int32, (capacity, tokens), 0).astype(F32)
    for side, (ref, p_ref) in enumerate(((d0_ref, p0_ref), (d1_ref, p1_ref))):
        info = jnp.transpose(ref[:, width:].astype(F32))
        chosen = jnp.where(info[0:TOPK] == wanted, 1.0, 0.0)
        gate = jnp.sum(
            chosen * (info[TOPK : 2 * TOPK] + info[2 * TOPK : 3 * TOPK] + info[3 * TOPK : 4 * TOPK]),
            0,
            keepdims=True,
        )
        named = jnp.sum(chosen, 0, keepdims=True)
        rank = mm(jnp.broadcast_to(named, (8, tokens)).astype(BF), before)[0:1]
        picks = jnp.where((places == rank) & (named > 0.5), 1.0, 0.0)
        weight = jnp.sum(picks * gate, 1, keepdims=True)
        picks = picks.astype(BF)
        p_ref[0] = picks
        span = slice(side * capacity, (side + 1) * capacity)
        gate_ref[0, span] = jnp.broadcast_to(weight, (capacity, LANES))
        rows_ref[0, span] = (mm(picks, ref[:, :width]) * weight).astype(BF)
    hid_ref[0] = mm(rows_ref[0], held[0, expert])


def route_call(order, grads, shards, capacity, width, after=()):
    tokens = grads[0].shape[0]
    _, experts, size, hidden = shards[0].shape
    rows = 2 * capacity
    by_expert = lambda e, _: (e, 0, 0)
    grid = pltpu.PrefetchScalarGridSpec(
        num_scalar_prefetch=1,
        grid=(experts,),
        in_specs=[pl.BlockSpec(grads[0].shape, lambda e, _: (0, 0))] * 2
        + [ANY] * (len(shards) + len(after)),
        out_specs=[pl.BlockSpec((1, capacity, tokens), by_expert)] * 2
        + [
            pl.BlockSpec((1, rows, LANES), by_expert),
            pl.BlockSpec((1, rows, width), by_expert),
            pl.BlockSpec((1, rows, hidden), by_expert),
        ],
        scratch_shapes=[
            pltpu.VMEM((1, experts, width, hidden), BF),
            pltpu.SemaphoreType.DMA((1, experts, len(shards))),
        ],
    )
    return pl.pallas_call(
        without(
            lambda *refs: route_kernel(len(shards), capacity, *refs), 3 + len(shards), len(after)
        ),
        name="route",
        grid_spec=grid,
        out_shape=[sds((experts, capacity, tokens), BF)] * 2
        + [
            sds((experts, rows, LANES), F32),
            sds((experts, rows, width), BF),
            sds((experts, rows, hidden), F32),
        ],
        compiler_params=params(1),
        cost_estimate=busy(8.5),
    )(order, *grads, *shards, *after)


def expert_kernel(shards_of, capacity, order_ref, x0_ref, x1_ref, p0_ref, p1_ref, gh_ref, *rest):
    shards = rest[:shards_of]
    rows_ref, hid_ref, gg_ref, gu_ref, out0_ref, out1_ref, held, slot, acc, sems = rest[shards_of:]
    expert = pl.program_id(0)
    hidden = gh_ref.shape[2]
    width = x0_ref.shape[1]
    fetch_weights(shards, order_ref[0], (0, 1), held, sems)
    for side, (ref, p_ref) in enumerate(((x0_ref, p0_ref), (x1_ref, p1_ref))):
        span = slice(side * capacity, (side + 1) * capacity)
        rows_ref[0, span] = mm(p_ref[0], ref[...]).astype(BF)
    rows = rows_ref[0]
    tile = 256
    for start in range(0, hidden, tile):
        span = slice(start, start + tile)
        gate = mm(rows, held[0, expert, :, span])
        up = mm(rows, held[1, expert, :, span])
        grad = gh_ref[0, :, span]
        sigma = 1.0 / (1.0 + jnp.exp(-gate))
        active = gate * sigma
        hid_ref[0, :, span] = (active * up).astype(BF)
        gg_ref[0, :, span] = (grad * up * (sigma * (1.0 + gate * (1.0 - sigma)))).astype(BF)
        gu_ref[0, :, span] = (grad * active).astype(BF)
    tile = 512
    for start in range(0, width, tile):
        span = slice(start, start + tile)
        slot[:, span] = (
            mm(gg_ref[0], held[0, expert, span, :], NT)
            + mm(gu_ref[0], held[1, expert, span, :], NT)
        ).astype(BF)
    for side, (p_ref, out_ref) in enumerate(((p0_ref, out0_ref), (p1_ref, out1_ref))):
        span = slice(side * capacity, (side + 1) * capacity)
        term = mm(p_ref[0], slot[span], TN)

        @pl.when(expert == 0)
        def _():
            acc[side] = term

        @pl.when(expert > 0)
        def _():
            acc[side] += term

        @pl.when(expert == pl.num_programs(0) - 1)
        def _():
            out_ref[...] = acc[side].astype(BF)


def expert_call(order, xs, picks, grad_hidden, shards, capacity, after=()):
    tokens, width = xs[0].shape
    _, experts, size, hidden = shards[0].shape
    rows = 2 * capacity
    by_expert = lambda e, _: (e, 0, 0)
    fixed = lambda e, _: (0, 0)
    grid = pltpu.PrefetchScalarGridSpec(
        num_scalar_prefetch=1,
        grid=(experts,),
        in_specs=[pl.BlockSpec((tokens, width), fixed)] * 2
        + [pl.BlockSpec((1, capacity, tokens), by_expert)] * 2
        + [pl.BlockSpec((1, rows, hidden), by_expert)]
        + [ANY] * (len(shards) + len(after)),
        out_specs=[pl.BlockSpec((1, rows, width), by_expert)]
        + [pl.BlockSpec((1, rows, hidden), by_expert)] * 3
        + [pl.BlockSpec((tokens, width), fixed)] * 2,
        scratch_shapes=[
            pltpu.VMEM((2, experts, width, hidden), BF),
            pltpu.VMEM((rows, width), BF),
            pltpu.VMEM((2, tokens, width), F32),
            pltpu.SemaphoreType.DMA((2, experts, len(shards))),
        ],
    )
    return pl.pallas_call(
        without(
            lambda *refs: expert_kernel(len(shards), capacity, *refs), 6 + len(shards), len(after)
        ),
        name="experts",
        grid_spec=grid,
        out_shape=[sds((experts, rows, width), BF)]
        + [sds((experts, rows, hidden), BF)] * 3
        + [sds((tokens, width), BF)] * 2,
        compiler_params=params(1),
        cost_estimate=busy(17),
    )(order, *xs, *picks, grad_hidden, *shards, *after)


def down_kernel(shards_of, capacity, place, order_ref, hid_ref, gate_ref, p0_ref, p1_ref, *rest):
    shards = rest[:shards_of]
    out_ref, pair_ref, held, slot, acc, packed, sems, out_sem = rest[-8:]
    expert = pl.program_id(0)
    width = out_ref.shape[1]
    fetch_weights(shards, order_ref[0], (2,), held, sems)
    tile = 512
    for start in range(0, width, tile):
        span = slice(start, start + tile)
        made = mm(hid_ref[0], held[0, expert, span, :], NT).astype(BF).astype(F32)
        slot[:, span] = (made * gate_ref[0, :, 0:1]).astype(BF)
    for side, p_ref in enumerate((p0_ref, p1_ref)):
        span = slice(side * capacity, (side + 1) * capacity)
        term = mm(p_ref[0], slot[span], TN)

        @pl.when(expert == 0)
        def _():
            acc[side] = term

        @pl.when(expert > 0)
        def _():
            acc[side] += term

    @pl.when(expert == pl.num_programs(0) - 1)
    def _():
        packed[...] = acc[1].astype(BF)
        copy = pltpu.make_async_copy(packed, pair_ref.at[place], out_sem)
        copy.start()
        out_ref[...] = acc[0].astype(BF)
        copy.wait()


def down_call(order, hid, gates, picks, shards, capacity, width, place, pair, total, after=()):
    tokens = picks[0].shape[2]
    _, experts, size, hidden = shards[0].shape
    rows = 2 * capacity
    by_expert = lambda e, _: (e, 0, 0)
    pair = [] if pair is None else [pair]
    grid = pltpu.PrefetchScalarGridSpec(
        num_scalar_prefetch=1,
        grid=(experts,),
        in_specs=[
            pl.BlockSpec((1, rows, hidden), by_expert),
            pl.BlockSpec((1, rows, LANES), by_expert),
        ]
        + [pl.BlockSpec((1, capacity, tokens), by_expert)] * 2
        + [ANY] * (len(shards) + len(pair) + len(after)),
        out_specs=[whole((tokens, width)), ANY],
        scratch_shapes=[
            pltpu.VMEM((1, experts, width, hidden), BF),
            pltpu.VMEM((rows, width), BF),
            pltpu.VMEM((2, tokens, width), F32),
            pltpu.VMEM((tokens, width), BF),
            pltpu.SemaphoreType.DMA((1, experts, len(shards))),
            pltpu.SemaphoreType.DMA,
        ],
    )
    return pl.pallas_call(
        lambda *refs: down_kernel(len(shards), capacity, place, *refs),
        name="experts_down",
        grid_spec=grid,
        out_shape=[sds((tokens, width), BF), sds((total, tokens, width), BF)],
        input_output_aliases={5 + len(shards): 1} if pair else {},
        compiler_params=params(1),
        cost_estimate=busy(9.3),
    )(order, hid, gates, *picks, *shards, *pair, *after)


def weight_grad_kernel(chunks, *rest):
    xs, gs = rest[:chunks], rest[chunks : 2 * chunks]
    ggs, gus = rest[2 * chunks : 3 * chunks], rest[3 * chunks : 4 * chunks]
    hids = rest[4 * chunks : 5 * chunks]
    out_ref, left, rights = rest[5 * chunks :]
    rows = xs[0].shape[1]

    @pl.when(pl.program_id(0) == 0)
    def _():
        for kind, group in enumerate((ggs, gus, hids)):
            for place, ref in enumerate(group):
                rights[kind, place * rows : (place + 1) * rows] = ref[0]

    for kind, group in ((0, xs), (2, gs)):
        for place, ref in enumerate(group):
            left[place * rows : (place + 1) * rows] = ref[0]
        out_ref[kind] = mm(left[...], rights[kind], TN).astype(BF)
        if kind == 0:
            out_ref[1] = mm(left[...], rights[1], TN).astype(BF)


def weight_grad_call(expert, xs, gs, ggs, gus, hids, after=()):
    chunks = len(xs)
    _, rows, width = xs[0].shape
    hidden = ggs[0].shape[2]
    tile = 256
    return pl.pallas_call(
        without(lambda *refs: weight_grad_kernel(chunks, *refs), 5 * chunks, len(after)),
        name="expert_weight_grads",
        grid=(width // tile,),
        in_specs=[pl.BlockSpec((1, rows, tile), lambda i: (expert, 0, i))] * (2 * chunks)
        + [pl.BlockSpec((1, rows, hidden), lambda i: (expert, 0, 0))] * (3 * chunks)
        + [ANY] * len(after),
        out_specs=pl.BlockSpec((3, tile, hidden), lambda i: (0, i, 0)),
        out_shape=sds((3, width, hidden), BF),
        scratch_shapes=[
            pltpu.VMEM((chunks * rows, tile), BF),
            pltpu.VMEM((3, chunks * rows, hidden), BF),
        ],
        compiler_params=params(1),
        cost_estimate=busy(18),
    )(*xs, *gs, *ggs, *gus, *hids, *after)


def resid_back_kernel(
    terms, x_ref, rows_ref, dy_ref, gain_ref, att_ref, *rest
):
    w_refs, rest = rest[: HQ // 512], rest[HQ // 512 :]
    parts = rest[:terms]
    resid_ref, attn_ref, do_ref, delta_ref, gain_out, deltas = rest[terms:]
    step = pl.program_id(0)
    grad = parts[0][...].astype(F32)
    for part in parts[1:]:
        grad += part[...].astype(F32)
    resid = x_ref[...].astype(F32) + rows_ref[...].astype(F32)
    scale = lax.rsqrt(jnp.mean(resid * resid, -1, keepdims=True) + EPS)
    normed = resid * scale
    product = grad * normed
    partial = jnp.sum(product, 0, keepdims=True)

    @pl.when(step == 0)
    def _():
        gain_out[...] = jnp.broadcast_to(partial, gain_out.shape)

    @pl.when(step > 0)
    def _():
        gain_out[...] += partial

    gain = gain_ref[1:2]
    mean = jnp.mean(product * gain, -1, keepdims=True)
    total = dy_ref[...].astype(F32) + scale * (grad * gain - normed * mean)
    resid_ref[...] = total
    low = total.astype(BF)
    attn_ref[...] = low
    for place, w_ref in enumerate(w_refs):
        do_ref[:, place * 512 : (place + 1) * 512] = mm(low, w_ref[...]).astype(BF)
    each = do_ref[...].astype(F32) * att_ref[...].astype(F32)
    lanes = lax.broadcasted_iota(jnp.int32, deltas.shape, 1)
    made = jnp.zeros(deltas.shape, F32)
    for head in range(HEADS):
        value = jnp.sum(each[:, head * HEAD : (head + 1) * HEAD], -1, keepdims=True)
        made = jnp.where(lanes == head, value, made)
    deltas[...] = made
    turned = jnp.transpose(deltas[...])
    for head in range(HEADS):
        delta_ref[head // COUPLE, head % COUPLE : head % COUPLE + 1] = turned[head : head + 1]


def resid_back_call(x, rows, dy, gains, wo_t, attended, parts, after=()):
    tokens, width = x.shape
    tile = 128
    by_row = lambda i: (i, 0)
    return pl.pallas_call(
        without(
            lambda *refs: resid_back_kernel(len(parts), *refs),
            5 + HQ // 512 + len(parts),
            len(after),
        ),
        name="resid_back",
        grid=(tokens // tile,),
        in_specs=[pl.BlockSpec((tile, width), by_row)] * 3
        + [whole((8, width)), pl.BlockSpec((tile, HQ), by_row)]
        + wo_specs(width)
        + [pl.BlockSpec((tile, width), by_row)] * len(parts)
        + [ANY] * len(after),
        out_specs=[pl.BlockSpec((tile, width), by_row)] * 2
        + [
            pl.BlockSpec((tile, HQ), by_row),
            pl.BlockSpec((COUPLES, 8, tile), lambda i: (0, 0, i)),
            whole((8, width)),
        ],
        out_shape=[
            sds((tokens, width), F32),
            sds((tokens, width), BF),
            sds((tokens, HQ), BF),
            sds((COUPLES, 8, tokens), F32),
            sds((8, width), F32),
        ],
        scratch_shapes=[pltpu.VMEM((tile, LANES), F32)],
        compiler_params=params(1),
        cost_estimate=busy(10.5),
    )(x, rows, dy, gains, attended, *[wo_t] * (HQ // 512), *parts, *after)


def block_copies(order_ref, source, near, far, sems):
    shards_of, sides, steps, rows, _ = near.shape
    shards_of = 2 * shards_of
    copies = []
    for slot in range(shards_of):
        for place in range(sides * steps):
            block = order_ref[2 + place] * shards_of + (order_ref[0] ^ slot)
            target = far if slot % 2 else near
            copies.append(
                pltpu.make_async_copy(
                    source.at[pl.ds(pl.multiple_of(block * rows, 16), rows)],
                    target.at[slot // 2, place % 2, place // 2],
                    sems.at[slot * sides * steps + place],
                )
            )
    return copies


def cross_kernel(order_ref, left_ref, right_ref, near, far, made, sems):
    step = pl.program_id(0)
    tile = left_ref.shape[1]
    made[pl.ds(pl.multiple_of(step * tile, tile), tile)] = mm(
        left_ref[...], right_ref[...], TN
    ).astype(BF)

    @pl.when(step == pl.num_programs(0) - 1)
    def _():
        copies = block_copies(order_ref, made, near, far, sems)
        for copy in copies:
            copy.start()
        for copy in copies:
            copy.wait()


def blocks_shape(count, shards_of, rows, columns):
    return (shards_of // 2, 2, count // 2, rows // (count * shards_of), columns)


def cross_call(order, left, right, count, shards_of, name):
    tokens, rows = left.shape
    columns = right.shape[1]
    tile = 512
    grid = pltpu.PrefetchScalarGridSpec(
        num_scalar_prefetch=1,
        grid=(rows // tile,),
        in_specs=[
            pl.BlockSpec((tokens, tile), lambda i, _: (0, i)),
            pl.BlockSpec((tokens, columns), lambda i, _: (0, 0)),
        ],
        out_specs=[ANY] * 2,
        scratch_shapes=[
            pltpu.VMEM((rows, columns), BF),
            pltpu.SemaphoreType.DMA((count * shards_of,)),
        ],
    )
    return pl.pallas_call(
        cross_kernel,
        name=name,
        grid_spec=grid,
        out_shape=[sds(blocks_shape(count, shards_of, rows, columns), BF)] * 2,
        compiler_params=params(1),
        cost_estimate=busy(7.5),
    )(order, left, right)


def plain_cross_kernel(left_ref, right_ref, out_ref):
    out_ref[...] = mm(left_ref[...], right_ref[...], TN).astype(out_ref.dtype)


def plain_cross_call(left, right, name):
    tokens, rows = left.shape
    columns = right.shape[1]
    tile = 512
    return pl.pallas_call(
        plain_cross_kernel,
        name=name,
        grid=(rows // tile,),
        in_specs=[pl.BlockSpec((tokens, tile), lambda i: (0, i)), whole((tokens, columns))],
        out_specs=pl.BlockSpec((tile, columns), lambda i: (i, 0)),
        out_shape=sds((rows, columns), BF),
        compiler_params=params(1),
        cost_estimate=busy(7.5),
    )(left, right)


def input_q_kernel(dq_ref, w_ref, out_ref):
    out_ref[...] = mm(dq_ref[...], w_ref[...], NT)


def input_q_call(d_q, w_full):
    tokens = d_q.shape[0]
    width = w_full.shape[0]
    tile = 512
    return pl.pallas_call(
        input_q_kernel,
        name="input_grad_q",
        grid=(width // tile,),
        in_specs=[whole((tokens, HQ)), pl.BlockSpec((tile, HQ), lambda i: (i, 0))],
        out_specs=pl.BlockSpec((tokens, tile), lambda i: (0, i)),
        out_shape=sds((tokens, width), F32),
        compiler_params=params(1),
        cost_estimate=busy(6),
    )(d_q, w_full)


def final_kernel(
    terms,
    order_ref,
    x_ref,
    low_ref,
    resid_ref,
    gq_ref,
    gain_ref,
    moe_ref,
    w_ref,
    cos_ref,
    sin_ref,
    *rest,
):
    parts = rest[:terms]
    grad_ref = rest[terms]
    outs = rest[terms + 1 : -2]
    made, sems = rest[-2:]
    scale_k = HEAD ** (-0.5)
    cosine, sine = cos_ref[...], -sin_ref[...]
    key_grads, value_grads = [], []
    for group in range(KV_HEADS):
        span = slice(group * 2 * HEAD, (group + 1) * 2 * HEAD)
        total = parts[0][:, span].astype(F32)
        for part in parts[1:]:
            total += part[:, span].astype(F32)
        key_grads.append(turn(total[:, 0:HEAD] * scale_k, cosine, sine).astype(BF))
        value_grads.append(total[:, HEAD:].astype(BF))
    low = jnp.concatenate(key_grads + value_grads, 1)
    made[:, 0 : 2 * KVW] = mm(low_ref[...], low, TN).astype(BF)
    wide = x_ref[...].astype(F32)
    scale = lax.rsqrt(jnp.mean(wide * wide, -1, keepdims=True) + EPS)
    normed = wide * scale
    grad = gq_ref[...] + mm(low, w_ref[...], NT)
    product = grad * normed
    gain_part = jnp.sum(product, 0, keepdims=True)
    width = x_ref.shape[1]
    lines = lax.broadcasted_iota(jnp.int32, (LANES, width), 0)
    both = jnp.where(lines == 0, gain_part, jnp.where(lines == 1, moe_ref[0:1], 0.0))
    made[:, 2 * KVW :] = jnp.transpose(both).astype(BF)
    if len(outs) == 2:
        copies = block_copies(order_ref, made, *outs, sems)
    else:
        copies = [pltpu.make_async_copy(made, outs[0], sems.at[0])]
    for copy in copies:
        copy.start()
    gain = gain_ref[0:1]
    mean = jnp.mean(product * gain, -1, keepdims=True)
    own = (scale * (grad * gain - normed * mean)).astype(BF)
    grad_ref[...] = (resid_ref[...] + own.astype(F32)).astype(BF)
    for copy in copies:
        copy.wait()


def final_call(
    order, x, low, resid, grad_q, gains, moe_part, w_full, cosine, sine, parts, layout, after=()
):
    tokens, width = x.shape
    columns = 2 * KVW + LANES
    if layout:
        outs = [sds(blocks_shape(*layout, width, columns), BF)] * 2
    else:
        outs = [sds((width, columns), BF)]
    grid = pltpu.PrefetchScalarGridSpec(
        num_scalar_prefetch=1,
        grid=(1,),
        in_specs=[whole((tokens, width))] * 4
        + [whole((8, width))] * 2
        + [pl.BlockSpec((width, 2 * KVW), lambda i, _: (0, HQ // (2 * KVW)))]
        + [whole((tokens, HEAD))] * 2
        + [whole((tokens, 2 * KVW))] * len(parts)
        + [ANY] * len(after),
        out_specs=[whole((tokens, width))] + [ANY] * len(outs),
        scratch_shapes=[
            pltpu.VMEM((width, columns), BF),
            pltpu.SemaphoreType.DMA((layout[0] * layout[1] if layout else 1,)),
        ],
    )
    return pl.pallas_call(
        without(lambda *refs: final_kernel(len(parts), *refs), 10 + len(parts), len(after)),
        name="final",
        grid_spec=grid,
        out_shape=[sds((tokens, width), BF)] + outs,
        compiler_params=params(1),
        cost_estimate=busy(10),
    )(order, x, low, resid, grad_q, gains, moe_part, w_full, cosine, sine, *parts, *after)


def hold_kernel(count, *refs):
    del count, refs


def hold(arrays, *until):
    until = [array for array in until if array is not None]
    if not until:
        return arrays
    count = len(arrays)
    return pl.pallas_call(
        lambda *refs: hold_kernel(count, *refs),
        name="hold",
        in_specs=[ANY] * (count + len(until)),
        out_specs=[ANY] * count,
        out_shape=[sds(array.shape, array.dtype) for array in arrays],
        input_output_aliases={place: place for place in range(count)},
        cost_estimate=busy(0.5),
    )(*arrays, *until)


def local(
    layer_input,
    lengths,
    expert_ids,
    gate_weights,
    attn_gain,
    wq,
    wk,
    wv,
    wo,
    moe_gain,
    w_gate,
    w_up,
    w_down,
    cotangent,
):
    count = lax.axis_size("ctx")
    shards_of = lax.axis_size("fsdp")
    both = ("ctx", "fsdp")
    ring = Ring(count)
    me = lax.axis_index("ctx").astype(jnp.int32)
    own = lax.axis_index("fsdp").astype(jnp.int32)
    x = layer_input[0]
    dy = cotangent[0]
    tokens, width = x.shape
    exp_dev = w_gate.shape[0]
    experts = exp_dev * count
    capacity = 3 * tokens * TOPK // (2 * experts)

    sources = ring.sources()
    places = jnp.concatenate([jnp.stack([own, me]), sources])
    layout = (count, shards_of) if ring.length == 4 and shards_of == 4 else None
    rows = wq.shape[0]
    gains_part = jnp.concatenate(
        [attn_gain[:, None], moe_gain[:, None], jnp.zeros((rows, LANES - 2), BF)], 1
    )
    w_full = lax.all_gather(
        jnp.concatenate([wq, wk, wv, wo.T, gains_part], 1), both, axis=0, tiled=True
    )

    gates = gate_weights[0]
    gate_high = gates.astype(BF)
    rest = gates - gate_high.astype(F32)
    gate_mid = rest.astype(BF)
    gate_low = (rest - gate_mid.astype(F32)).astype(BF)
    info = jnp.concatenate(
        [
            dy,
            expert_ids[0].astype(BF),
            gate_high,
            gate_mid,
            gate_low,
            jnp.zeros((tokens, LANES - 4 * TOPK), BF),
        ],
        1,
    )
    ends = jnp.cumsum(lengths[0])
    index = me * tokens + jnp.arange(tokens, dtype=jnp.int32)
    after = (index[:, None] >= ends[None, :]).astype(jnp.int32)
    start = jnp.sum(after * lengths[0][None, :], 1)
    half = HEAD // 2
    freq = jnp.exp(jnp.arange(half, dtype=F32) * (-2.0 * math.log(ROPE_BASE) / HEAD))
    angle = (index - start).astype(F32)[:, None] * freq[None, :]
    cosine = jnp.cos(angle)
    sine = jnp.sin(angle)
    cosine = jnp.concatenate([cosine, cosine], 1)
    sine = jnp.concatenate([-sine, sine], 1)
    order = jnp.concatenate(
        [me[None], (start[0] // tokens)[None], ends[: HEADER - 2], sources]
    )

    late = []
    run = ring.gather(info, late)
    next(run)
    grads = [run.send(None)]
    q, kv, low_one, gains = qkv_call(
        x, w_full, cosine, sine, [grads[0][1]] if layout else []
    )
    shards = gather_shards(
        jnp.stack([w_gate, w_up, jnp.swapaxes(w_down, 1, 2)]), shards_of, kv
    )
    kv_couples = ring.gather_now(kv)
    kv_slots = [part for couple in kv_couples for part in couple]
    half = count // 2
    parts, made, routed = [], [], []

    def route(step, after=()):
        routed.append(route_call(places, grads[step], shards, capacity, width, after))
        return routed[-1][4]

    late.append(kv_couples[3][0])
    grads.append(run.send(None))
    state = attn_call(order, q, kv_slots[:half], 0, False, after=[route(0)])
    attended, log_total = attn_call(order, q, kv_slots[half:], half, True, state)
    attn_rows, low_two = out_call(x, attended, w_full, gains)
    grads += [run.send(None) for _ in range(2, half)]

    def run_experts(step, couple, after):
        pick0, pick1, _, _, grad_hidden = routed[step]
        found = expert_call(
            places, couple, (pick0, pick1), grad_hidden, shards, capacity, after
        )
        made.append(found[:4])
        parts.append((found[4], found[5]))
        return found[4]

    rows_run = ring.gather(low_two)
    next(rows_run)
    mark = route(2, [route(1)])
    couple = rows_run.send(mark)
    mark = run_experts(0, couple, [mark])
    couple = rows_run.send(mark)
    for step in range(3, half):
        mark = route(step, [couple[1]])
    mark = run_experts(1, couple, [mark])
    for step in range(2, half):
        couple = rows_run.send(mark)
        mark = run_experts(step, couple, [mark])

    y_pairs = []

    def down(step, after):
        pick0, pick1, gate_rows = routed[step][:3]
        place = (half - 1 - step) % (half // 2)
        out, pair = down_call(
            places,
            made[step][1],
            gate_rows,
            (pick0, pick1),
            shards,
            capacity,
            width,
            place,
            y_pairs.pop() if place else None,
            half // 2,
            after,
        )
        y_pairs.append(pair)
        return out

    grad_run = ring.scatter(parts)
    grad_mark = next(grad_run)
    expert_grads = []
    for expert in range(exp_dev):
        made_grad = weight_grad_call(
            expert,
            [entry[0] for entry in made],
            [entry[3] for entry in routed],
            [entry[2] for entry in made],
            [entry[3] for entry in made],
            [entry[1] for entry in made],
            [mark, grad_mark],
        )
        expert_grads.append(
            lax.psum_scatter(made_grad, "fsdp", scatter_dimension=1, tiled=True).astype(F32)
        )
        mark = made_grad
        if expert < 2:
            grad_mark = grad_run.send(mark)
    expert_grads = jnp.stack(expert_grads, 1)
    y_parts = [None] * len(made)
    for step in reversed(range(len(made))):
        y_parts[step] = down(step, [mark, grad_mark])
        mark = y_parts[step]
        if step == len(made) // 2:
            grad_mark = grad_run.send(mark)
    grad_parts = grad_run.send(mark)
    y_run = ring.scatter_pairs(y_parts, hold(y_pairs, grad_mark))
    next(y_run)

    resid, grad_attn, grad_out, delta, moe_part = resid_back_call(
        x, attn_rows, dy, gains, w_full, attended, grad_parts
    )
    back = attn_back_call(
        0, order, q, grad_out, log_total, delta, cosine, sine, kv_slots
    )
    d_q = [back[0]]
    mark = y_run.send(back[0])
    back = attn_back_call(
        1,
        order,
        q,
        grad_out,
        log_total,
        delta,
        cosine,
        sine,
        kv_slots,
        back[1:],
        [mark],
    )
    d_q.append(back[0])
    kv_terms = ring.scatter_now(
        [(back[1 + 2 * step], back[2 + 2 * step]) for step in range(half)]
    )
    y_run.send(kv_terms[-1])

    d_q = jnp.concatenate(d_q, 1)
    grad_q = input_q_call(d_q, w_full)
    after = []
    if layout:
        wq_part = cross_call(places, low_one, d_q, *layout, "wq_grad")
        wo_part = cross_call(places, hold([grad_attn], d_q)[0], attended, *layout, "wo_grad")
        wo_terms, wo_sent = scatter_all_across(*wo_part, shards_of)
        wq_terms, wq_sent = scatter_all_across(*wq_part, shards_of)
        after = [wo_sent, wq_sent]
    else:
        wq_grad, wo_grad = [
            lax.psum_scatter(
                plain_cross_call(left, right, name), both, scatter_dimension=0, tiled=True
            ).astype(F32)
            for left, right, name in (
                (low_one, d_q, "wq_grad"),
                (grad_attn, attended, "wo_grad"),
            )
        ]
    input_grad, *tail = final_call(
        places,
        x,
        low_one,
        resid,
        grad_q,
        gains,
        moe_part,
        w_full,
        cosine,
        sine,
        kv_terms,
        layout,
        after,
    )
    if layout:
        terms = jnp.concatenate([wo_terms, wq_terms], -1)
        first_run = scatter_all_along(hold([terms], kv_terms[-1])[0], ring)
        next(first_run)
        tail, tail_sent = scatter_all_across(*tail, shards_of)
        y_run.send(tail_sent)
        last_run = scatter_all_along(tail, ring)
        next(last_run)
        for _ in range(4):
            terms = first_run.send(None)
            tail = last_run.send(None)
        wo_grad, wq_grad = terms[:, :HQ], terms[:, HQ:]
    else:
        y_run.send(None)
        tail = lax.psum_scatter(tail[0], both, scatter_dimension=0, tiled=True).astype(F32)
    y_terms = y_run.send(None)
    moe = y_terms[0].astype(F32)
    for term in y_terms[1:]:
        moe = moe + term.astype(F32)
    output = (x.astype(F32) + attn_rows.astype(F32) + moe).astype(BF)
    return (
        output[None],
        input_grad[None],
        tail[:, 2 * KVW],
        wq_grad,
        tail[:, 0:KVW],
        tail[:, KVW : 2 * KVW],
        wo_grad.T,
        tail[:, 2 * KVW + 1],
        expert_grads[0],
        expert_grads[1],
        jnp.swapaxes(expert_grads[2], 1, 2),
    )


def solution(mesh):
    return jax.shard_map(
        local,
        mesh=mesh,
        in_specs=(
            P("fsdp", "ctx", None),
            P("fsdp", None),
            P("fsdp", "ctx", None),
            P("fsdp", "ctx", None),
            P(("ctx", "fsdp")),
            P(("ctx", "fsdp"), None),
            P(("ctx", "fsdp"), None),
            P(("ctx", "fsdp"), None),
            P(None, ("ctx", "fsdp")),
            P(("ctx", "fsdp")),
            P("ctx", "fsdp", None),
            P("ctx", "fsdp", None),
            P("ctx", None, "fsdp"),
            P("fsdp", "ctx", None),
        ),
        out_specs=(
            P("fsdp", "ctx", None),
            P("fsdp", "ctx", None),
            P(("ctx", "fsdp")),
            P(("ctx", "fsdp"), None),
            P(("ctx", "fsdp"), None),
            P(("ctx", "fsdp"), None),
            P(None, ("ctx", "fsdp")),
            P(("ctx", "fsdp")),
            P("ctx", "fsdp", None),
            P("ctx", "fsdp", None),
            P("ctx", None, "fsdp"),
        ),
        check_vma=False,
    )
```

```python
import math

import jax
import jax.numpy as jnp
from jax import lax
from jax.experimental import pallas as pl
from jax.experimental.pallas import tpu as pltpu
from jax.sharding import PartitionSpec as P

HEADS = 12
KV_HEADS = 2
HEAD = 128
TOPK = 4
REPEAT = HEADS // KV_HEADS
HQ = HEADS * HEAD
KVW = KV_HEADS * HEAD
LANES = 128

EPS = 1e-06
ROPE_BASE = 10000.0
NEG = -1e30
BF = jnp.bfloat16
F32 = jnp.float32
NN = ((1,), (0,))
NT = ((1,), (1,))
TN = ((0,), (0,))
ANY = pl.BlockSpec(memory_space=pl.ANY)
MIB = 1024 * 1024
SCALE = 0.4


def mm(left, right, dims=NN):
    return lax.dot_general(left, right, (dims, ((), ())), preferred_element_type=F32)


def params(grid_rank, limit=56):
    return pltpu.CompilerParams(
        dimension_semantics=("arbitrary",) * grid_rank, vmem_limit_bytes=limit * MIB
    )


def busy(microseconds):
    return pl.CostEstimate(
        flops=int(microseconds * SCALE * 1.15e9), bytes_accessed=1024, transcendentals=0
    )


def sds(shape, dtype):
    return jax.ShapeDtypeStruct(shape, dtype)


def whole(shape):
    return pl.BlockSpec(shape, lambda *_: (0,) * len(shape))


def without(kernel, place, extra):
    def run(*refs):
        kernel(*refs[:place], *refs[place + extra :])

    return run


class Ring:
    def __init__(self, count):
        self.count = count
        self.low_pair = count == 8
        self.length = count // 2
        self.me = lax.axis_index("ctx")
        if self.low_pair:
            self.line, self.pair = self.me // 2, self.me % 2
        else:
            self.line, self.pair = self.me % self.length, self.me // self.length
        if self.length == 4:
            self.table = [[0, 1, 2, 3], [1, 0, 2, 3], [2, 3, 1, 0], [3, 2, 1, 0]]
        else:
            self.table = [
                [(place + step) % self.length for step in range(self.length)]
                for place in range(self.length)
            ]

    def index(self, line, pair):
        return line * 2 + pair if self.low_pair else pair * self.length + line

    def move(self, array, hops):
        pairs = [
            (self.index(source, side), self.index(target, side))
            for source, target in hops
            for side in (0, 1)
        ]
        return lax.ppermute(array, "ctx", pairs)

    def swap(self, array):
        pairs = [
            (self.index(place, side), self.index(place, 1 - side))
            for place in range(self.length)
            for side in (0, 1)
        ]
        return lax.ppermute(array, "ctx", pairs)

    def sources(self):
        line = jnp.asarray(self.table, jnp.int32)[self.line]
        side = jnp.stack([self.pair, 1 - self.pair]).astype(jnp.int32)
        return self.index(line[:, None], side[None, :]).reshape(-1).astype(jnp.int32)

    def spread(self, array):
        everything = lax.all_gather(array, "ctx", axis=0)
        order = self.sources()
        rows = [
            lax.dynamic_index_in_dim(everything, order[slot], 0, keepdims=False)
            for slot in range(self.count)
        ]
        return [(rows[2 * step], rows[2 * step + 1]) for step in range(self.length)]

    def gather(self, array):
        if self.length != 4:
            yield
            for couple in self.spread(array):
                yield couple
            return
        ends = [(1, 0), (2, 3)]
        middle = [(1, 2), (2, 1)]
        couples = [(0, 1), (1, 0), (2, 3), (3, 2)]
        first = self.move(array, couples)
        cross = self.move(array, middle)
        swapped = self.swap(array)
        until = yield
        first, cross = hold([first, cross], until, swapped)
        swapped = hold([swapped], cross)[0]
        outward = self.move(cross, ends)
        cross_two = self.move(first, middle)
        swapped_first = self.swap(first)
        until = yield (array, swapped)
        outward, cross_two = hold([outward, cross_two], until, swapped_first)
        second = cross + outward
        swapped_first = hold([swapped_first], second)[0]
        until = yield (first, swapped_first)
        cross_two, second = hold([cross_two, second], until)
        outward_two = self.move(cross_two, ends)
        swapped_second = self.swap(second)
        until = yield (second, swapped_second)
        outward_two = hold([outward_two], until, swapped_second)[0]
        third = cross_two + outward_two
        yield (third, self.swap(third))

    def gather_now(self, array):
        run = self.gather(array)
        next(run)
        return [run.send(None) for _ in range(self.length)]

    def scatter(self, parts, chained=False):
        if self.length != 4:
            order = self.sources()
            rows = jnp.stack([part for couple in parts for part in couple])
            placed = jnp.zeros_like(rows).at[order].set(rows)
            total = lax.psum_scatter(placed, "ctx", scatter_dimension=0, tiled=False)
            for _ in range(4):
                yield total
            yield [total]
            return
        inward = [(0, 1), (3, 2)]
        middle = [(1, 2), (2, 1)]
        couples = [(0, 1), (1, 0), (2, 3), (3, 2)]

        others = [part[1] for part in parts]
        if chained:
            others[:3] = hold(others[:3], others[3])
        swapped = [self.swap(other) for other in others]
        until = yield parts[3][1]
        arrived = hold([swapped[3]], until)[0]
        third = parts[3][0] + arrived
        from_end = self.move(third, inward)
        arrived = swapped[2]
        until = yield third
        from_end, arrived = hold([from_end, arrived], until)
        sent = third + from_end
        crossed = self.move(sent, middle)
        second = parts[2][0] + arrived
        from_end_two = self.move(second, inward)
        arrived = swapped[1]
        until = yield second
        crossed, from_end_two, arrived = hold([crossed, from_end_two, arrived], until)
        sent = parts[1][0] + arrived + crossed
        last = self.move(sent, couples)
        crossed_two = self.move(second + from_end_two, middle)
        arrived = swapped[0]
        until = yield sent
        last, crossed_two, arrived = hold([last, crossed_two, arrived], until)
        yield [parts[0][0], arrived, crossed_two, last]

    def scatter_late(self, parts, others):
        if self.length != 4:
            flat = [other[place] for other in others for place in range(other.shape[0])]
            yield from self.scatter(list(zip(parts, reversed(flat))))
            return
        inward = [(0, 1), (3, 2)]
        middle = [(1, 2), (2, 1)]
        couples = [(0, 1), (1, 0), (2, 3), (3, 2)]
        swapped = [self.swap(other) for other in others]
        until = yield others[0]
        third = parts[3] + hold([swapped[0]], until)[0][0]
        from_end = self.move(third, inward)
        until = yield third
        from_end, *swapped = hold([from_end, *swapped[1:]], until)
        until = yield from_end
        third, *swapped = hold([third, *swapped], until)
        crossed = self.move(third + from_end, middle)
        second = parts[2] + swapped[0][0]
        from_end_two = self.move(second, inward)
        until = yield second
        crossed, from_end_two = hold([crossed, from_end_two], until)
        last = self.move(parts[1] + swapped[1][0] + crossed, couples)
        crossed_two = self.move(second + from_end_two, middle)
        yield [parts[0], swapped[1][1], crossed_two, last]

    def scatter_now(self, parts):
        run = self.scatter(parts)
        next(run)
        made = [run.send(None) for _ in range(4)]
        return made[-1]


def neighbour(array, axis_size, bit):
    pairs = [(index, index ^ (1 << bit)) for index in range(axis_size)]
    return lax.ppermute(array, "fsdp", pairs)


def gather_shards(array, axis_size, until=None):
    slots = {0: array}
    bits = axis_size.bit_length() - 1
    for bit in reversed(range(bits)):
        for slot in list(slots):
            taken = slots[slot]
            if slot and bit == 0 and until is not None:
                taken = slots[slot] = hold([taken], until)[0]
            slots[slot | (1 << bit)] = neighbour(taken, axis_size, bit)
    return [slots[slot] for slot in range(axis_size)]


def scatter_all_across(near, far, axis_size):
    arrived = neighbour(far, axis_size, 0)
    sent = near[1] + arrived[1]
    return near[0] + arrived[0] + neighbour(sent, axis_size, 1), sent


def scatter_all_along(terms, ring):
    swapped = ring.swap(terms[1])
    swapped = hold([swapped], (yield))[0]
    lines = terms[0] + swapped
    ends = ring.move(lines[2:4], [(0, 1), (3, 2)])
    ends = hold([ends], (yield))[0]
    middle = ring.move(lines[2:4] + ends, [(1, 2), (2, 1)])
    middle = hold([middle], (yield))[0]
    last = ring.move(lines[1] + middle[1], [(0, 1), (1, 0), (2, 3), (3, 2)])
    last = hold([last], (yield))[0]
    yield lines[0].astype(F32) + middle[0].astype(F32) + last.astype(F32)


def turn(values, cosine, sine):
    return values * cosine + pltpu.roll(values, HEAD // 2, 1) * sine


def qkv_kernel(x_ref, w_ref, g_ref, cos_ref, sin_ref, q_ref, kv_ref, low_ref, gain_ref):
    step = pl.program_id(0)
    blocks = HQ // 512

    @pl.when(step == 0)
    def _():
        gains = jnp.transpose(g_ref[...].astype(F32))
        gain_ref[...] = gains[0:8]
        wide = x_ref[...].astype(F32)
        scale = lax.rsqrt(jnp.mean(wide * wide, -1, keepdims=True) + EPS)
        low_ref[...] = (wide * scale * gains[0:1]).astype(BF)

    raw = mm(low_ref[...], w_ref[...])
    cosine, sine = cos_ref[...], sin_ref[...]

    def turned(count):
        return [
            turn(raw[:, head * HEAD : (head + 1) * HEAD], cosine, sine).astype(BF)
            for head in range(count)
        ]

    @pl.when(step < blocks)
    def _():
        for head, value in enumerate(turned(4)):
            q_ref[:, head * HEAD : (head + 1) * HEAD] = value

    @pl.when(step == blocks)
    def _():
        for head, value in enumerate(turned(KV_HEADS)):
            kv_ref[:, head * HEAD : (head + 1) * HEAD] = value
        kv_ref[:, KVW:] = raw[:, KVW:].astype(BF)


def qkv_call(x, w_full, cosine, sine, after=()):
    tokens, width = x.shape
    blocks = HQ // 512
    return pl.pallas_call(
        without(qkv_kernel, 5, len(after)),
        name="qkv",
        grid=(blocks + 1,),
        in_specs=[
            whole((tokens, width)),
            pl.BlockSpec((width, 512), lambda i: (0, i)),
            pl.BlockSpec((width, LANES), lambda i: (0, (2 * HQ + 2 * KVW) // LANES)),
            whole((tokens, HEAD)),
            whole((tokens, HEAD)),
        ]
        + [ANY] * len(after),
        out_specs=[
            pl.BlockSpec((tokens, 512), lambda i: (0, jnp.minimum(i, HQ // 512 - 1))),
            whole((tokens, 2 * KVW)),
            whole((tokens, width)),
            whole((8, width)),
        ],
        out_shape=[
            sds((tokens, HQ), BF),
            sds((tokens, 2 * KVW), BF),
            sds((tokens, width), BF),
            sds((8, width), F32),
        ],
        compiler_params=params(1),
        cost_estimate=busy(9),
    )(x, w_full, w_full, cosine, sine, *after)


HEADER = 5
SEQS = 3
COUPLE = 2
COUPLES = HEADS // COUPLE
LOG2E = math.log2(math.e)


def load_kv(slots, kv_all, sems):
    copies = [
        pltpu.make_async_copy(slot, kv_all.at[place], sems.at[place])
        for place, slot in enumerate(slots)
    ]
    for copy in copies:
        copy.start()
    for copy in copies:
        copy.wait()


def sequence_of(order_ref, index):
    ends = [order_ref[2 + place] for place in range(SEQS - 1)]
    return sum((index >= end).astype(jnp.int32) for end in ends)


def extend_queries(order_ref, q_ref, wide):
    tokens = q_ref.shape[0]
    rows = order_ref[0] * tokens + lax.broadcasted_iota(jnp.int32, (tokens, LANES), 0)
    lanes = lax.broadcasted_iota(jnp.int32, (tokens, LANES), 1)
    other = (lanes < SEQS) & (lanes != sequence_of(order_ref, rows))
    extra = jnp.where(other | (lanes > SEQS + order_ref[0]), NEG, 0.0).astype(BF)
    for place in range(COUPLE):
        span = slice(place * tokens, (place + 1) * tokens)
        wide[span, 0:HEAD] = q_ref[:, place * HEAD : (place + 1) * HEAD]
        wide[span, HEAD:] = extra


def extend_keys(order_ref, base, kv_all, groups, wide, turned, which):
    count, tokens, columns = kv_all.shape
    lanes = lax.broadcasted_iota(jnp.int32, (tokens, LANES), 1)
    sublanes = lax.broadcasted_iota(jnp.int32, (tokens, LANES), 0)
    for slot in range(count):
        block = order_ref[HEADER + base + slot]
        mine = lanes == sequence_of(order_ref, block * tokens + sublanes)
        unit = jnp.where(mine | (lanes == SEQS + block), 1.0, 0.0).astype(BF)
        for group in range(groups):
            span = slice(group * HEAD, (group + 1) * HEAD)
            wide[group, slot, :, 0:HEAD] = kv_all[slot, :, span]
            wide[group, slot, :, HEAD:] = unit
            start = which * groups * HEAD + group * HEAD
            taken = kv_all[slot, :, start : start + HEAD].astype(F32)
            turned[
                group * HEAD : (group + 1) * HEAD, slot * tokens : (slot + 1) * tokens
            ] = jnp.transpose(taken).astype(BF)


def causal(scores):
    tokens = scores.shape[0]
    keys = lax.broadcasted_iota(jnp.int32, (tokens, tokens), 0)
    queries = lax.broadcasted_iota(jnp.int32, (tokens, tokens), 1)
    kept = jnp.concatenate([keys <= queries] * COUPLE, 1)
    return jnp.where(kept, scores, NEG)


def attn_kernel(count, base, last, order_ref, q_ref, *rest):
    slots, rest = rest[:count], rest[count:]
    if base:
        acc_in, stat_in, *rest = rest
    if last:
        out_ref, total_ref, *rest = rest
    else:
        acc_out, stat_out, *rest = rest
    kv_all, keys, values, queries, spread, acc, stat, sems = rest
    step = pl.program_id(0)
    tokens = q_ref.shape[0]
    factor = HEAD ** (-0.5) * LOG2E

    @pl.when(step == 0)
    def _():
        load_kv(slots, kv_all, sems)
        extend_keys(order_ref, base, kv_all, KV_HEADS, keys, values, 1)

    group = step * COUPLE // REPEAT
    extend_queries(order_ref, q_ref, queries)
    if base:
        acc[...] = acc_in[0]
        stat[...] = stat_in[0]
    else:
        acc[...] = jnp.zeros_like(acc)
        stat[...] = jnp.zeros_like(stat)
        stat[0:1] = jnp.full((1, COUPLE * tokens), NEG, F32)

    scores = []
    new_peak = stat[0:1]
    for slot in range(count):
        made = mm(keys[group, slot], queries[...], NT)
        if base + slot == 0:
            made = causal(made)
        new_peak = jnp.maximum(new_peak, jnp.max(made, 0, keepdims=True))
        scores.append(made)
    keep = jnp.exp2((stat[0:1] - new_peak) * factor)
    total = stat[1:2] * keep
    added = acc[...] * keep
    for slot in range(count):
        weights = jnp.exp2((scores[slot] - new_peak) * factor)
        total += jnp.sum(weights, 0, keepdims=True)
        spread[slot * tokens : (slot + 1) * tokens] = weights.astype(BF)
    own = pl.ds(pl.multiple_of(group * HEAD, HEAD), HEAD)
    added += mm(values[own, :], spread[...])
    stat[0:1] = new_peak
    stat[1:2] = total
    acc[...] = added

    if last:
        made = acc[...] / stat[1:2]
        log_total = stat[0:1] * factor + jnp.log(stat[1:2]) * LOG2E
        for place in range(COUPLE):
            span = slice(place * tokens, (place + 1) * tokens)
            out_ref[:, place * HEAD : (place + 1) * HEAD] = jnp.transpose(made[:, span]).astype(BF)
            total_ref[0, place : place + 1] = log_total[:, span]
    else:
        acc_out[0] = acc[...]
        stat_out[0] = stat[...]


def attn_call(order, q, slots, base, last, state=(), after=()):
    tokens = q.shape[0]
    count = len(slots)
    wide = COUPLE * tokens
    column = lambda h, _: (0, h)
    by_step = lambda h, _: (h, 0, 0)
    if last:
        out_specs = [
            pl.BlockSpec((tokens, COUPLE * HEAD), column),
            pl.BlockSpec((1, 8, tokens), by_step),
        ]
        out_shape = [sds((tokens, HQ), BF), sds((COUPLES, 8, tokens), F32)]
    else:
        out_specs = [
            pl.BlockSpec((1, HEAD, wide), by_step),
            pl.BlockSpec((1, 8, wide), by_step),
        ]
        out_shape = [sds((COUPLES, HEAD, wide), F32), sds((COUPLES, 8, wide), F32)]
    state_specs = [
        pl.BlockSpec((1, HEAD, wide), by_step),
        pl.BlockSpec((1, 8, wide), by_step),
    ]
    grid = pltpu.PrefetchScalarGridSpec(
        num_scalar_prefetch=1,
        grid=(COUPLES,),
        in_specs=[pl.BlockSpec((tokens, COUPLE * HEAD), column)]
        + [ANY] * count
        + (state_specs if base else [])
        + [ANY] * len(after),
        out_specs=out_specs,
        scratch_shapes=[
            pltpu.VMEM((count, tokens, 2 * KVW), BF),
            pltpu.VMEM((KV_HEADS, count, tokens, 2 * HEAD), BF),
            pltpu.VMEM((KV_HEADS * HEAD, count * tokens), BF),
            pltpu.VMEM((wide, 2 * HEAD), BF),
            pltpu.VMEM((count * tokens, wide), BF),
            pltpu.VMEM((HEAD, wide), F32),
            pltpu.VMEM((8, wide), F32),
            pltpu.SemaphoreType.DMA((count,)),
        ],
    )
    return pl.pallas_call(
        without(
            lambda *refs: attn_kernel(count, base, last, *refs),
            2 + count + len(state),
            len(after),
        ),
        name="attention",
        grid_spec=grid,
        out_shape=out_shape,
        compiler_params=params(1),
        cost_estimate=busy(18),
    )(order, q, *slots, *state, *after)


def attn_back_kernel(count, group, order_ref, q_ref, do_ref, total_ref, delta_ref, *rest):
    cos_ref, sin_ref = rest[:2]
    slots, rest = rest[2 : 2 + count], rest[2 + count :]
    if group:
        rest = rest[count:]
    dq_ref, rest = rest[0], rest[1:]
    outs, rest = rest[:count], rest[count:]
    kv_all, keys, turned, queries, grads, spread, d_k, d_v, packed, sems = rest
    step = pl.program_id(0)
    tokens = q_ref.shape[0]
    scale = HEAD ** (-0.5)

    @pl.when(step == 0)
    def _():
        for part in range(2):
            columns = slice(part * KVW + group * HEAD, part * KVW + (group + 1) * HEAD)
            load_kv(
                [slot.at[:, columns] for slot in slots],
                kv_all.at[:, :, part * HEAD : (part + 1) * HEAD],
                sems,
            )
        extend_keys(order_ref, 0, kv_all, 1, keys, turned, 0)
        d_k[...] = jnp.zeros_like(d_k)
        d_v[...] = jnp.zeros_like(d_v)

    extend_queries(order_ref, q_ref, queries)
    for place in range(COUPLE):
        span = slice(place * tokens, (place + 1) * tokens)
        grads[span] = do_ref[:, place * HEAD : (place + 1) * HEAD]

    log_total = jnp.concatenate([total_ref[0, place : place + 1] for place in range(COUPLE)], 1)
    delta = jnp.concatenate([delta_ref[0, place : place + 1] for place in range(COUPLE)], 1)

    for slot in range(count):
        scores = mm(keys[0, slot], queries[...], NT)
        if slot == 0:
            scores = causal(scores)
        probs = jnp.exp2(scores * (scale * LOG2E) - log_total)
        grad_probs = mm(kv_all[slot, :, HEAD:], grads[...], NT)
        grad_scores = (probs * (grad_probs - delta)).astype(BF)
        spread[slot * tokens : (slot + 1) * tokens] = grad_scores
        d_v[slot] += mm(probs.astype(BF), grads[...])
        d_k[slot] += mm(grad_scores, queries[:, 0:HEAD])
    d_q = mm(turned[...], spread[...])
    for place in range(COUPLE):
        span = slice(place * tokens, (place + 1) * tokens)
        piece = jnp.transpose(d_q[:, span]) * scale
        dq_ref[:, place * HEAD : (place + 1) * HEAD] = turn(
            piece, cos_ref[...], -sin_ref[...]
        ).astype(BF)

    @pl.when(step == pl.num_programs(0) - 1)
    def _():
        copies = []
        for place in range(count):
            packed[place, :, 0:HEAD] = d_k[place].astype(BF)
            packed[place, :, HEAD:] = d_v[place].astype(BF)
            columns = pl.ds(group * 2 * HEAD, 2 * HEAD)
            copies.append(
                pltpu.make_async_copy(
                    packed.at[place], outs[place].at[:, columns], sems.at[place]
                )
            )
            copies[-1].start()
        for copy in copies:
            copy.wait()


def attn_back_call(
    group, order, q, grad, log_total, delta, cosine, sine, slots, held=(), after=()
):
    tokens = q.shape[0]
    count = len(slots)
    steps = REPEAT // COUPLE
    column = lambda h, _: (0, group * steps + h)
    by_step = lambda h, _: (group * steps + h, 0, 0)
    fixed = lambda h, _: (0, 0)
    grid = pltpu.PrefetchScalarGridSpec(
        num_scalar_prefetch=1,
        grid=(steps,),
        in_specs=[
            pl.BlockSpec((tokens, COUPLE * HEAD), column),
            pl.BlockSpec((tokens, COUPLE * HEAD), column),
            pl.BlockSpec((1, 8, tokens), by_step),
            pl.BlockSpec((1, 8, tokens), by_step),
            pl.BlockSpec((tokens, HEAD), fixed),
            pl.BlockSpec((tokens, HEAD), fixed),
        ]
        + [ANY] * (count + len(held) + len(after)),
        out_specs=[pl.BlockSpec((tokens, COUPLE * HEAD), lambda h, _: (0, h))] + [ANY] * count,
        scratch_shapes=[
            pltpu.VMEM((count, tokens, 2 * HEAD), BF),
            pltpu.VMEM((1, count, tokens, 2 * HEAD), BF),
            pltpu.VMEM((HEAD, count * tokens), BF),
            pltpu.VMEM((COUPLE * tokens, 2 * HEAD), BF),
            pltpu.VMEM((COUPLE * tokens, HEAD), BF),
            pltpu.VMEM((count * tokens, COUPLE * tokens), BF),
            pltpu.VMEM((count, tokens, HEAD), F32),
            pltpu.VMEM((count, tokens, HEAD), F32),
            pltpu.VMEM((count, tokens, 2 * HEAD), BF),
            pltpu.SemaphoreType.DMA((count,)),
        ],
    )
    return pl.pallas_call(
        without(
            lambda *refs: attn_back_kernel(count, group, *refs),
            7 + count + len(held),
            len(after),
        ),
        name="attention_back",
        input_output_aliases={7 + count + place: 1 + place for place in range(len(held))},
        grid_spec=grid,
        out_shape=[sds((tokens, HQ // KV_HEADS), BF)] + [sds((tokens, 2 * KVW), BF)] * count,
        compiler_params=params(1),
        cost_estimate=busy(26),
    )(order, q, grad, log_total, delta, cosine, sine, *slots, *held, *after)


def out_kernel(x_ref, a_ref, *rest):
    w_refs, (gain_ref, rows_ref, low_ref) = rest[:-3], rest[-3:]
    made = mm(a_ref[:, 0:512], w_refs[0][...], NT)
    for place, w_ref in enumerate(w_refs[1:], 1):
        made += mm(a_ref[:, place * 512 : (place + 1) * 512], w_ref[...], NT)
    rows = made.astype(BF)
    rows_ref[...] = rows
    resid = x_ref[...].astype(F32) + rows.astype(F32)
    scale = lax.rsqrt(jnp.mean(resid * resid, -1, keepdims=True) + EPS)
    low_ref[...] = (resid * scale * gain_ref[1:2]).astype(BF)


def wo_specs(width):
    start = (HQ + 2 * KVW) // 512
    return [
        pl.BlockSpec((width, 512), lambda i, place=place: (0, start + place))
        for place in range(HQ // 512)
    ]


def out_call(x, attended, wo_t, gains, after=()):
    tokens, width = x.shape
    tile = 128
    return pl.pallas_call(
        without(out_kernel, 3 + HQ // 512, len(after)),
        name="attention_out",
        grid=(tokens // tile,),
        in_specs=[
            pl.BlockSpec((tile, width), lambda i: (i, 0)),
            pl.BlockSpec((tile, HQ), lambda i: (i, 0)),
            *wo_specs(width),
            whole((8, width)),
        ]
        + [ANY] * len(after),
        out_specs=[pl.BlockSpec((tile, width), lambda i: (i, 0))] * 2,
        out_shape=[sds((tokens, width), BF)] * 2,
        compiler_params=params(1),
        cost_estimate=busy(9),
    )(x, attended, *[wo_t] * (HQ // 512), gains, *after)


def weight_copies(shards, own, kinds, held, sems):
    size = shards[0].shape[2]
    groups = []
    for expert in range(shards[0].shape[1]):
        copies = []
        for slot, shard in enumerate(shards):
            rows = pl.ds(pl.multiple_of((own ^ slot) * size, 16), size)
            for place, kind in enumerate(kinds):
                copies.append(
                    pltpu.make_async_copy(
                        shard.at[kind, expert],
                        held.at[place, expert, rows],
                        sems.at[place, expert, slot],
                    )
                )
        groups.append(copies)
    return groups


def fetch_weights(shards, own, kinds, held, sems):
    groups = weight_copies(shards, own, kinds, held, sems)
    step = pl.program_id(0)

    @pl.when(step == 0)
    def _():
        for copies in groups:
            for copy in copies:
                copy.start()

    for expert, copies in enumerate(groups):

        @pl.when(step == expert)
        def _():
            for copy in copies:
                copy.wait()


def route_kernel(shards_of, capacity, order_ref, d0_ref, d1_ref, *rest):
    shards = rest[:shards_of]
    p0_ref, p1_ref, gate_ref, rows_ref, hid_ref, held, sems = rest[shards_of:]
    expert = pl.program_id(0)
    tokens = d0_ref.shape[0]
    width = rows_ref.shape[2]
    fetch_weights(shards, order_ref[0], (2,), held, sems)
    wanted = (order_ref[1] * held.shape[1] + expert).astype(F32)
    before = lax.broadcasted_iota(jnp.int32, (tokens, tokens), 0) < lax.broadcasted_iota(
        jnp.int32, (tokens, tokens), 1
    )
    before = jnp.where(before, 1.0, 0.0).astype(BF)
    places = lax.broadcasted_iota(jnp.int32, (capacity, tokens), 0).astype(F32)
    for side, (ref, p_ref) in enumerate(((d0_ref, p0_ref), (d1_ref, p1_ref))):
        info = jnp.transpose(ref[:, width:].astype(F32))
        chosen = jnp.where(info[0:TOPK] == wanted, 1.0, 0.0)
        gate = jnp.sum(
            chosen * (info[TOPK : 2 * TOPK] + info[2 * TOPK : 3 * TOPK] + info[3 * TOPK : 4 * TOPK]),
            0,
            keepdims=True,
        )
        named = jnp.sum(chosen, 0, keepdims=True)
        rank = mm(jnp.broadcast_to(named, (8, tokens)).astype(BF), before)[0:1]
        picks = jnp.where((places == rank) & (named > 0.5), 1.0, 0.0)
        weight = jnp.sum(picks * gate, 1, keepdims=True)
        picks = picks.astype(BF)
        p_ref[0] = picks
        span = slice(side * capacity, (side + 1) * capacity)
        gate_ref[0, span] = jnp.broadcast_to(weight, (capacity, LANES))
        rows_ref[0, span] = (mm(picks, ref[:, :width]) * weight).astype(BF)
    hid_ref[0] = mm(rows_ref[0], held[0, expert])


def route_call(order, grads, shards, capacity, width, after=()):
    tokens = grads[0].shape[0]
    _, experts, size, hidden = shards[0].shape
    rows = 2 * capacity
    by_expert = lambda e, _: (e, 0, 0)
    grid = pltpu.PrefetchScalarGridSpec(
        num_scalar_prefetch=1,
        grid=(experts,),
        in_specs=[pl.BlockSpec(grads[0].shape, lambda e, _: (0, 0))] * 2
        + [ANY] * (len(shards) + len(after)),
        out_specs=[pl.BlockSpec((1, capacity, tokens), by_expert)] * 2
        + [
            pl.BlockSpec((1, rows, LANES), by_expert),
            pl.BlockSpec((1, rows, width), by_expert),
            pl.BlockSpec((1, rows, hidden), by_expert),
        ],
        scratch_shapes=[
            pltpu.VMEM((1, experts, width, hidden), BF),
            pltpu.SemaphoreType.DMA((1, experts, len(shards))),
        ],
    )
    return pl.pallas_call(
        without(
            lambda *refs: route_kernel(len(shards), capacity, *refs), 3 + len(shards), len(after)
        ),
        name="route",
        grid_spec=grid,
        out_shape=[sds((experts, capacity, tokens), BF)] * 2
        + [
            sds((experts, rows, LANES), F32),
            sds((experts, rows, width), BF),
            sds((experts, rows, hidden), F32),
        ],
        compiler_params=params(1),
        cost_estimate=busy(8.5),
    )(order, *grads, *shards, *after)


def expert_kernel(shards_of, capacity, order_ref, x0_ref, x1_ref, p0_ref, p1_ref, gh_ref, *rest):
    shards = rest[:shards_of]
    rows_ref, hid_ref, gg_ref, gu_ref, out0_ref, out1_ref, held, slot, acc, sems = rest[shards_of:]
    expert = pl.program_id(0)
    hidden = gh_ref.shape[2]
    width = x0_ref.shape[1]
    fetch_weights(shards, order_ref[0], (0, 1), held, sems)
    for side, (ref, p_ref) in enumerate(((x0_ref, p0_ref), (x1_ref, p1_ref))):
        span = slice(side * capacity, (side + 1) * capacity)
        rows_ref[0, span] = mm(p_ref[0], ref[...]).astype(BF)
    rows = rows_ref[0]
    tile = 256
    for start in range(0, hidden, tile):
        span = slice(start, start + tile)
        gate = mm(rows, held[0, expert, :, span])
        up = mm(rows, held[1, expert, :, span])
        grad = gh_ref[0, :, span]
        sigma = 1.0 / (1.0 + jnp.exp(-gate))
        active = gate * sigma
        hid_ref[0, :, span] = (active * up).astype(BF)
        gg_ref[0, :, span] = (grad * up * (sigma * (1.0 + gate * (1.0 - sigma)))).astype(BF)
        gu_ref[0, :, span] = (grad * active).astype(BF)
    tile = 512
    for start in range(0, width, tile):
        span = slice(start, start + tile)
        slot[:, span] = (
            mm(gg_ref[0], held[0, expert, span, :], NT)
            + mm(gu_ref[0], held[1, expert, span, :], NT)
        ).astype(BF)
    for side, (p_ref, out_ref) in enumerate(((p0_ref, out0_ref), (p1_ref, out1_ref))):
        span = slice(side * capacity, (side + 1) * capacity)
        term = mm(p_ref[0], slot[span], TN)

        @pl.when(expert == 0)
        def _():
            acc[side] = term

        @pl.when(expert > 0)
        def _():
            acc[side] += term

        @pl.when(expert == pl.num_programs(0) - 1)
        def _():
            out_ref[...] = acc[side].astype(BF)


def expert_call(order, xs, picks, grad_hidden, shards, capacity, after=()):
    tokens, width = xs[0].shape
    _, experts, size, hidden = shards[0].shape
    rows = 2 * capacity
    by_expert = lambda e, _: (e, 0, 0)
    fixed = lambda e, _: (0, 0)
    grid = pltpu.PrefetchScalarGridSpec(
        num_scalar_prefetch=1,
        grid=(experts,),
        in_specs=[pl.BlockSpec((tokens, width), fixed)] * 2
        + [pl.BlockSpec((1, capacity, tokens), by_expert)] * 2
        + [pl.BlockSpec((1, rows, hidden), by_expert)]
        + [ANY] * (len(shards) + len(after)),
        out_specs=[pl.BlockSpec((1, rows, width), by_expert)]
        + [pl.BlockSpec((1, rows, hidden), by_expert)] * 3
        + [pl.BlockSpec((tokens, width), fixed)] * 2,
        scratch_shapes=[
            pltpu.VMEM((2, experts, width, hidden), BF),
            pltpu.VMEM((rows, width), BF),
            pltpu.VMEM((2, tokens, width), F32),
            pltpu.SemaphoreType.DMA((2, experts, len(shards))),
        ],
    )
    return pl.pallas_call(
        without(
            lambda *refs: expert_kernel(len(shards), capacity, *refs), 6 + len(shards), len(after)
        ),
        name="experts",
        grid_spec=grid,
        out_shape=[sds((experts, rows, width), BF)]
        + [sds((experts, rows, hidden), BF)] * 3
        + [sds((tokens, width), BF)] * 2,
        compiler_params=params(1),
        cost_estimate=busy(17),
    )(order, *xs, *picks, grad_hidden, *shards, *after)


def down_kernel(shards_of, capacity, place, order_ref, hid_ref, gate_ref, p0_ref, p1_ref, *rest):
    shards = rest[:shards_of]
    out_ref, pair_ref, held, slot, acc, packed, sems, out_sem = rest[-8:]
    expert = pl.program_id(0)
    width = out_ref.shape[1]
    fetch_weights(shards, order_ref[0], (2,), held, sems)
    tile = 512
    for start in range(0, width, tile):
        span = slice(start, start + tile)
        made = mm(hid_ref[0], held[0, expert, span, :], NT).astype(BF).astype(F32)
        slot[:, span] = (made * gate_ref[0, :, 0:1]).astype(BF)
    for side, p_ref in enumerate((p0_ref, p1_ref)):
        span = slice(side * capacity, (side + 1) * capacity)
        term = mm(p_ref[0], slot[span], TN)

        @pl.when(expert == 0)
        def _():
            acc[side] = term

        @pl.when(expert > 0)
        def _():
            acc[side] += term

    @pl.when(expert == pl.num_programs(0) - 1)
    def _():
        packed[...] = acc[1].astype(BF)
        copy = pltpu.make_async_copy(packed, pair_ref.at[place], out_sem)
        copy.start()
        out_ref[...] = acc[0].astype(BF)
        copy.wait()


def down_call(order, hid, gates, picks, shards, capacity, width, place, pair, total, after=()):
    tokens = picks[0].shape[2]
    _, experts, size, hidden = shards[0].shape
    rows = 2 * capacity
    by_expert = lambda e, _: (e, 0, 0)
    pair = [] if pair is None else [pair]
    grid = pltpu.PrefetchScalarGridSpec(
        num_scalar_prefetch=1,
        grid=(experts,),
        in_specs=[
            pl.BlockSpec((1, rows, hidden), by_expert),
            pl.BlockSpec((1, rows, LANES), by_expert),
        ]
        + [pl.BlockSpec((1, capacity, tokens), by_expert)] * 2
        + [ANY] * (len(shards) + len(pair) + len(after)),
        out_specs=[whole((tokens, width)), ANY],
        scratch_shapes=[
            pltpu.VMEM((1, experts, width, hidden), BF),
            pltpu.VMEM((rows, width), BF),
            pltpu.VMEM((2, tokens, width), F32),
            pltpu.VMEM((tokens, width), BF),
            pltpu.SemaphoreType.DMA((1, experts, len(shards))),
            pltpu.SemaphoreType.DMA,
        ],
    )
    return pl.pallas_call(
        lambda *refs: down_kernel(len(shards), capacity, place, *refs),
        name="experts_down",
        grid_spec=grid,
        out_shape=[sds((tokens, width), BF), sds((total, tokens, width), BF)],
        input_output_aliases={5 + len(shards): 1} if pair else {},
        compiler_params=params(1),
        cost_estimate=busy(9.3),
    )(order, hid, gates, *picks, *shards, *pair, *after)


def weight_grad_kernel(chunks, *rest):
    xs, gs = rest[:chunks], rest[chunks : 2 * chunks]
    ggs, gus = rest[2 * chunks : 3 * chunks], rest[3 * chunks : 4 * chunks]
    hids = rest[4 * chunks : 5 * chunks]
    out_ref, left, rights = rest[5 * chunks :]
    rows = xs[0].shape[1]

    @pl.when(pl.program_id(0) == 0)
    def _():
        for kind, group in enumerate((ggs, gus, hids)):
            for place, ref in enumerate(group):
                rights[kind, place * rows : (place + 1) * rows] = ref[0]

    for kind, group in ((0, xs), (2, gs)):
        for place, ref in enumerate(group):
            left[place * rows : (place + 1) * rows] = ref[0]
        out_ref[kind] = mm(left[...], rights[kind], TN).astype(BF)
        if kind == 0:
            out_ref[1] = mm(left[...], rights[1], TN).astype(BF)


def weight_grad_call(expert, xs, gs, ggs, gus, hids, after=()):
    chunks = len(xs)
    _, rows, width = xs[0].shape
    hidden = ggs[0].shape[2]
    tile = 256
    return pl.pallas_call(
        without(lambda *refs: weight_grad_kernel(chunks, *refs), 5 * chunks, len(after)),
        name="expert_weight_grads",
        grid=(width // tile,),
        in_specs=[pl.BlockSpec((1, rows, tile), lambda i: (expert, 0, i))] * (2 * chunks)
        + [pl.BlockSpec((1, rows, hidden), lambda i: (expert, 0, 0))] * (3 * chunks)
        + [ANY] * len(after),
        out_specs=pl.BlockSpec((3, tile, hidden), lambda i: (0, i, 0)),
        out_shape=sds((3, width, hidden), BF),
        scratch_shapes=[
            pltpu.VMEM((chunks * rows, tile), BF),
            pltpu.VMEM((3, chunks * rows, hidden), BF),
        ],
        compiler_params=params(1),
        cost_estimate=busy(18),
    )(*xs, *gs, *ggs, *gus, *hids, *after)


def resid_back_kernel(
    terms, x_ref, rows_ref, dy_ref, gain_ref, att_ref, *rest
):
    w_refs, rest = rest[: HQ // 512], rest[HQ // 512 :]
    parts = rest[:terms]
    resid_ref, attn_ref, do_ref, delta_ref, gain_out, deltas = rest[terms:]
    step = pl.program_id(0)
    grad = parts[0][...].astype(F32)
    for part in parts[1:]:
        grad += part[...].astype(F32)
    resid = x_ref[...].astype(F32) + rows_ref[...].astype(F32)
    scale = lax.rsqrt(jnp.mean(resid * resid, -1, keepdims=True) + EPS)
    normed = resid * scale
    product = grad * normed
    partial = jnp.sum(product, 0, keepdims=True)

    @pl.when(step == 0)
    def _():
        gain_out[...] = jnp.broadcast_to(partial, gain_out.shape)

    @pl.when(step > 0)
    def _():
        gain_out[...] += partial

    gain = gain_ref[1:2]
    mean = jnp.mean(product * gain, -1, keepdims=True)
    total = dy_ref[...].astype(F32) + scale * (grad * gain - normed * mean)
    resid_ref[...] = total
    low = total.astype(BF)
    attn_ref[...] = low
    for place, w_ref in enumerate(w_refs):
        do_ref[:, place * 512 : (place + 1) * 512] = mm(low, w_ref[...]).astype(BF)
    each = do_ref[...].astype(F32) * att_ref[...].astype(F32)
    lanes = lax.broadcasted_iota(jnp.int32, deltas.shape, 1)
    made = jnp.zeros(deltas.shape, F32)
    for head in range(HEADS):
        value = jnp.sum(each[:, head * HEAD : (head + 1) * HEAD], -1, keepdims=True)
        made = jnp.where(lanes == head, value, made)
    deltas[...] = made
    turned = jnp.transpose(deltas[...])
    for head in range(HEADS):
        delta_ref[head // COUPLE, head % COUPLE : head % COUPLE + 1] = turned[head : head + 1]


def resid_back_call(x, rows, dy, gains, wo_t, attended, parts, after=()):
    tokens, width = x.shape
    tile = 128
    by_row = lambda i: (i, 0)
    return pl.pallas_call(
        without(
            lambda *refs: resid_back_kernel(len(parts), *refs),
            5 + HQ // 512 + len(parts),
            len(after),
        ),
        name="resid_back",
        grid=(tokens // tile,),
        in_specs=[pl.BlockSpec((tile, width), by_row)] * 3
        + [whole((8, width)), pl.BlockSpec((tile, HQ), by_row)]
        + wo_specs(width)
        + [pl.BlockSpec((tile, width), by_row)] * len(parts)
        + [ANY] * len(after),
        out_specs=[pl.BlockSpec((tile, width), by_row)] * 2
        + [
            pl.BlockSpec((tile, HQ), by_row),
            pl.BlockSpec((COUPLES, 8, tile), lambda i: (0, 0, i)),
            whole((8, width)),
        ],
        out_shape=[
            sds((tokens, width), F32),
            sds((tokens, width), BF),
            sds((tokens, HQ), BF),
            sds((COUPLES, 8, tokens), F32),
            sds((8, width), F32),
        ],
        scratch_shapes=[pltpu.VMEM((tile, LANES), F32)],
        compiler_params=params(1),
        cost_estimate=busy(10.5),
    )(x, rows, dy, gains, attended, *[wo_t] * (HQ // 512), *parts, *after)


def block_copies(order_ref, source, near, far, sems):
    shards_of, sides, steps, rows, _ = near.shape
    shards_of = 2 * shards_of
    copies = []
    for slot in range(shards_of):
        for place in range(sides * steps):
            block = order_ref[2 + place] * shards_of + (order_ref[0] ^ slot)
            target = far if slot % 2 else near
            copies.append(
                pltpu.make_async_copy(
                    source.at[pl.ds(pl.multiple_of(block * rows, 16), rows)],
                    target.at[slot // 2, place % 2, place // 2],
                    sems.at[slot * sides * steps + place],
                )
            )
    return copies


def cross_kernel(order_ref, left_ref, right_ref, near, far, made, sems):
    step = pl.program_id(0)
    tile = left_ref.shape[1]
    made[pl.ds(pl.multiple_of(step * tile, tile), tile)] = mm(
        left_ref[...], right_ref[...], TN
    ).astype(BF)

    @pl.when(step == pl.num_programs(0) - 1)
    def _():
        copies = block_copies(order_ref, made, near, far, sems)
        for copy in copies:
            copy.start()
        for copy in copies:
            copy.wait()


def blocks_shape(count, shards_of, rows, columns):
    return (shards_of // 2, 2, count // 2, rows // (count * shards_of), columns)


def cross_call(order, left, right, count, shards_of, name):
    tokens, rows = left.shape
    columns = right.shape[1]
    tile = 512
    grid = pltpu.PrefetchScalarGridSpec(
        num_scalar_prefetch=1,
        grid=(rows // tile,),
        in_specs=[
            pl.BlockSpec((tokens, tile), lambda i, _: (0, i)),
            pl.BlockSpec((tokens, columns), lambda i, _: (0, 0)),
        ],
        out_specs=[ANY] * 2,
        scratch_shapes=[
            pltpu.VMEM((rows, columns), BF),
            pltpu.SemaphoreType.DMA((count * shards_of,)),
        ],
    )
    return pl.pallas_call(
        cross_kernel,
        name=name,
        grid_spec=grid,
        out_shape=[sds(blocks_shape(count, shards_of, rows, columns), BF)] * 2,
        compiler_params=params(1),
        cost_estimate=busy(7.5),
    )(order, left, right)


def plain_cross_kernel(left_ref, right_ref, out_ref):
    out_ref[...] = mm(left_ref[...], right_ref[...], TN).astype(out_ref.dtype)


def plain_cross_call(left, right, name):
    tokens, rows = left.shape
    columns = right.shape[1]
    tile = 512
    return pl.pallas_call(
        plain_cross_kernel,
        name=name,
        grid=(rows // tile,),
        in_specs=[pl.BlockSpec((tokens, tile), lambda i: (0, i)), whole((tokens, columns))],
        out_specs=pl.BlockSpec((tile, columns), lambda i: (i, 0)),
        out_shape=sds((rows, columns), BF),
        compiler_params=params(1),
        cost_estimate=busy(7.5),
    )(left, right)


def input_q_kernel(dq_ref, w_ref, out_ref):
    out_ref[...] = mm(dq_ref[...], w_ref[...], NT)


def input_q_call(d_q, w_full):
    tokens = d_q.shape[0]
    width = w_full.shape[0]
    tile = 512
    return pl.pallas_call(
        input_q_kernel,
        name="input_grad_q",
        grid=(width // tile,),
        in_specs=[whole((tokens, HQ)), pl.BlockSpec((tile, HQ), lambda i: (i, 0))],
        out_specs=pl.BlockSpec((tokens, tile), lambda i: (0, i)),
        out_shape=sds((tokens, width), F32),
        compiler_params=params(1),
        cost_estimate=busy(6),
    )(d_q, w_full)


def final_kernel(
    terms,
    order_ref,
    x_ref,
    low_ref,
    resid_ref,
    gq_ref,
    gain_ref,
    moe_ref,
    w_ref,
    cos_ref,
    sin_ref,
    *rest,
):
    parts = rest[:terms]
    grad_ref = rest[terms]
    outs = rest[terms + 1 : -2]
    made, sems = rest[-2:]
    scale_k = HEAD ** (-0.5)
    cosine, sine = cos_ref[...], -sin_ref[...]
    key_grads, value_grads = [], []
    for group in range(KV_HEADS):
        span = slice(group * 2 * HEAD, (group + 1) * 2 * HEAD)
        total = parts[0][:, span].astype(F32)
        for part in parts[1:]:
            total += part[:, span].astype(F32)
        key_grads.append(turn(total[:, 0:HEAD] * scale_k, cosine, sine).astype(BF))
        value_grads.append(total[:, HEAD:].astype(BF))
    low = jnp.concatenate(key_grads + value_grads, 1)
    made[:, 0 : 2 * KVW] = mm(low_ref[...], low, TN).astype(BF)
    wide = x_ref[...].astype(F32)
    scale = lax.rsqrt(jnp.mean(wide * wide, -1, keepdims=True) + EPS)
    normed = wide * scale
    grad = gq_ref[...] + mm(low, w_ref[...], NT)
    product = grad * normed
    gain_part = jnp.sum(product, 0, keepdims=True)
    width = x_ref.shape[1]
    lines = lax.broadcasted_iota(jnp.int32, (LANES, width), 0)
    both = jnp.where(lines == 0, gain_part, jnp.where(lines == 1, moe_ref[0:1], 0.0))
    made[:, 2 * KVW :] = jnp.transpose(both).astype(BF)
    if len(outs) == 2:
        copies = block_copies(order_ref, made, *outs, sems)
    else:
        copies = [pltpu.make_async_copy(made, outs[0], sems.at[0])]
    for copy in copies:
        copy.start()
    gain = gain_ref[0:1]
    mean = jnp.mean(product * gain, -1, keepdims=True)
    own = (scale * (grad * gain - normed * mean)).astype(BF)
    grad_ref[...] = (resid_ref[...] + own.astype(F32)).astype(BF)
    for copy in copies:
        copy.wait()


def final_call(
    order, x, low, resid, grad_q, gains, moe_part, w_full, cosine, sine, parts, layout, after=()
):
    tokens, width = x.shape
    columns = 2 * KVW + LANES
    if layout:
        outs = [sds(blocks_shape(*layout, width, columns), BF)] * 2
    else:
        outs = [sds((width, columns), BF)]
    grid = pltpu.PrefetchScalarGridSpec(
        num_scalar_prefetch=1,
        grid=(1,),
        in_specs=[whole((tokens, width))] * 4
        + [whole((8, width))] * 2
        + [pl.BlockSpec((width, 2 * KVW), lambda i, _: (0, HQ // (2 * KVW)))]
        + [whole((tokens, HEAD))] * 2
        + [whole((tokens, 2 * KVW))] * len(parts)
        + [ANY] * len(after),
        out_specs=[whole((tokens, width))] + [ANY] * len(outs),
        scratch_shapes=[
            pltpu.VMEM((width, columns), BF),
            pltpu.SemaphoreType.DMA((layout[0] * layout[1] if layout else 1,)),
        ],
    )
    return pl.pallas_call(
        without(lambda *refs: final_kernel(len(parts), *refs), 10 + len(parts), len(after)),
        name="final",
        grid_spec=grid,
        out_shape=[sds((tokens, width), BF)] + outs,
        compiler_params=params(1),
        cost_estimate=busy(10),
    )(order, x, low, resid, grad_q, gains, moe_part, w_full, cosine, sine, *parts, *after)


def hold_kernel(count, *refs):
    del count, refs


def hold(arrays, *until):
    until = [array for array in until if array is not None]
    if not until:
        return arrays
    count = len(arrays)
    return pl.pallas_call(
        lambda *refs: hold_kernel(count, *refs),
        name="hold",
        in_specs=[ANY] * (count + len(until)),
        out_specs=[ANY] * count,
        out_shape=[sds(array.shape, array.dtype) for array in arrays],
        input_output_aliases={place: place for place in range(count)},
        cost_estimate=busy(0.5),
    )(*arrays, *until)


def local(
    layer_input,
    lengths,
    expert_ids,
    gate_weights,
    attn_gain,
    wq,
    wk,
    wv,
    wo,
    moe_gain,
    w_gate,
    w_up,
    w_down,
    cotangent,
):
    count = lax.axis_size("ctx")
    shards_of = lax.axis_size("fsdp")
    both = ("ctx", "fsdp")
    ring = Ring(count)
    me = lax.axis_index("ctx").astype(jnp.int32)
    own = lax.axis_index("fsdp").astype(jnp.int32)
    x = layer_input[0]
    dy = cotangent[0]
    tokens, width = x.shape
    exp_dev = w_gate.shape[0]
    experts = exp_dev * count
    capacity = 3 * tokens * TOPK // (2 * experts)

    sources = ring.sources()
    places = jnp.concatenate([jnp.stack([own, me]), sources])
    layout = (count, shards_of) if ring.length == 4 and shards_of == 4 else None
    rows = wq.shape[0]
    gains_part = jnp.concatenate(
        [attn_gain[:, None], moe_gain[:, None], jnp.zeros((rows, LANES - 2), BF)], 1
    )
    w_full = lax.all_gather(
        jnp.concatenate([wq, wk, wv, wo.T, gains_part], 1), both, axis=0, tiled=True
    )

    gates = gate_weights[0]
    gate_high = gates.astype(BF)
    rest = gates - gate_high.astype(F32)
    gate_mid = rest.astype(BF)
    gate_low = (rest - gate_mid.astype(F32)).astype(BF)
    info = jnp.concatenate(
        [
            dy,
            expert_ids[0].astype(BF),
            gate_high,
            gate_mid,
            gate_low,
            jnp.zeros((tokens, LANES - 4 * TOPK), BF),
        ],
        1,
    )
    ends = jnp.cumsum(lengths[0])
    index = me * tokens + jnp.arange(tokens, dtype=jnp.int32)
    after = (index[:, None] >= ends[None, :]).astype(jnp.int32)
    start = jnp.sum(after * lengths[0][None, :], 1)
    half = HEAD // 2
    freq = jnp.exp(jnp.arange(half, dtype=F32) * (-2.0 * math.log(ROPE_BASE) / HEAD))
    angle = (index - start).astype(F32)[:, None] * freq[None, :]
    cosine = jnp.cos(angle)
    sine = jnp.sin(angle)
    cosine = jnp.concatenate([cosine, cosine], 1)
    sine = jnp.concatenate([-sine, sine], 1)
    order = jnp.concatenate(
        [me[None], (start[0] // tokens)[None], ends[: HEADER - 2], sources]
    )

    run = ring.gather(info)
    next(run)
    grads = [run.send(None), run.send(None)]
    q, kv, low_one, gains = qkv_call(
        x, w_full, cosine, sine, [grads[1][1]] if layout else []
    )
    shards = gather_shards(
        jnp.stack([w_gate, w_up, jnp.swapaxes(w_down, 1, 2)]), shards_of, grads[1][1]
    )
    kv_couples = ring.gather_now(kv)
    kv_slots = [part for couple in kv_couples for part in couple]
    half = count // 2
    parts, made, routed = [], [], []

    def route(step, after=()):
        routed.append(route_call(places, grads[step], shards, capacity, width, after))
        return routed[-1][4]

    grads.append(run.send(kv_couples[3][1]))
    state = attn_call(order, q, kv_slots[:half], 0, False, after=[route(0)])
    grads += [run.send(state[1]) for _ in range(3, half)]
    attended, log_total = attn_call(
        order, q, kv_slots[half:], half, True, state, [grads[3][0]]
    )
    attn_rows, low_two = out_call(x, attended, w_full, gains, [grads[3][1]])

    def run_experts(step, couple, after):
        pick0, pick1, _, _, grad_hidden = routed[step]
        found = expert_call(
            places, couple, (pick0, pick1), grad_hidden, shards, capacity, after
        )
        made.append(found[:4])
        parts.append((found[4], found[5]))
        return found[4]

    rows_run = ring.gather(low_two)
    next(rows_run)
    mark = route(2, [route(1)])
    couple = rows_run.send(mark)
    mark = run_experts(0, couple, [mark])
    couple = rows_run.send(mark)
    mark = run_experts(1, couple, [mark])
    for step in range(3, half):
        mark = route(step, [mark])
    couple = rows_run.send(None)
    couples = [couple] + [rows_run.send(mark) for _ in range(3, half)]
    for step in range(2, half):
        mark = run_experts(step, couples[step - 2], [mark, couples[1][0]])

    y_pairs = []

    def down(step, after):
        pick0, pick1, gate_rows = routed[step][:3]
        packed = step < half // 2
        place = half // 2 - 1 - step if packed else 0
        out, pair = down_call(
            places,
            made[step][1],
            gate_rows,
            (pick0, pick1),
            shards,
            capacity,
            width,
            place,
            y_pairs.pop() if place else None,
            half // 2 if packed else 1,
            after,
        )
        y_pairs.append(pair)
        return out

    grad_run = ring.scatter(parts, True)
    grad_mark = next(grad_run)
    expert_grads = []
    for expert in range(exp_dev):
        made_grad = weight_grad_call(
            expert,
            [entry[0] for entry in made],
            [entry[3] for entry in routed],
            [entry[2] for entry in made],
            [entry[3] for entry in made],
            [entry[1] for entry in made],
            [mark, grad_mark],
        )
        mark = made_grad
        if expert < 2:
            grad_mark = grad_run.send(mark)
        expert_grads.append(
            lax.psum_scatter(
                hold([made_grad], grad_mark)[0], "fsdp", scatter_dimension=1, tiled=True
            )
        )
    y_parts = [None] * len(made)
    for step in reversed(range(len(made))):
        y_parts[step] = down(step, [mark, grad_mark])
        mark = y_parts[step]
        if step == len(made) // 2:
            grad_mark = grad_run.send(mark)
    grad_parts = grad_run.send(mark)
    y_run = ring.scatter_late(y_parts, hold(y_pairs, grad_mark))
    next(y_run)

    resid, grad_attn, grad_out, delta, moe_part = resid_back_call(
        x, attn_rows, dy, gains, w_full, attended, grad_parts
    )
    back = attn_back_call(
        0, order, q, grad_out, log_total, delta, cosine, sine, kv_slots
    )
    d_q = [back[0]]
    mark = y_run.send(back[0])
    back = attn_back_call(
        1,
        order,
        q,
        grad_out,
        log_total,
        delta,
        cosine,
        sine,
        kv_slots,
        back[1:],
        [mark] + expert_grads,
    )
    d_q.append(back[0])
    expert_grads = jnp.stack(expert_grads, 1).astype(F32)
    d_q = jnp.concatenate(d_q, 1)
    waits = [y_run.send(back[0])]
    if layout:
        wo_part = cross_call(places, hold([grad_attn], back[0])[0], attended, *layout, "wo_grad")
        wq_part = cross_call(places, low_one, d_q, *layout, "wq_grad")
        waits += [wo_part[0], wq_part[0]]
    kv_parts = hold(back[1:], *waits)
    kv_run = ring.scatter([(kv_parts[2 * step], kv_parts[2 * step + 1]) for step in range(half)])
    next(kv_run)
    for _ in range(4):
        kv_terms = kv_run.send(None)
    y_run.send(kv_terms[-1])

    grad_q = input_q_call(d_q, w_full)
    after = []
    if layout:
        wo_terms, wo_sent = scatter_all_across(*wo_part, shards_of)
        wq_terms, wq_sent = scatter_all_across(*wq_part, shards_of)
        after = [wo_terms, wq_sent]
    else:
        wq_grad, wo_grad = [
            lax.psum_scatter(
                plain_cross_call(left, right, name), both, scatter_dimension=0, tiled=True
            ).astype(F32)
            for left, right, name in (
                (low_one, d_q, "wq_grad"),
                (grad_attn, attended, "wo_grad"),
            )
        ]
    input_grad, *tail = final_call(
        places,
        x,
        low_one,
        resid,
        grad_q,
        gains,
        moe_part,
        w_full,
        cosine,
        sine,
        kv_terms,
        layout,
        after,
    )
    if layout:
        wo_terms = hold([wo_terms], kv_terms[-1])[0]
        tail, _ = scatter_all_across(*tail, shards_of)
        runs = [scatter_all_along(terms, ring) for terms in (wo_terms, wq_terms, tail)]
        for one in runs:
            next(one)
        for _ in range(4):
            wo_grad, wq_grad, tail = [one.send(None) for one in runs]
    else:
        tail = lax.psum_scatter(tail[0], both, scatter_dimension=0, tiled=True).astype(F32)
    y_terms = y_run.send(None)
    moe = y_terms[0].astype(F32)
    for term in y_terms[1:]:
        moe = moe + term.astype(F32)
    output = (x.astype(F32) + attn_rows.astype(F32) + moe).astype(BF)
    return (
        output[None],
        input_grad[None],
        tail[:, 2 * KVW],
        wq_grad,
        tail[:, 0:KVW],
        tail[:, KVW : 2 * KVW],
        wo_grad.T,
        tail[:, 2 * KVW + 1],
        expert_grads[0],
        expert_grads[1],
        jnp.swapaxes(expert_grads[2], 1, 2),
    )


def solution(mesh):
    return jax.shard_map(
        local,
        mesh=mesh,
        in_specs=(
            P("fsdp", "ctx", None),
            P("fsdp", None),
            P("fsdp", "ctx", None),
            P("fsdp", "ctx", None),
            P(("ctx", "fsdp")),
            P(("ctx", "fsdp"), None),
            P(("ctx", "fsdp"), None),
            P(("ctx", "fsdp"), None),
            P(None, ("ctx", "fsdp")),
            P(("ctx", "fsdp")),
            P("ctx", "fsdp", None),
            P("ctx", "fsdp", None),
            P("ctx", None, "fsdp"),
            P("fsdp", "ctx", None),
        ),
        out_specs=(
            P("fsdp", "ctx", None),
            P("fsdp", "ctx", None),
            P(("ctx", "fsdp")),
            P(("ctx", "fsdp"), None),
            P(("ctx", "fsdp"), None),
            P(("ctx", "fsdp"), None),
            P(None, ("ctx", "fsdp")),
            P(("ctx", "fsdp")),
            P("ctx", "fsdp", None),
            P("ctx", "fsdp", None),
            P("ctx", None, "fsdp"),
        ),
        check_vma=False,
    )
```

```python
import math

import jax
import jax.numpy as jnp
from jax import lax
from jax.experimental import pallas as pl
from jax.experimental.pallas import tpu as pltpu
from jax.sharding import PartitionSpec as P

HEADS = 12
KV_HEADS = 2
HEAD = 128
TOPK = 4
REPEAT = HEADS // KV_HEADS
HQ = HEADS * HEAD
KVW = KV_HEADS * HEAD
LANES = 128

EPS = 1e-06
ROPE_BASE = 10000.0
NEG = -1e30
BF = jnp.bfloat16
F32 = jnp.float32
NN = ((1,), (0,))
NT = ((1,), (1,))
TN = ((0,), (0,))
ANY = pl.BlockSpec(memory_space=pl.ANY)
MIB = 1024 * 1024
SCALE = 0.4


def mm(left, right, dims=NN):
    return lax.dot_general(left, right, (dims, ((), ())), preferred_element_type=F32)


def params(grid_rank, limit=56):
    return pltpu.CompilerParams(
        dimension_semantics=("arbitrary",) * grid_rank, vmem_limit_bytes=limit * MIB
    )


def busy(microseconds):
    return pl.CostEstimate(
        flops=int(microseconds * SCALE * 1.15e9), bytes_accessed=1024, transcendentals=0
    )


def sds(shape, dtype):
    return jax.ShapeDtypeStruct(shape, dtype)


def whole(shape):
    return pl.BlockSpec(shape, lambda *_: (0,) * len(shape))


def without(kernel, place, extra):
    def run(*refs):
        kernel(*refs[:place], *refs[place + extra :])

    return run


class Ring:
    def __init__(self, count):
        self.count = count
        self.low_pair = count == 8
        self.length = count // 2
        self.me = lax.axis_index("ctx")
        if self.low_pair:
            self.line, self.pair = self.me // 2, self.me % 2
        else:
            self.line, self.pair = self.me % self.length, self.me // self.length
        if self.length == 4:
            self.table = [[0, 1, 2, 3], [1, 0, 2, 3], [2, 3, 1, 0], [3, 2, 1, 0]]
        else:
            self.table = [
                [(place + step) % self.length for step in range(self.length)]
                for place in range(self.length)
            ]

    def index(self, line, pair):
        return line * 2 + pair if self.low_pair else pair * self.length + line

    def move(self, array, hops):
        pairs = [
            (self.index(source, side), self.index(target, side))
            for source, target in hops
            for side in (0, 1)
        ]
        return lax.ppermute(array, "ctx", pairs)

    def swap(self, array):
        pairs = [
            (self.index(place, side), self.index(place, 1 - side))
            for place in range(self.length)
            for side in (0, 1)
        ]
        return lax.ppermute(array, "ctx", pairs)

    def sources(self):
        line = jnp.asarray(self.table, jnp.int32)[self.line]
        side = jnp.stack([self.pair, 1 - self.pair]).astype(jnp.int32)
        return self.index(line[:, None], side[None, :]).reshape(-1).astype(jnp.int32)

    def spread(self, array):
        everything = lax.all_gather(array, "ctx", axis=0)
        order = self.sources()
        rows = [
            lax.dynamic_index_in_dim(everything, order[slot], 0, keepdims=False)
            for slot in range(self.count)
        ]
        return [(rows[2 * step], rows[2 * step + 1]) for step in range(self.length)]

    def gather(self, array):
        if self.length != 4:
            yield
            for couple in self.spread(array):
                yield couple
            return
        ends = [(1, 0), (2, 3)]
        middle = [(1, 2), (2, 1)]
        couples = [(0, 1), (1, 0), (2, 3), (3, 2)]
        first = self.move(array, couples)
        cross = self.move(array, middle)
        swapped = self.swap(array)
        until = yield
        first, cross = hold([first, cross], until, swapped)
        swapped = hold([swapped], cross)[0]
        outward = self.move(cross, ends)
        cross_two = self.move(first, middle)
        swapped_first = self.swap(first)
        until = yield (array, swapped)
        outward, cross_two = hold([outward, cross_two], until, swapped_first)
        second = cross + outward
        swapped_first = hold([swapped_first], second)[0]
        until = yield (first, swapped_first)
        cross_two, second = hold([cross_two, second], until)
        outward_two = self.move(cross_two, ends)
        swapped_second = self.swap(second)
        until = yield (second, swapped_second)
        outward_two = hold([outward_two], until, swapped_second)[0]
        third = cross_two + outward_two
        yield (third, self.swap(third))

    def gather_now(self, array):
        run = self.gather(array)
        next(run)
        return [run.send(None) for _ in range(self.length)]

    def scatter(self, parts, chained=False):
        if self.length != 4:
            order = self.sources()
            rows = jnp.stack([part for couple in parts for part in couple])
            placed = jnp.zeros_like(rows).at[order].set(rows)
            total = lax.psum_scatter(placed, "ctx", scatter_dimension=0, tiled=False)
            for _ in range(4):
                yield total
            yield [total]
            return
        inward = [(0, 1), (3, 2)]
        middle = [(1, 2), (2, 1)]
        couples = [(0, 1), (1, 0), (2, 3), (3, 2)]

        others = [part[1] for part in parts]
        if chained:
            others[:3] = hold(others[:3], others[3])
        swapped = [self.swap(other) for other in others]
        until = yield parts[3][1]
        arrived = hold([swapped[3]], until)[0]
        third = parts[3][0] + arrived
        from_end = self.move(third, inward)
        arrived = swapped[2]
        until = yield third
        from_end, arrived = hold([from_end, arrived], until)
        sent = third + from_end
        crossed = self.move(sent, middle)
        second = parts[2][0] + arrived
        from_end_two = self.move(second, inward)
        arrived = swapped[1]
        until = yield second
        crossed, from_end_two, arrived = hold([crossed, from_end_two, arrived], until)
        sent = parts[1][0] + arrived + crossed
        last = self.move(sent, couples)
        crossed_two = self.move(second + from_end_two, middle)
        arrived = swapped[0]
        until = yield sent
        last, crossed_two, arrived = hold([last, crossed_two, arrived], until)
        yield [parts[0][0], arrived, crossed_two, last]

    def scatter_late(self, parts, others):
        if self.length != 4:
            flat = [other[place] for other in others for place in range(other.shape[0])]
            yield from self.scatter(list(zip(parts, reversed(flat))))
            return
        inward = [(0, 1), (3, 2)]
        middle = [(1, 2), (2, 1)]
        couples = [(0, 1), (1, 0), (2, 3), (3, 2)]
        swapped = [self.swap(other) for other in others]
        until = yield others[0]
        third = parts[3] + hold([swapped[0]], until)[0][0]
        from_end = self.move(third, inward)
        until = yield third
        from_end, *swapped = hold([from_end, *swapped[1:]], until)
        until = yield from_end
        third, *swapped = hold([third, *swapped], until)
        crossed = self.move(third + from_end, middle)
        second = parts[2] + swapped[0][0]
        from_end_two = self.move(second, inward)
        until = yield second
        crossed, from_end_two = hold([crossed, from_end_two], until)
        last = self.move(parts[1] + swapped[1][0] + crossed, couples)
        crossed_two = self.move(second + from_end_two, middle)
        yield [parts[0], swapped[1][1], crossed_two, last]

    def scatter_now(self, parts):
        run = self.scatter(parts)
        next(run)
        made = [run.send(None) for _ in range(4)]
        return made[-1]


def neighbour(array, axis_size, bit):
    pairs = [(index, index ^ (1 << bit)) for index in range(axis_size)]
    return lax.ppermute(array, "fsdp", pairs)


def gather_shards(array, axis_size, until=None):
    slots = {0: array}
    bits = axis_size.bit_length() - 1
    for bit in reversed(range(bits)):
        for slot in list(slots):
            taken = slots[slot]
            if slot and bit == 0 and until is not None:
                taken = slots[slot] = hold([taken], until)[0]
            slots[slot | (1 << bit)] = neighbour(taken, axis_size, bit)
    return [slots[slot] for slot in range(axis_size)]


def scatter_all_across(near, far, axis_size):
    arrived = neighbour(far, axis_size, 0)
    sent = near[1] + arrived[1]
    return near[0] + arrived[0] + neighbour(sent, axis_size, 1), sent


def scatter_all_along(terms, ring):
    swapped = ring.swap(terms[1])
    swapped = hold([swapped], (yield))[0]
    lines = terms[0] + swapped
    ends = ring.move(lines[2:4], [(0, 1), (3, 2)])
    ends = hold([ends], (yield))[0]
    middle = ring.move(lines[2:4] + ends, [(1, 2), (2, 1)])
    middle = hold([middle], (yield))[0]
    last = ring.move(lines[1] + middle[1], [(0, 1), (1, 0), (2, 3), (3, 2)])
    last = hold([last], (yield))[0]
    yield lines[0].astype(F32) + middle[0].astype(F32) + last.astype(F32)


def turn(values, cosine, sine):
    return values * cosine + pltpu.roll(values, HEAD // 2, 1) * sine


def qkv_kernel(x_ref, w_ref, g_ref, cos_ref, sin_ref, q_ref, kv_ref, low_ref, gain_ref):
    step = pl.program_id(0)
    blocks = HQ // 512

    @pl.when(step == 0)
    def _():
        gains = jnp.transpose(g_ref[...].astype(F32))
        gain_ref[...] = gains[0:8]
        wide = x_ref[...].astype(F32)
        scale = lax.rsqrt(jnp.mean(wide * wide, -1, keepdims=True) + EPS)
        low_ref[...] = (wide * scale * gains[0:1]).astype(BF)

    raw = mm(low_ref[...], w_ref[...])
    cosine, sine = cos_ref[...], sin_ref[...]

    def turned(count):
        return [
            turn(raw[:, head * HEAD : (head + 1) * HEAD], cosine, sine).astype(BF)
            for head in range(count)
        ]

    @pl.when(step < blocks)
    def _():
        for head, value in enumerate(turned(4)):
            q_ref[:, head * HEAD : (head + 1) * HEAD] = value

    @pl.when(step == blocks)
    def _():
        for head, value in enumerate(turned(KV_HEADS)):
            kv_ref[:, head * HEAD : (head + 1) * HEAD] = value
        kv_ref[:, KVW:] = raw[:, KVW:].astype(BF)


def qkv_call(x, w_full, cosine, sine, after=()):
    tokens, width = x.shape
    blocks = HQ // 512
    return pl.pallas_call(
        without(qkv_kernel, 5, len(after)),
        name="qkv",
        grid=(blocks + 1,),
        in_specs=[
            whole((tokens, width)),
            pl.BlockSpec((width, 512), lambda i: (0, i)),
            pl.BlockSpec((width, LANES), lambda i: (0, (2 * HQ + 2 * KVW) // LANES)),
            whole((tokens, HEAD)),
            whole((tokens, HEAD)),
        ]
        + [ANY] * len(after),
        out_specs=[
            pl.BlockSpec((tokens, 512), lambda i: (0, jnp.minimum(i, HQ // 512 - 1))),
            whole((tokens, 2 * KVW)),
            whole((tokens, width)),
            whole((8, width)),
        ],
        out_shape=[
            sds((tokens, HQ), BF),
            sds((tokens, 2 * KVW), BF),
            sds((tokens, width), BF),
            sds((8, width), F32),
        ],
        compiler_params=params(1),
        cost_estimate=busy(9),
    )(x, w_full, w_full, cosine, sine, *after)


HEADER = 5
SEQS = 3
COUPLE = 2
COUPLES = HEADS // COUPLE
LOG2E = math.log2(math.e)


def load_kv(slots, kv_all, sems):
    copies = [
        pltpu.make_async_copy(slot, kv_all.at[place], sems.at[place])
        for place, slot in enumerate(slots)
    ]
    for copy in copies:
        copy.start()
    for copy in copies:
        copy.wait()


def sequence_of(order_ref, index):
    ends = [order_ref[2 + place] for place in range(SEQS - 1)]
    return sum((index >= end).astype(jnp.int32) for end in ends)


def extend_queries(order_ref, q_ref, wide):
    tokens = q_ref.shape[0]
    rows = order_ref[0] * tokens + lax.broadcasted_iota(jnp.int32, (tokens, LANES), 0)
    lanes = lax.broadcasted_iota(jnp.int32, (tokens, LANES), 1)
    other = (lanes < SEQS) & (lanes != sequence_of(order_ref, rows))
    extra = jnp.where(other | (lanes > SEQS + order_ref[0]), NEG, 0.0).astype(BF)
    for place in range(COUPLE):
        span = slice(place * tokens, (place + 1) * tokens)
        wide[span, 0:HEAD] = q_ref[:, place * HEAD : (place + 1) * HEAD]
        wide[span, HEAD:] = extra


def extend_keys(order_ref, base, kv_all, groups, wide, turned, which):
    count, tokens, columns = kv_all.shape
    lanes = lax.broadcasted_iota(jnp.int32, (tokens, LANES), 1)
    sublanes = lax.broadcasted_iota(jnp.int32, (tokens, LANES), 0)
    for slot in range(count):
        block = order_ref[HEADER + base + slot]
        mine = lanes == sequence_of(order_ref, block * tokens + sublanes)
        unit = jnp.where(mine | (lanes == SEQS + block), 1.0, 0.0).astype(BF)
        for group in range(groups):
            span = slice(group * HEAD, (group + 1) * HEAD)
            wide[group, slot, :, 0:HEAD] = kv_all[slot, :, span]
            wide[group, slot, :, HEAD:] = unit
            start = which * groups * HEAD + group * HEAD
            taken = kv_all[slot, :, start : start + HEAD].astype(F32)
            turned[
                group * HEAD : (group + 1) * HEAD, slot * tokens : (slot + 1) * tokens
            ] = jnp.transpose(taken).astype(BF)


def causal(scores):
    tokens = scores.shape[0]
    keys = lax.broadcasted_iota(jnp.int32, (tokens, tokens), 0)
    queries = lax.broadcasted_iota(jnp.int32, (tokens, tokens), 1)
    kept = jnp.concatenate([keys <= queries] * COUPLE, 1)
    return jnp.where(kept, scores, NEG)


def attn_kernel(count, base, last, order_ref, q_ref, *rest):
    slots, rest = rest[:count], rest[count:]
    if base:
        acc_in, stat_in, *rest = rest
    if last:
        out_ref, total_ref, *rest = rest
    else:
        acc_out, stat_out, *rest = rest
    kv_all, keys, values, queries, spread, acc, stat, sems = rest
    step = pl.program_id(0)
    tokens = q_ref.shape[0]
    factor = HEAD ** (-0.5) * LOG2E

    @pl.when(step == 0)
    def _():
        load_kv(slots, kv_all, sems)
        extend_keys(order_ref, base, kv_all, KV_HEADS, keys, values, 1)

    group = step * COUPLE // REPEAT
    extend_queries(order_ref, q_ref, queries)
    if base:
        acc[...] = acc_in[0]
        stat[...] = stat_in[0]
    else:
        acc[...] = jnp.zeros_like(acc)
        stat[...] = jnp.zeros_like(stat)
        stat[0:1] = jnp.full((1, COUPLE * tokens), NEG, F32)

    scores = []
    new_peak = stat[0:1]
    for slot in range(count):
        made = mm(keys[group, slot], queries[...], NT)
        if base + slot == 0:
            made = causal(made)
        new_peak = jnp.maximum(new_peak, jnp.max(made, 0, keepdims=True))
        scores.append(made)
    keep = jnp.exp2((stat[0:1] - new_peak) * factor)
    total = stat[1:2] * keep
    added = acc[...] * keep
    for slot in range(count):
        weights = jnp.exp2((scores[slot] - new_peak) * factor)
        total += jnp.sum(weights, 0, keepdims=True)
        spread[slot * tokens : (slot + 1) * tokens] = weights.astype(BF)
    own = pl.ds(pl.multiple_of(group * HEAD, HEAD), HEAD)
    added += mm(values[own, :], spread[...])
    stat[0:1] = new_peak
    stat[1:2] = total
    acc[...] = added

    if last:
        made = acc[...] / stat[1:2]
        log_total = stat[0:1] * factor + jnp.log(stat[1:2]) * LOG2E
        for place in range(COUPLE):
            span = slice(place * tokens, (place + 1) * tokens)
            out_ref[:, place * HEAD : (place + 1) * HEAD] = jnp.transpose(made[:, span]).astype(BF)
            total_ref[0, place : place + 1] = log_total[:, span]
    else:
        acc_out[0] = acc[...]
        stat_out[0] = stat[...]


def attn_call(order, q, slots, base, last, state=(), after=()):
    tokens = q.shape[0]
    count = len(slots)
    wide = COUPLE * tokens
    column = lambda h, _: (0, h)
    by_step = lambda h, _: (h, 0, 0)
    if last:
        out_specs = [
            pl.BlockSpec((tokens, COUPLE * HEAD), column),
            pl.BlockSpec((1, 8, tokens), by_step),
        ]
        out_shape = [sds((tokens, HQ), BF), sds((COUPLES, 8, tokens), F32)]
    else:
        out_specs = [
            pl.BlockSpec((1, HEAD, wide), by_step),
            pl.BlockSpec((1, 8, wide), by_step),
        ]
        out_shape = [sds((COUPLES, HEAD, wide), F32), sds((COUPLES, 8, wide), F32)]
    state_specs = [
        pl.BlockSpec((1, HEAD, wide), by_step),
        pl.BlockSpec((1, 8, wide), by_step),
    ]
    grid = pltpu.PrefetchScalarGridSpec(
        num_scalar_prefetch=1,
        grid=(COUPLES,),
        in_specs=[pl.BlockSpec((tokens, COUPLE * HEAD), column)]
        + [ANY] * count
        + (state_specs if base else [])
        + [ANY] * len(after),
        out_specs=out_specs,
        scratch_shapes=[
            pltpu.VMEM((count, tokens, 2 * KVW), BF),
            pltpu.VMEM((KV_HEADS, count, tokens, 2 * HEAD), BF),
            pltpu.VMEM((KV_HEADS * HEAD, count * tokens), BF),
            pltpu.VMEM((wide, 2 * HEAD), BF),
            pltpu.VMEM((count * tokens, wide), BF),
            pltpu.VMEM((HEAD, wide), F32),
            pltpu.VMEM((8, wide), F32),
            pltpu.SemaphoreType.DMA((count,)),
        ],
    )
    return pl.pallas_call(
        without(
            lambda *refs: attn_kernel(count, base, last, *refs),
            2 + count + len(state),
            len(after),
        ),
        name="attention",
        grid_spec=grid,
        out_shape=out_shape,
        compiler_params=params(1),
        cost_estimate=busy(18),
    )(order, q, *slots, *state, *after)


def attn_back_kernel(count, group, order_ref, q_ref, do_ref, total_ref, delta_ref, *rest):
    cos_ref, sin_ref = rest[:2]
    slots, rest = rest[2 : 2 + count], rest[2 + count :]
    if group:
        rest = rest[count:]
    dq_ref, rest = rest[0], rest[1:]
    outs, rest = rest[:count], rest[count:]
    kv_all, keys, turned, queries, grads, spread, d_k, d_v, packed, sems = rest
    step = pl.program_id(0)
    tokens = q_ref.shape[0]
    scale = HEAD ** (-0.5)

    @pl.when(step == 0)
    def _():
        for part in range(2):
            columns = slice(part * KVW + group * HEAD, part * KVW + (group + 1) * HEAD)
            load_kv(
                [slot.at[:, columns] for slot in slots],
                kv_all.at[:, :, part * HEAD : (part + 1) * HEAD],
                sems,
            )
        extend_keys(order_ref, 0, kv_all, 1, keys, turned, 0)
        d_k[...] = jnp.zeros_like(d_k)
        d_v[...] = jnp.zeros_like(d_v)

    extend_queries(order_ref, q_ref, queries)
    for place in range(COUPLE):
        span = slice(place * tokens, (place + 1) * tokens)
        grads[span] = do_ref[:, place * HEAD : (place + 1) * HEAD]

    log_total = jnp.concatenate([total_ref[0, place : place + 1] for place in range(COUPLE)], 1)
    delta = jnp.concatenate([delta_ref[0, place : place + 1] for place in range(COUPLE)], 1)

    for slot in range(count):
        scores = mm(keys[0, slot], queries[...], NT)
        if slot == 0:
            scores = causal(scores)
        probs = jnp.exp2(scores * (scale * LOG2E) - log_total)
        grad_probs = mm(kv_all[slot, :, HEAD:], grads[...], NT)
        grad_scores = (probs * (grad_probs - delta)).astype(BF)
        spread[slot * tokens : (slot + 1) * tokens] = grad_scores
        d_v[slot] += mm(probs.astype(BF), grads[...])
        d_k[slot] += mm(grad_scores, queries[:, 0:HEAD])
    d_q = mm(turned[...], spread[...])
    for place in range(COUPLE):
        span = slice(place * tokens, (place + 1) * tokens)
        piece = jnp.transpose(d_q[:, span]) * scale
        dq_ref[:, place * HEAD : (place + 1) * HEAD] = turn(
            piece, cos_ref[...], -sin_ref[...]
        ).astype(BF)

    @pl.when(step == pl.num_programs(0) - 1)
    def _():
        copies = []
        for place in range(count):
            packed[place, :, 0:HEAD] = d_k[place].astype(BF)
            packed[place, :, HEAD:] = d_v[place].astype(BF)
            columns = pl.ds(group * 2 * HEAD, 2 * HEAD)
            copies.append(
                pltpu.make_async_copy(
                    packed.at[place], outs[place].at[:, columns], sems.at[place]
                )
            )
            copies[-1].start()
        for copy in copies:
            copy.wait()


def attn_back_call(
    group, order, q, grad, log_total, delta, cosine, sine, slots, held=(), after=()
):
    tokens = q.shape[0]
    count = len(slots)
    steps = REPEAT // COUPLE
    column = lambda h, _: (0, group * steps + h)
    by_step = lambda h, _: (group * steps + h, 0, 0)
    fixed = lambda h, _: (0, 0)
    grid = pltpu.PrefetchScalarGridSpec(
        num_scalar_prefetch=1,
        grid=(steps,),
        in_specs=[
            pl.BlockSpec((tokens, COUPLE * HEAD), column),
            pl.BlockSpec((tokens, COUPLE * HEAD), column),
            pl.BlockSpec((1, 8, tokens), by_step),
            pl.BlockSpec((1, 8, tokens), by_step),
            pl.BlockSpec((tokens, HEAD), fixed),
            pl.BlockSpec((tokens, HEAD), fixed),
        ]
        + [ANY] * (count + len(held) + len(after)),
        out_specs=[pl.BlockSpec((tokens, COUPLE * HEAD), lambda h, _: (0, h))] + [ANY] * count,
        scratch_shapes=[
            pltpu.VMEM((count, tokens, 2 * HEAD), BF),
            pltpu.VMEM((1, count, tokens, 2 * HEAD), BF),
            pltpu.VMEM((HEAD, count * tokens), BF),
            pltpu.VMEM((COUPLE * tokens, 2 * HEAD), BF),
            pltpu.VMEM((COUPLE * tokens, HEAD), BF),
            pltpu.VMEM((count * tokens, COUPLE * tokens), BF),
            pltpu.VMEM((count, tokens, HEAD), F32),
            pltpu.VMEM((count, tokens, HEAD), F32),
            pltpu.VMEM((count, tokens, 2 * HEAD), BF),
            pltpu.SemaphoreType.DMA((count,)),
        ],
    )
    return pl.pallas_call(
        without(
            lambda *refs: attn_back_kernel(count, group, *refs),
            7 + count + len(held),
            len(after),
        ),
        name="attention_back",
        input_output_aliases={7 + count + place: 1 + place for place in range(len(held))},
        grid_spec=grid,
        out_shape=[sds((tokens, HQ // KV_HEADS), BF)] + [sds((tokens, 2 * KVW), BF)] * count,
        compiler_params=params(1),
        cost_estimate=busy(26),
    )(order, q, grad, log_total, delta, cosine, sine, *slots, *held, *after)


def out_kernel(x_ref, a_ref, *rest):
    w_refs, (gain_ref, rows_ref, low_ref) = rest[:-3], rest[-3:]
    made = mm(a_ref[:, 0:512], w_refs[0][...], NT)
    for place, w_ref in enumerate(w_refs[1:], 1):
        made += mm(a_ref[:, place * 512 : (place + 1) * 512], w_ref[...], NT)
    rows = made.astype(BF)
    rows_ref[...] = rows
    resid = x_ref[...].astype(F32) + rows.astype(F32)
    scale = lax.rsqrt(jnp.mean(resid * resid, -1, keepdims=True) + EPS)
    low_ref[...] = (resid * scale * gain_ref[1:2]).astype(BF)


def wo_specs(width):
    start = (HQ + 2 * KVW) // 512
    return [
        pl.BlockSpec((width, 512), lambda i, place=place: (0, start + place))
        for place in range(HQ // 512)
    ]


def out_call(x, attended, wo_t, gains, after=()):
    tokens, width = x.shape
    tile = 384
    return pl.pallas_call(
        without(out_kernel, 3 + HQ // 512, len(after)),
        name="attention_out",
        grid=(tokens // tile,),
        in_specs=[
            pl.BlockSpec((tile, width), lambda i: (i, 0)),
            pl.BlockSpec((tile, HQ), lambda i: (i, 0)),
            *wo_specs(width),
            whole((8, width)),
        ]
        + [ANY] * len(after),
        out_specs=[pl.BlockSpec((tile, width), lambda i: (i, 0))] * 2,
        out_shape=[sds((tokens, width), BF)] * 2,
        compiler_params=params(1),
        cost_estimate=busy(9),
    )(x, attended, *[wo_t] * (HQ // 512), gains, *after)


def weight_copies(shards, own, kinds, held, sems):
    size = shards[0].shape[2]
    groups = []
    for expert in range(shards[0].shape[1]):
        copies = []
        for slot, shard in enumerate(shards):
            rows = pl.ds(pl.multiple_of((own ^ slot) * size, 16), size)
            for place, kind in enumerate(kinds):
                copies.append(
                    pltpu.make_async_copy(
                        shard.at[kind, expert],
                        held.at[place, expert, rows],
                        sems.at[place, expert, slot],
                    )
                )
        groups.append(copies)
    return groups


def fetch_weights(shards, own, kinds, held, sems):
    groups = weight_copies(shards, own, kinds, held, sems)
    step = pl.program_id(0)

    @pl.when(step == 0)
    def _():
        for copies in groups:
            for copy in copies:
                copy.start()

    for expert, copies in enumerate(groups):

        @pl.when(step == expert)
        def _():
            for copy in copies:
                copy.wait()


def route_kernel(shards_of, capacity, order_ref, d0_ref, d1_ref, *rest):
    shards = rest[:shards_of]
    p0_ref, p1_ref, gate_ref, rows_ref, hid_ref, held, sems = rest[shards_of:]
    expert = pl.program_id(0)
    tokens = d0_ref.shape[0]
    width = rows_ref.shape[2]
    fetch_weights(shards, order_ref[0], (2,), held, sems)
    wanted = (order_ref[1] * held.shape[1] + expert).astype(F32)
    before = lax.broadcasted_iota(jnp.int32, (tokens, tokens), 0) < lax.broadcasted_iota(
        jnp.int32, (tokens, tokens), 1
    )
    before = jnp.where(before, 1.0, 0.0).astype(BF)
    places = lax.broadcasted_iota(jnp.int32, (capacity, tokens), 0).astype(F32)
    for side, (ref, p_ref) in enumerate(((d0_ref, p0_ref), (d1_ref, p1_ref))):
        info = jnp.transpose(ref[:, width:].astype(F32))
        chosen = jnp.where(info[0:TOPK] == wanted, 1.0, 0.0)
        gate = jnp.sum(
            chosen * (info[TOPK : 2 * TOPK] + info[2 * TOPK : 3 * TOPK] + info[3 * TOPK : 4 * TOPK]),
            0,
            keepdims=True,
        )
        named = jnp.sum(chosen, 0, keepdims=True)
        rank = mm(jnp.broadcast_to(named, (8, tokens)).astype(BF), before)[0:1]
        picks = jnp.where((places == rank) & (named > 0.5), 1.0, 0.0)
        weight = jnp.sum(picks * gate, 1, keepdims=True)
        picks = picks.astype(BF)
        p_ref[0] = picks
        span = slice(side * capacity, (side + 1) * capacity)
        gate_ref[0, span] = jnp.broadcast_to(weight, (capacity, LANES))
        rows_ref[0, span] = (mm(picks, ref[:, :width]) * weight).astype(BF)
    hid_ref[0] = mm(rows_ref[0], held[0, expert])


def route_call(order, grads, shards, capacity, width, after=()):
    tokens = grads[0].shape[0]
    _, experts, size, hidden = shards[0].shape
    rows = 2 * capacity
    by_expert = lambda e, _: (e, 0, 0)
    grid = pltpu.PrefetchScalarGridSpec(
        num_scalar_prefetch=1,
        grid=(experts,),
        in_specs=[pl.BlockSpec(grads[0].shape, lambda e, _: (0, 0))] * 2
        + [ANY] * (len(shards) + len(after)),
        out_specs=[pl.BlockSpec((1, capacity, tokens), by_expert)] * 2
        + [
            pl.BlockSpec((1, rows, LANES), by_expert),
            pl.BlockSpec((1, rows, width), by_expert),
            pl.BlockSpec((1, rows, hidden), by_expert),
        ],
        scratch_shapes=[
            pltpu.VMEM((1, experts, width, hidden), BF),
            pltpu.SemaphoreType.DMA((1, experts, len(shards))),
        ],
    )
    return pl.pallas_call(
        without(
            lambda *refs: route_kernel(len(shards), capacity, *refs), 3 + len(shards), len(after)
        ),
        name="route",
        grid_spec=grid,
        out_shape=[sds((experts, capacity, tokens), BF)] * 2
        + [
            sds((experts, rows, LANES), F32),
            sds((experts, rows, width), BF),
            sds((experts, rows, hidden), F32),
        ],
        compiler_params=params(1),
        cost_estimate=busy(8.5),
    )(order, *grads, *shards, *after)


def expert_kernel(shards_of, capacity, order_ref, x0_ref, x1_ref, p0_ref, p1_ref, gh_ref, *rest):
    shards = rest[:shards_of]
    rows_ref, hid_ref, gg_ref, gu_ref, out0_ref, out1_ref, held, slot, acc, sems = rest[shards_of:]
    expert = pl.program_id(0)
    hidden = gh_ref.shape[2]
    width = x0_ref.shape[1]
    fetch_weights(shards, order_ref[0], (0, 1), held, sems)
    for side, (ref, p_ref) in enumerate(((x0_ref, p0_ref), (x1_ref, p1_ref))):
        span = slice(side * capacity, (side + 1) * capacity)
        rows_ref[0, span] = mm(p_ref[0], ref[...]).astype(BF)
    rows = rows_ref[0]
    tile = 256
    for start in range(0, hidden, tile):
        span = slice(start, start + tile)
        gate = mm(rows, held[0, expert, :, span])
        up = mm(rows, held[1, expert, :, span])
        grad = gh_ref[0, :, span]
        sigma = 1.0 / (1.0 + jnp.exp(-gate))
        active = gate * sigma
        hid_ref[0, :, span] = (active * up).astype(BF)
        gg_ref[0, :, span] = (grad * up * (sigma * (1.0 + gate * (1.0 - sigma)))).astype(BF)
        gu_ref[0, :, span] = (grad * active).astype(BF)
    tile = 512
    for start in range(0, width, tile):
        span = slice(start, start + tile)
        slot[:, span] = (
            mm(gg_ref[0], held[0, expert, span, :], NT)
            + mm(gu_ref[0], held[1, expert, span, :], NT)
        ).astype(BF)
    for side, (p_ref, out_ref) in enumerate(((p0_ref, out0_ref), (p1_ref, out1_ref))):
        span = slice(side * capacity, (side + 1) * capacity)
        term = mm(p_ref[0], slot[span], TN)

        @pl.when(expert == 0)
        def _():
            acc[side] = term

        @pl.when(expert > 0)
        def _():
            acc[side] += term

        @pl.when(expert == pl.num_programs(0) - 1)
        def _():
            out_ref[...] = acc[side].astype(BF)


def expert_call(order, xs, picks, grad_hidden, shards, capacity, after=()):
    tokens, width = xs[0].shape
    _, experts, size, hidden = shards[0].shape
    rows = 2 * capacity
    by_expert = lambda e, _: (e, 0, 0)
    fixed = lambda e, _: (0, 0)
    grid = pltpu.PrefetchScalarGridSpec(
        num_scalar_prefetch=1,
        grid=(experts,),
        in_specs=[pl.BlockSpec((tokens, width), fixed)] * 2
        + [pl.BlockSpec((1, capacity, tokens), by_expert)] * 2
        + [pl.BlockSpec((1, rows, hidden), by_expert)]
        + [ANY] * (len(shards) + len(after)),
        out_specs=[pl.BlockSpec((1, rows, width), by_expert)]
        + [pl.BlockSpec((1, rows, hidden), by_expert)] * 3
        + [pl.BlockSpec((tokens, width), fixed)] * 2,
        scratch_shapes=[
            pltpu.VMEM((2, experts, width, hidden), BF),
            pltpu.VMEM((rows, width), BF),
            pltpu.VMEM((2, tokens, width), F32),
            pltpu.SemaphoreType.DMA((2, experts, len(shards))),
        ],
    )
    return pl.pallas_call(
        without(
            lambda *refs: expert_kernel(len(shards), capacity, *refs), 6 + len(shards), len(after)
        ),
        name="experts",
        grid_spec=grid,
        out_shape=[sds((experts, rows, width), BF)]
        + [sds((experts, rows, hidden), BF)] * 3
        + [sds((tokens, width), BF)] * 2,
        compiler_params=params(1),
        cost_estimate=busy(17),
    )(order, *xs, *picks, grad_hidden, *shards, *after)


def down_kernel(shards_of, capacity, place, order_ref, hid_ref, gate_ref, p0_ref, p1_ref, *rest):
    shards = rest[:shards_of]
    out_ref, pair_ref, held, slot, acc, packed, sems, out_sem = rest[-8:]
    expert = pl.program_id(0)
    width = out_ref.shape[1]
    fetch_weights(shards, order_ref[0], (2,), held, sems)
    tile = 512
    for start in range(0, width, tile):
        span = slice(start, start + tile)
        made = mm(hid_ref[0], held[0, expert, span, :], NT).astype(BF).astype(F32)
        slot[:, span] = (made * gate_ref[0, :, 0:1]).astype(BF)
    for side, p_ref in enumerate((p0_ref, p1_ref)):
        span = slice(side * capacity, (side + 1) * capacity)
        term = mm(p_ref[0], slot[span], TN)

        @pl.when(expert == 0)
        def _():
            acc[side] = term

        @pl.when(expert > 0)
        def _():
            acc[side] += term

    @pl.when(expert == pl.num_programs(0) - 1)
    def _():
        packed[...] = acc[1].astype(BF)
        copy = pltpu.make_async_copy(packed, pair_ref.at[place], out_sem)
        copy.start()
        out_ref[...] = acc[0].astype(BF)
        copy.wait()


def down_call(order, hid, gates, picks, shards, capacity, width, place, pair, total, after=()):
    tokens = picks[0].shape[2]
    _, experts, size, hidden = shards[0].shape
    rows = 2 * capacity
    by_expert = lambda e, _: (e, 0, 0)
    pair = [] if pair is None else [pair]
    grid = pltpu.PrefetchScalarGridSpec(
        num_scalar_prefetch=1,
        grid=(experts,),
        in_specs=[
            pl.BlockSpec((1, rows, hidden), by_expert),
            pl.BlockSpec((1, rows, LANES), by_expert),
        ]
        + [pl.BlockSpec((1, capacity, tokens), by_expert)] * 2
        + [ANY] * (len(shards) + len(pair) + len(after)),
        out_specs=[whole((tokens, width)), ANY],
        scratch_shapes=[
            pltpu.VMEM((1, experts, width, hidden), BF),
            pltpu.VMEM((rows, width), BF),
            pltpu.VMEM((2, tokens, width), F32),
            pltpu.VMEM((tokens, width), BF),
            pltpu.SemaphoreType.DMA((1, experts, len(shards))),
            pltpu.SemaphoreType.DMA,
        ],
    )
    return pl.pallas_call(
        lambda *refs: down_kernel(len(shards), capacity, place, *refs),
        name="experts_down",
        grid_spec=grid,
        out_shape=[sds((tokens, width), BF), sds((total, tokens, width), BF)],
        input_output_aliases={5 + len(shards): 1} if pair else {},
        compiler_params=params(1),
        cost_estimate=busy(9.3),
    )(order, hid, gates, *picks, *shards, *pair, *after)


def weight_grad_kernel(chunks, *rest):
    xs, gs = rest[:chunks], rest[chunks : 2 * chunks]
    ggs, gus = rest[2 * chunks : 3 * chunks], rest[3 * chunks : 4 * chunks]
    hids = rest[4 * chunks : 5 * chunks]
    out_ref, left, rights = rest[5 * chunks :]
    rows = xs[0].shape[1]

    @pl.when(pl.program_id(0) == 0)
    def _():
        for kind, group in enumerate((ggs, gus, hids)):
            for place, ref in enumerate(group):
                rights[kind, place * rows : (place + 1) * rows] = ref[0]

    for kind, group in ((0, xs), (2, gs)):
        for place, ref in enumerate(group):
            left[place * rows : (place + 1) * rows] = ref[0]
        out_ref[kind] = mm(left[...], rights[kind], TN).astype(BF)
        if kind == 0:
            out_ref[1] = mm(left[...], rights[1], TN).astype(BF)


def weight_grad_call(expert, xs, gs, ggs, gus, hids, after=()):
    chunks = len(xs)
    _, rows, width = xs[0].shape
    hidden = ggs[0].shape[2]
    tile = 256
    return pl.pallas_call(
        without(lambda *refs: weight_grad_kernel(chunks, *refs), 5 * chunks, len(after)),
        name="expert_weight_grads",
        grid=(width // tile,),
        in_specs=[pl.BlockSpec((1, rows, tile), lambda i: (expert, 0, i))] * (2 * chunks)
        + [pl.BlockSpec((1, rows, hidden), lambda i: (expert, 0, 0))] * (3 * chunks)
        + [ANY] * len(after),
        out_specs=pl.BlockSpec((3, tile, hidden), lambda i: (0, i, 0)),
        out_shape=sds((3, width, hidden), BF),
        scratch_shapes=[
            pltpu.VMEM((chunks * rows, tile), BF),
            pltpu.VMEM((3, chunks * rows, hidden), BF),
        ],
        compiler_params=params(1),
        cost_estimate=busy(18),
    )(*xs, *gs, *ggs, *gus, *hids, *after)


def resid_back_kernel(
    terms, x_ref, rows_ref, dy_ref, gain_ref, att_ref, *rest
):
    w_refs, rest = rest[: HQ // 512], rest[HQ // 512 :]
    parts = rest[:terms]
    resid_ref, attn_ref, do_ref, delta_ref, gain_out, deltas = rest[terms:]
    step = pl.program_id(0)
    grad = parts[0][...].astype(F32)
    for part in parts[1:]:
        grad += part[...].astype(F32)
    resid = x_ref[...].astype(F32) + rows_ref[...].astype(F32)
    scale = lax.rsqrt(jnp.mean(resid * resid, -1, keepdims=True) + EPS)
    normed = resid * scale
    product = grad * normed
    partial = jnp.sum(product, 0, keepdims=True)

    @pl.when(step == 0)
    def _():
        gain_out[...] = jnp.broadcast_to(partial, gain_out.shape)

    @pl.when(step > 0)
    def _():
        gain_out[...] += partial

    gain = gain_ref[1:2]
    mean = jnp.mean(product * gain, -1, keepdims=True)
    total = dy_ref[...].astype(F32) + scale * (grad * gain - normed * mean)
    resid_ref[...] = total
    low = total.astype(BF)
    attn_ref[...] = low
    for place, w_ref in enumerate(w_refs):
        do_ref[:, place * 512 : (place + 1) * 512] = mm(low, w_ref[...]).astype(BF)
    each = do_ref[...].astype(F32) * att_ref[...].astype(F32)
    lanes = lax.broadcasted_iota(jnp.int32, deltas.shape, 1)
    made = jnp.zeros(deltas.shape, F32)
    for head in range(HEADS):
        value = jnp.sum(each[:, head * HEAD : (head + 1) * HEAD], -1, keepdims=True)
        made = jnp.where(lanes == head, value, made)
    deltas[...] = made
    turned = jnp.transpose(deltas[...])
    for head in range(HEADS):
        delta_ref[head // COUPLE, head % COUPLE : head % COUPLE + 1] = turned[head : head + 1]


def resid_back_call(x, rows, dy, gains, wo_t, attended, parts, after=()):
    tokens, width = x.shape
    tile = 384
    by_row = lambda i: (i, 0)
    return pl.pallas_call(
        without(
            lambda *refs: resid_back_kernel(len(parts), *refs),
            5 + HQ // 512 + len(parts),
            len(after),
        ),
        name="resid_back",
        grid=(tokens // tile,),
        in_specs=[pl.BlockSpec((tile, width), by_row)] * 3
        + [whole((8, width)), pl.BlockSpec((tile, HQ), by_row)]
        + wo_specs(width)
        + [pl.BlockSpec((tile, width), by_row)] * len(parts)
        + [ANY] * len(after),
        out_specs=[pl.BlockSpec((tile, width), by_row)] * 2
        + [
            pl.BlockSpec((tile, HQ), by_row),
            pl.BlockSpec((COUPLES, 8, tile), lambda i: (0, 0, i)),
            whole((8, width)),
        ],
        out_shape=[
            sds((tokens, width), F32),
            sds((tokens, width), BF),
            sds((tokens, HQ), BF),
            sds((COUPLES, 8, tokens), F32),
            sds((8, width), F32),
        ],
        scratch_shapes=[pltpu.VMEM((tile, LANES), F32)],
        compiler_params=params(1),
        cost_estimate=busy(10.5),
    )(x, rows, dy, gains, attended, *[wo_t] * (HQ // 512), *parts, *after)


def block_copies(order_ref, source, near, far, sems):
    shards_of, sides, steps, rows, _ = near.shape
    shards_of = 2 * shards_of
    copies = []
    for slot in range(shards_of):
        for place in range(sides * steps):
            block = order_ref[2 + place] * shards_of + (order_ref[0] ^ slot)
            target = far if slot % 2 else near
            copies.append(
                pltpu.make_async_copy(
                    source.at[pl.ds(pl.multiple_of(block * rows, 16), rows)],
                    target.at[slot // 2, place % 2, place // 2],
                    sems.at[slot * sides * steps + place],
                )
            )
    return copies


def cross_kernel(order_ref, left_ref, right_ref, near, far, made, sems):
    step = pl.program_id(0)
    tile = left_ref.shape[1]
    made[pl.ds(pl.multiple_of(step * tile, tile), tile)] = mm(
        left_ref[...], right_ref[...], TN
    ).astype(BF)

    @pl.when(step == pl.num_programs(0) - 1)
    def _():
        copies = block_copies(order_ref, made, near, far, sems)
        for copy in copies:
            copy.start()
        for copy in copies:
            copy.wait()


def blocks_shape(count, shards_of, rows, columns):
    return (shards_of // 2, 2, count // 2, rows // (count * shards_of), columns)


def cross_call(order, left, right, count, shards_of, name):
    tokens, rows = left.shape
    columns = right.shape[1]
    tile = 512
    grid = pltpu.PrefetchScalarGridSpec(
        num_scalar_prefetch=1,
        grid=(rows // tile,),
        in_specs=[
            pl.BlockSpec((tokens, tile), lambda i, _: (0, i)),
            pl.BlockSpec((tokens, columns), lambda i, _: (0, 0)),
        ],
        out_specs=[ANY] * 2,
        scratch_shapes=[
            pltpu.VMEM((rows, columns), BF),
            pltpu.SemaphoreType.DMA((count * shards_of,)),
        ],
    )
    return pl.pallas_call(
        cross_kernel,
        name=name,
        grid_spec=grid,
        out_shape=[sds(blocks_shape(count, shards_of, rows, columns), BF)] * 2,
        compiler_params=params(1),
        cost_estimate=busy(7.5),
    )(order, left, right)


def plain_cross_kernel(left_ref, right_ref, out_ref):
    out_ref[...] = mm(left_ref[...], right_ref[...], TN).astype(out_ref.dtype)


def plain_cross_call(left, right, name):
    tokens, rows = left.shape
    columns = right.shape[1]
    tile = 512
    return pl.pallas_call(
        plain_cross_kernel,
        name=name,
        grid=(rows // tile,),
        in_specs=[pl.BlockSpec((tokens, tile), lambda i: (0, i)), whole((tokens, columns))],
        out_specs=pl.BlockSpec((tile, columns), lambda i: (i, 0)),
        out_shape=sds((rows, columns), BF),
        compiler_params=params(1),
        cost_estimate=busy(7.5),
    )(left, right)


def input_q_kernel(dq_ref, w_ref, out_ref):
    out_ref[...] = mm(dq_ref[...], w_ref[...], NT)


def input_q_call(d_q, w_full):
    tokens = d_q.shape[0]
    width = w_full.shape[0]
    tile = 512
    return pl.pallas_call(
        input_q_kernel,
        name="input_grad_q",
        grid=(width // tile,),
        in_specs=[whole((tokens, HQ)), pl.BlockSpec((tile, HQ), lambda i: (i, 0))],
        out_specs=pl.BlockSpec((tokens, tile), lambda i: (0, i)),
        out_shape=sds((tokens, width), F32),
        compiler_params=params(1),
        cost_estimate=busy(6),
    )(d_q, w_full)


def final_kernel(
    terms,
    order_ref,
    x_ref,
    low_ref,
    resid_ref,
    gq_ref,
    gain_ref,
    moe_ref,
    w_ref,
    cos_ref,
    sin_ref,
    *rest,
):
    parts = rest[:terms]
    grad_ref = rest[terms]
    outs = rest[terms + 1 : -2]
    made, sems = rest[-2:]
    scale_k = HEAD ** (-0.5)
    cosine, sine = cos_ref[...], -sin_ref[...]
    key_grads, value_grads = [], []
    for group in range(KV_HEADS):
        span = slice(group * 2 * HEAD, (group + 1) * 2 * HEAD)
        total = parts[0][:, span].astype(F32)
        for part in parts[1:]:
            total += part[:, span].astype(F32)
        key_grads.append(turn(total[:, 0:HEAD] * scale_k, cosine, sine).astype(BF))
        value_grads.append(total[:, HEAD:].astype(BF))
    low = jnp.concatenate(key_grads + value_grads, 1)
    made[:, 0 : 2 * KVW] = mm(low_ref[...], low, TN).astype(BF)
    wide = x_ref[...].astype(F32)
    scale = lax.rsqrt(jnp.mean(wide * wide, -1, keepdims=True) + EPS)
    normed = wide * scale
    grad = gq_ref[...] + mm(low, w_ref[...], NT)
    product = grad * normed
    gain_part = jnp.sum(product, 0, keepdims=True)
    width = x_ref.shape[1]
    lines = lax.broadcasted_iota(jnp.int32, (LANES, width), 0)
    both = jnp.where(lines == 0, gain_part, jnp.where(lines == 1, moe_ref[0:1], 0.0))
    made[:, 2 * KVW :] = jnp.transpose(both).astype(BF)
    if len(outs) == 2:
        copies = block_copies(order_ref, made, *outs, sems)
    else:
        copies = [pltpu.make_async_copy(made, outs[0], sems.at[0])]
    for copy in copies:
        copy.start()
    gain = gain_ref[0:1]
    mean = jnp.mean(product * gain, -1, keepdims=True)
    own = (scale * (grad * gain - normed * mean)).astype(BF)
    grad_ref[...] = (resid_ref[...] + own.astype(F32)).astype(BF)
    for copy in copies:
        copy.wait()


def final_call(
    order, x, low, resid, grad_q, gains, moe_part, w_full, cosine, sine, parts, layout, after=()
):
    tokens, width = x.shape
    columns = 2 * KVW + LANES
    if layout:
        outs = [sds(blocks_shape(*layout, width, columns), BF)] * 2
    else:
        outs = [sds((width, columns), BF)]
    grid = pltpu.PrefetchScalarGridSpec(
        num_scalar_prefetch=1,
        grid=(1,),
        in_specs=[whole((tokens, width))] * 4
        + [whole((8, width))] * 2
        + [pl.BlockSpec((width, 2 * KVW), lambda i, _: (0, HQ // (2 * KVW)))]
        + [whole((tokens, HEAD))] * 2
        + [whole((tokens, 2 * KVW))] * len(parts)
        + [ANY] * len(after),
        out_specs=[whole((tokens, width))] + [ANY] * len(outs),
        scratch_shapes=[
            pltpu.VMEM((width, columns), BF),
            pltpu.SemaphoreType.DMA((layout[0] * layout[1] if layout else 1,)),
        ],
    )
    return pl.pallas_call(
        without(lambda *refs: final_kernel(len(parts), *refs), 10 + len(parts), len(after)),
        name="final",
        grid_spec=grid,
        out_shape=[sds((tokens, width), BF)] + outs,
        compiler_params=params(1),
        cost_estimate=busy(10),
    )(order, x, low, resid, grad_q, gains, moe_part, w_full, cosine, sine, *parts, *after)


def hold_kernel(count, *refs):
    del count, refs


def hold(arrays, *until):
    until = [array for array in until if array is not None]
    if not until:
        return arrays
    count = len(arrays)
    return pl.pallas_call(
        lambda *refs: hold_kernel(count, *refs),
        name="hold",
        in_specs=[ANY] * (count + len(until)),
        out_specs=[ANY] * count,
        out_shape=[sds(array.shape, array.dtype) for array in arrays],
        input_output_aliases={place: place for place in range(count)},
        cost_estimate=busy(0.5),
    )(*arrays, *until)


def local(
    layer_input,
    lengths,
    expert_ids,
    gate_weights,
    attn_gain,
    wq,
    wk,
    wv,
    wo,
    moe_gain,
    w_gate,
    w_up,
    w_down,
    cotangent,
):
    count = lax.axis_size("ctx")
    shards_of = lax.axis_size("fsdp")
    both = ("ctx", "fsdp")
    ring = Ring(count)
    me = lax.axis_index("ctx").astype(jnp.int32)
    own = lax.axis_index("fsdp").astype(jnp.int32)
    x = layer_input[0]
    dy = cotangent[0]
    tokens, width = x.shape
    exp_dev = w_gate.shape[0]
    experts = exp_dev * count
    capacity = 3 * tokens * TOPK // (2 * experts)

    sources = ring.sources()
    places = jnp.concatenate([jnp.stack([own, me]), sources])
    layout = (count, shards_of) if ring.length == 4 and shards_of == 4 else None
    rows = wq.shape[0]
    gains_part = jnp.concatenate(
        [attn_gain[:, None], moe_gain[:, None], jnp.zeros((rows, LANES - 2), BF)], 1
    )
    w_full = lax.all_gather(
        jnp.concatenate([wq, wk, wv, wo.T, gains_part], 1), both, axis=0, tiled=True
    )

    gates = gate_weights[0]
    gate_high = gates.astype(BF)
    rest = gates - gate_high.astype(F32)
    gate_mid = rest.astype(BF)
    gate_low = (rest - gate_mid.astype(F32)).astype(BF)
    info = jnp.concatenate(
        [
            dy,
            expert_ids[0].astype(BF),
            gate_high,
            gate_mid,
            gate_low,
            jnp.zeros((tokens, LANES - 4 * TOPK), BF),
        ],
        1,
    )
    ends = jnp.cumsum(lengths[0])
    index = me * tokens + jnp.arange(tokens, dtype=jnp.int32)
    after = (index[:, None] >= ends[None, :]).astype(jnp.int32)
    start = jnp.sum(after * lengths[0][None, :], 1)
    half = HEAD // 2
    freq = jnp.exp(jnp.arange(half, dtype=F32) * (-2.0 * math.log(ROPE_BASE) / HEAD))
    angle = (index - start).astype(F32)[:, None] * freq[None, :]
    cosine = jnp.cos(angle)
    sine = jnp.sin(angle)
    cosine = jnp.concatenate([cosine, cosine], 1)
    sine = jnp.concatenate([-sine, sine], 1)
    order = jnp.concatenate(
        [me[None], (start[0] // tokens)[None], ends[: HEADER - 2], sources]
    )

    run = ring.gather(info)
    next(run)
    grads = [run.send(None), run.send(None)]
    q, kv, low_one, gains = qkv_call(
        x, w_full, cosine, sine, [grads[1][1]] if layout else []
    )
    shards = gather_shards(
        jnp.stack([w_gate, w_up, jnp.swapaxes(w_down, 1, 2)]), shards_of, grads[1][1]
    )
    kv_couples = ring.gather_now(kv)
    kv_slots = [part for couple in kv_couples for part in couple]
    half = count // 2
    parts, made, routed = [], [], []

    def route(step, after=()):
        routed.append(route_call(places, grads[step], shards, capacity, width, after))
        return routed[-1][4]

    grads.append(run.send(kv_couples[3][1]))
    state = attn_call(order, q, kv_slots[:half], 0, False, after=[route(0)])
    grads += [run.send(state[1]) for _ in range(3, half)]
    attended, log_total = attn_call(
        order, q, kv_slots[half:], half, True, state, [grads[3][0]]
    )
    attn_rows, low_two = out_call(x, attended, w_full, gains, [grads[3][1]])

    def run_experts(step, couple, after):
        pick0, pick1, _, _, grad_hidden = routed[step]
        found = expert_call(
            places, couple, (pick0, pick1), grad_hidden, shards, capacity, after
        )
        made.append(found[:4])
        parts.append((found[4], found[5]))
        return found[4]

    rows_run = ring.gather(low_two)
    next(rows_run)
    mark = route(2, [route(1)])
    couple = rows_run.send(mark)
    mark = run_experts(0, couple, [mark])
    couple = rows_run.send(mark)
    mark = run_experts(1, couple, [mark])
    for step in range(3, half):
        mark = route(step, [mark])
    couple = rows_run.send(None)
    couples = [couple] + [rows_run.send(mark) for _ in range(3, half)]
    for step in range(2, half):
        mark = run_experts(step, couples[step - 2], [mark, couples[1][0]])

    y_pairs = []

    def down(step, after):
        pick0, pick1, gate_rows = routed[step][:3]
        packed = step < half // 2
        place = half // 2 - 1 - step if packed else 0
        out, pair = down_call(
            places,
            made[step][1],
            gate_rows,
            (pick0, pick1),
            shards,
            capacity,
            width,
            place,
            y_pairs.pop() if place else None,
            half // 2 if packed else 1,
            after,
        )
        y_pairs.append(pair)
        return out

    grad_run = ring.scatter(parts, True)
    grad_mark = next(grad_run)
    expert_grads = []
    for expert in range(exp_dev):
        made_grad = weight_grad_call(
            expert,
            [entry[0] for entry in made],
            [entry[3] for entry in routed],
            [entry[2] for entry in made],
            [entry[3] for entry in made],
            [entry[1] for entry in made],
            [mark, grad_mark],
        )
        mark = made_grad
        if expert < 2:
            grad_mark = grad_run.send(mark)
        expert_grads.append(
            lax.psum_scatter(
                hold([made_grad], grad_mark)[0], "fsdp", scatter_dimension=1, tiled=True
            )
        )
    y_parts = [None] * len(made)
    for step in reversed(range(len(made))):
        y_parts[step] = down(step, [mark, grad_mark])
        mark = y_parts[step]
        if step == len(made) // 2:
            grad_mark = grad_run.send(mark)
    grad_parts = grad_run.send(mark)
    y_run = ring.scatter_late(y_parts, hold(y_pairs, grad_mark))
    next(y_run)

    resid, grad_attn, grad_out, delta, moe_part = resid_back_call(
        x, attn_rows, dy, gains, w_full, attended, grad_parts
    )
    back = attn_back_call(
        0, order, q, grad_out, log_total, delta, cosine, sine, kv_slots
    )
    d_q = [back[0]]
    mark = y_run.send(back[0])
    back = attn_back_call(
        1,
        order,
        q,
        grad_out,
        log_total,
        delta,
        cosine,
        sine,
        kv_slots,
        back[1:],
        [mark] + expert_grads,
    )
    d_q.append(back[0])
    expert_grads = jnp.stack(expert_grads, 1).astype(F32)
    d_q = jnp.concatenate(d_q, 1)
    waits = [y_run.send(back[0])]
    if layout:
        wo_part = cross_call(places, hold([grad_attn], back[0])[0], attended, *layout, "wo_grad")
        wq_part = cross_call(places, low_one, d_q, *layout, "wq_grad")
        waits += [wo_part[0], wq_part[0]]
    kv_parts = hold(back[1:], *waits)
    kv_run = ring.scatter([(kv_parts[2 * step], kv_parts[2 * step + 1]) for step in range(half)])
    next(kv_run)
    for _ in range(4):
        kv_terms = kv_run.send(None)
    y_run.send(kv_terms[-1])

    grad_q = input_q_call(d_q, w_full)
    after = []
    if layout:
        wo_terms, wo_sent = scatter_all_across(*wo_part, shards_of)
        wq_terms, wq_sent = scatter_all_across(*wq_part, shards_of)
        after = [wo_terms, wq_sent]
    else:
        wq_grad, wo_grad = [
            lax.psum_scatter(
                plain_cross_call(left, right, name), both, scatter_dimension=0, tiled=True
            ).astype(F32)
            for left, right, name in (
                (low_one, d_q, "wq_grad"),
                (grad_attn, attended, "wo_grad"),
            )
        ]
    input_grad, *tail = final_call(
        places,
        x,
        low_one,
        resid,
        grad_q,
        gains,
        moe_part,
        w_full,
        cosine,
        sine,
        kv_terms,
        layout,
        after,
    )
    if layout:
        wo_terms = hold([wo_terms], kv_terms[-1])[0]
        tail, _ = scatter_all_across(*tail, shards_of)
        runs = [scatter_all_along(terms, ring) for terms in (wo_terms, wq_terms, tail)]
        for one in runs:
            next(one)
        for _ in range(4):
            wo_grad, wq_grad, tail = [one.send(None) for one in runs]
    else:
        tail = lax.psum_scatter(tail[0], both, scatter_dimension=0, tiled=True).astype(F32)
    y_terms = y_run.send(None)
    moe = y_terms[0].astype(F32)
    for term in y_terms[1:]:
        moe = moe + term.astype(F32)
    output = (x.astype(F32) + attn_rows.astype(F32) + moe).astype(BF)
    return (
        output[None],
        input_grad[None],
        tail[:, 2 * KVW],
        wq_grad,
        tail[:, 0:KVW],
        tail[:, KVW : 2 * KVW],
        wo_grad.T,
        tail[:, 2 * KVW + 1],
        expert_grads[0],
        expert_grads[1],
        jnp.swapaxes(expert_grads[2], 1, 2),
    )


def solution(mesh):
    return jax.shard_map(
        local,
        mesh=mesh,
        in_specs=(
            P("fsdp", "ctx", None),
            P("fsdp", None),
            P("fsdp", "ctx", None),
            P("fsdp", "ctx", None),
            P(("ctx", "fsdp")),
            P(("ctx", "fsdp"), None),
            P(("ctx", "fsdp"), None),
            P(("ctx", "fsdp"), None),
            P(None, ("ctx", "fsdp")),
            P(("ctx", "fsdp")),
            P("ctx", "fsdp", None),
            P("ctx", "fsdp", None),
            P("ctx", None, "fsdp"),
            P("fsdp", "ctx", None),
        ),
        out_specs=(
            P("fsdp", "ctx", None),
            P("fsdp", "ctx", None),
            P(("ctx", "fsdp")),
            P(("ctx", "fsdp"), None),
            P(("ctx", "fsdp"), None),
            P(("ctx", "fsdp"), None),
            P(None, ("ctx", "fsdp")),
            P(("ctx", "fsdp")),
            P("ctx", "fsdp", None),
            P("ctx", "fsdp", None),
            P("ctx", None, "fsdp"),
        ),
        check_vma=False,
    )
```
